128 devices in a mesh: ctx: 8 (over z, core), tp: 16 (over y, x).
Axes of the slice: x: 4, y: 4, z: 4, core: 2. Of those that a mesh axis runs over, the one named last changes fastest.
Arguments:
- hidden: bfloat16 [4, 2048, 2048], P(None, 'ctx'), may hold values from -6 to 6
- segments: int32 [4, 2048], replicated, may hold values from 0 to 3, as said below
- key_attendable: int32 [4, 2048], replicated, may hold values 0 or 1
- attention_gain: bfloat16 [2048], replicated, may hold values from 0.5 to 1.5
- feedforward_gain: bfloat16 [2048], replicated, may hold values from 0.5 to 1.5
- attend_frozen: bfloat16 [3, 2048, 2048], P(None, None, 'tp'), may hold values from -0.125 to 0.125
- output_frozen: bfloat16 [2048, 2048], P('tp'), may hold values from -0.125 to 0.125
- expand_frozen: bfloat16 [2, 2048, 5632], P(None, None, 'tp'), may hold values from -0.125 to 0.125
- reduce_frozen: bfloat16 [5632, 2048], P('tp'), may hold values from -0.078125 to 0.078125
- attend_lower: float32 [3, 2048, 16], replicated, may hold values from -0.125 to 0.125
- attend_upper: float32 [3, 16, 2048], P(None, None, 'tp'), may hold values from -0.6 to 0.6
- attend_magnitude: float32 [3, 2048], P(None, 'tp'), may hold values from 0.8 to 1.6
- output_lower: float32 [2048, 16], P('tp'), may hold values from -0.125 to 0.125
- output_upper: float32 [16, 2048], replicated, may hold values from -0.6 to 0.6
- output_magnitude: float32 [2048], replicated, may hold values from 6 to 14
- expand_lower: float32 [2, 2048, 16], replicated, may hold values from -0.125 to 0.125
- expand_upper: float32 [2, 16, 5632], P(None, None, 'tp'), may hold values from -0.6 to 0.6
- expand_magnitude: float32 [2, 5632], P(None, 'tp'), may hold values from 0.8 to 1.6
- reduce_lower: float32 [5632, 16], P('tp'), may hold values from -0.078125 to 0.078125
- reduce_upper: float32 [16, 2048], replicated, may hold values from -0.6 to 0.6
- reduce_magnitude: float32 [2048], replicated, may hold values from 0.8 to 2
- cotangent: bfloat16 [4, 2048, 2048], P(None, 'ctx'), may hold values from -6 to 6
Outputs:
- block_output: bfloat16 [4, 2048, 2048], P(None, 'ctx')
- hidden_grad: float32 [4, 2048, 2048], P(None, 'ctx')
- attend_lower_grad: float32 [3, 2048, 16], replicated
- attend_upper_grad: float32 [3, 16, 2048], P(None, None, 'tp')
- attend_magnitude_grad: float32 [3, 2048], P(None, 'tp')
- output_lower_grad: float32 [2048, 16], P('tp')
- output_upper_grad: float32 [16, 2048], replicated
- output_magnitude_grad: float32 [2048], replicated
- expand_lower_grad: float32 [2, 2048, 16], replicated
- expand_upper_grad: float32 [2, 16, 5632], P(None, None, 'tp')
- expand_magnitude_grad: float32 [2, 5632], P(None, 'tp')
- reduce_lower_grad: float32 [5632, 16], P('tp')
- reduce_upper_grad: float32 [16, 2048], replicated
- reduce_magnitude_grad: float32 [2048], replicated
The draws below stay inside these ranges and needn't reach their ends.
Inputs may be any that keep to these rules, and one draw needn't show every extreme that they name: `segments`: ids never fall along a row; in every row one segment starts within the first 256 positions and ends within the last 256.
All inputs are finite; a program needn't handle non-finite values.
Results may differ from the reference program's by a relative error of at most 0.015.
The reference program's roundings to bfloat16 on the way count: a program that leaves them out, or rounds other values in their place, can miss the bound.
Values may be sent and summed in bfloat16 or wider, within the bound.
A program may use at most 256 MiB of HBM per device.

```python
import jax
import jax.numpy as jnp
from jax import lax

MODEL_DIMENSION = 2048
HEADS = 16
HD = 128
FF = 5632
RANK = 16
SEGS = 4
PACKED_LENGTH = 2048
PACKED_ROWS = 4
TOKENS_PER_PART = 256


def draw_segments(key, part):
    key = jax.random.fold_in(key, 7)
    key_one, key_two, third_random_key = jax.random.split(key, 3)
    early_one = jax.random.randint(key_one, (PACKED_ROWS, 1), 1, TOKENS_PER_PART)
    early_two = jax.random.randint(key_two, (PACKED_ROWS, 1), 1, TOKENS_PER_PART)
    trailing_boundary = jax.random.randint(third_random_key, (PACKED_ROWS, 1), PACKED_LENGTH - TOKENS_PER_PART + 1, PACKED_LENGTH)
    token_positions = jnp.arange(PACKED_LENGTH, dtype=jnp.int32)[None, :]
    first_part = (token_positions >= early_one).astype(jnp.int32)
    second_part = (token_positions >= early_two).astype(jnp.int32)
    third_part = (token_positions >= trailing_boundary).astype(jnp.int32)
    return first_part + second_part + third_part


def plant(array, stream_key, smallest, high):
    longest = array.shape.index(max(array.shape))
    spots = []
    for shift in (0, 1):
        where = [jax.random.randint(jax.random.fold_in(stream_key, axis), (), 0, length) for axis, length in enumerate(array.shape)]
        where[longest] = (where[longest] + shift) % array.shape[longest]
        spots.append(tuple(where))
    return array.at[spots[0]].set(smallest).at[spots[1]].set(high)


def steps_of(key, shape, cuts, low, largest):
    loudness, own = 1.0, jax.random.fold_in(key, 6)
    for dim, blocks in cuts:
        steps = jnp.exp(jax.random.uniform(jax.random.fold_in(own, dim), (blocks,), jnp.float32, low / len(cuts), largest / len(cuts)))
        loudness = loudness * jnp.repeat(steps, shape[dim] // blocks).reshape([-1 if axis == dim else 1 for axis in range(len(shape))])
    return loudness


def noise(stream_key, shape, width, bound, cuts=(), held_as=jnp.bfloat16):
    loudness = steps_of(stream_key, shape, cuts, -0.22, 0.18) if cuts else 1.0
    drawn = jax.random.normal(stream_key, shape, jnp.float32) * width * loudness
    return jnp.minimum(jnp.maximum(drawn, -bound), bound).astype(held_as)


def setup_inputs(seed: int = 0) -> dict:
    splits = jax.random.split(jax.random.key(seed), 23)
    return {
        "hidden": noise(splits[0], (PACKED_ROWS, PACKED_LENGTH, MODEL_DIMENSION), 1.0, 6.0, ((1, 8),)),
        "segments": draw_segments(jax.random.fold_in(splits[22], 71), 0),
        "key_attendable": plant((jax.random.randint(splits[2], (PACKED_ROWS, PACKED_LENGTH), 0, 8) < 7).astype(jnp.int32), jax.random.fold_in(splits[2], 1), 0, 1),
        "attention_gain": jnp.clip(1.0 + 0.1 * jax.random.normal(splits[3], (MODEL_DIMENSION,), jnp.float32), 0.5, 1.5).astype(jnp.bfloat16),
        "feedforward_gain": jnp.clip(1.0 + 0.1 * jax.random.normal(splits[4], (MODEL_DIMENSION,), jnp.float32), 0.5, 1.5).astype(jnp.bfloat16),
        "attend_frozen": noise(splits[5], (3, MODEL_DIMENSION, MODEL_DIMENSION), MODEL_DIMENSION ** -0.5, 0.125, ((2, 16),)),
        "output_frozen": noise(splits[6], (MODEL_DIMENSION, MODEL_DIMENSION), MODEL_DIMENSION ** -0.5, 0.125, ((0, 16),)),
        "expand_frozen": noise(splits[7], (2, MODEL_DIMENSION, FF), MODEL_DIMENSION ** -0.5, 0.125, ((2, 16),)),
        "reduce_frozen": noise(splits[8], (FF, MODEL_DIMENSION), FF ** -0.5, 0.078125, ((0, 16),)),
        "attend_lower": noise(splits[9], (3, MODEL_DIMENSION, RANK), MODEL_DIMENSION ** -0.5, 0.125, (), jnp.float32),
        "attend_upper": noise(splits[10], (3, RANK, MODEL_DIMENSION), 0.1, 0.6, ((2, 16),), jnp.float32),
        "attend_magnitude": jnp.clip(0.8 + 0.8 * jax.random.uniform(splits[11], (3, MODEL_DIMENSION), jnp.float32) ** steps_of(splits[11], (3, MODEL_DIMENSION), ((1, 16),), -0.2, 0.2), 0.8, 1.6),
        "output_lower": noise(splits[12], (MODEL_DIMENSION, RANK), MODEL_DIMENSION ** -0.5, 0.125, ((0, 16),), jnp.float32),
        "output_upper": noise(splits[13], (RANK, MODEL_DIMENSION), 0.1, 0.6, (), jnp.float32),
        "output_magnitude": jnp.clip(jax.random.uniform(splits[14], (MODEL_DIMENSION,), jnp.float32, 6.0, 14.0), 6.0, 14.0),
        "expand_lower": noise(splits[15], (2, MODEL_DIMENSION, RANK), MODEL_DIMENSION ** -0.5, 0.125, (), jnp.float32),
        "expand_upper": noise(splits[16], (2, RANK, FF), 0.1, 0.6, ((2, 16),), jnp.float32),
        "expand_magnitude": jnp.clip(0.8 + 0.8 * jax.random.uniform(splits[17], (2, FF), jnp.float32) ** steps_of(splits[17], (2, FF), ((1, 16),), -0.2, 0.2), 0.8, 1.6),
        "reduce_lower": noise(splits[18], (FF, RANK), FF ** -0.5, 0.078125, ((0, 16),), jnp.float32),
        "reduce_upper": noise(splits[19], (RANK, MODEL_DIMENSION), 0.1, 0.6, (), jnp.float32),
        "reduce_magnitude": jnp.clip(jax.random.uniform(splits[20], (MODEL_DIMENSION,), jnp.float32, 0.8, 2.0), 0.8, 2.0),
        "cotangent": noise(splits[21], (PACKED_ROWS, PACKED_LENGTH, MODEL_DIMENSION), 1.0, 6.0, ((1, 8),)),
    }


epsilon = 1e-05
adapter_scale = 2.0
rotary_base = 10000.0
top_precision = lax.Precision.HIGHEST

@jax.custom_vjp
def low(v):
    return lax.optimization_barrier(v.astype(jnp.bfloat16)).astype(jnp.float32)

@jax.custom_vjp
def low_back(v):
    return v

def low_keep(v):
    return (low(v), None)

def low_pass(kept, grad):
    return (grad,)

def back_keep(v):
    return (v, None)

def back_low(kept, grad):
    return (low(grad),)
low.defvjp(low_keep, low_pass)
low_back.defvjp(back_keep, back_low)

def merged(base_weights, down_factor, up_factor, magnitude):
    combined_weight = base_weights + adapter_scale * jnp.dot(down_factor, up_factor, precision=top_precision)
    column = jnp.sqrt(lax.optimization_barrier(jnp.sum(combined_weight * combined_weight, axis=0)))
    return low(combined_weight * (magnitude / column))

def rms_norm(tensor, scaling):
    return tensor * lax.rsqrt(lax.optimization_barrier(jnp.mean(tensor * tensor, axis=-1, keepdims=True)) + epsilon) * scaling

def rotate(tensor, cosine, sine_part):
    half_width = tensor.shape[-1] // 2
    turned = jnp.concatenate([-tensor[..., half_width:], tensor[..., :half_width]], axis=-1)
    return tensor * cosine + turned * sine_part

def project(tensor, weight):
    return jnp.einsum('rld,de->rle', tensor, weight, precision=top_precision)

def attend_row(pieces):
    row_queries, row_keys, row_values, row_allowed = pieces
    raw_scores = low_back(jnp.einsum('qhd,khd->hqk', row_queries, row_keys, precision=top_precision) / HD ** 0.5)
    masked = jnp.where(row_allowed[None], raw_scores, -1e+30)
    row_peak = lax.optimization_barrier(jnp.max(masked, axis=-1, keepdims=True))
    powers = jnp.exp(masked - row_peak)
    attention_probs = low(powers / lax.optimization_barrier(jnp.sum(powers, axis=-1, keepdims=True)))
    return jnp.einsum('hqk,khd->qhd', attention_probs, row_values, precision=top_precision)

def reference(hidden, segments, key_attendable, attention_gain, feedforward_gain, attend_frozen, output_frozen, expand_frozen, reduce_frozen, attend_lower, attend_upper, attend_magnitude, output_lower, output_upper, output_magnitude, expand_lower, expand_upper, expand_magnitude, reduce_lower, reduce_upper, reduce_magnitude, cotangent):
    batch_rows = segments.shape[0]
    length = segments.shape[1]
    levels = jnp.arange(SEGS, dtype=jnp.int32)
    below_count = lax.optimization_barrier(jnp.sum((segments[:, None, :] < levels[None, :, None]).astype(jnp.float32), axis=2))
    seg_begin = lax.optimization_barrier(jnp.sum((segments[:, :, None] == levels[None, None, :]).astype(jnp.float32) * below_count[:, None, :], axis=2))
    places = jnp.arange(length).astype(jnp.float32)[None, :] - seg_begin
    frequency = rotary_base ** (-(2.0 * jnp.arange(HD // 2).astype(jnp.float32)) / HD)
    angles = places[:, :, None] * frequency[None, None, :]
    angles = jnp.concatenate([angles, angles], axis=-1)[:, :, None, :]
    cosine = jnp.cos(angles)
    sine_part = jnp.sin(angles)
    token_positions = jnp.arange(length, dtype=jnp.int32)
    causal = token_positions[None, :] <= token_positions[:, None]
    diagonal = token_positions[None, :] == token_positions[:, None]
    same_segment = segments[:, :, None] == segments[:, None, :]
    open_keys = (key_attendable[:, None, :] == 1) | diagonal[None]
    allowed = same_segment & causal[None] & open_keys
    gain_one = attention_gain.astype(jnp.float32)
    gain_two = feedforward_gain.astype(jnp.float32)
    attend_base = attend_frozen.astype(jnp.float32)
    output_base = output_frozen.astype(jnp.float32)
    expand_base = expand_frozen.astype(jnp.float32)
    reduce_base = reduce_frozen.astype(jnp.float32)

    def forward(inputs, *adapters):
        lower_attend, upper_attend, scale_attend, lower_output, upper_output, scale_output, lower_expand, upper_expand, scale_expand, lower_reduce, upper_reduce, scale_reduce = adapters
        weight_query = merged(attend_base[0], lower_attend[0], upper_attend[0], scale_attend[0])
        weight_key = merged(attend_base[1], lower_attend[1], upper_attend[1], scale_attend[1])
        weight_value = merged(attend_base[2], lower_attend[2], upper_attend[2], scale_attend[2])
        weight_out = merged(output_base, lower_output, upper_output, scale_output)
        weight_gate = merged(expand_base[0], lower_expand[0], upper_expand[0], scale_expand[0])
        weight_up = merged(expand_base[1], lower_expand[1], upper_expand[1], scale_expand[1])
        weight_reduce = merged(reduce_base, lower_reduce, upper_reduce, scale_reduce)
        normed_one = low(rms_norm(inputs, gain_one))
        queries = low_back(project(normed_one, weight_query)).reshape(batch_rows, length, HEADS, HD)
        queries = low(rotate(queries, cosine, sine_part))
        keys = low_back(project(normed_one, weight_key)).reshape(batch_rows, length, HEADS, HD)
        keys = low(rotate(keys, cosine, sine_part))
        values = low(low_back(project(normed_one, weight_value))).reshape(batch_rows, length, HEADS, HD)
        mixed_heads = lax.map(jax.checkpoint(attend_row), (queries, keys, values, allowed))
        mixed_heads = low(low_back(mixed_heads.reshape(batch_rows, length, HEADS * HD)))
        resid = inputs + low_back(project(mixed_heads, weight_out))
        normed_two = low(rms_norm(resid, gain_two))
        gate_proj = low_back(project(normed_two, weight_gate))
        up_proj = low_back(project(normed_two, weight_up))
        activated = low(gate_proj * jax.nn.sigmoid(gate_proj) * up_proj)
        return resid + low_back(project(activated, weight_reduce))
    inputs = hidden.astype(jnp.float32)
    adapters = (attend_lower, attend_upper, attend_magnitude, output_lower, output_upper, output_magnitude, expand_lower, expand_upper, expand_magnitude, reduce_lower, reduce_upper, reduce_magnitude)
    block_out, pull_back = jax.vjp(forward, inputs, *adapters)
    grads = pull_back(cotangent.astype(jnp.float32))
    return (block_out.astype(jnp.bfloat16), grads[0], grads[1], grads[2], grads[3], grads[4], grads[5], grads[6], grads[7], grads[8], grads[9], grads[10], grads[11], grads[12])
```

```python
import jax
import jax.numpy as jnp
from jax import lax
from jax.experimental import pallas as pl
from jax.experimental.pallas import tpu as pltpu
from jax.sharding import PartitionSpec as P

HD = 128
SEGS = 4
X = 4
Y = 4
Z = 4

epsilon = 1e-05
adapter_scale = 2.0
rotary_base = 10000.0
F32 = jnp.float32
BF16 = jnp.bfloat16


def roll_blocks(a, axis, start):
    n = a.shape[axis]
    return lax.dynamic_slice_in_dim(jnp.concatenate([a, a], axis=axis), start, n, axis)


def halves(a):
    high = lax.reduce_precision(a, 8, 7)
    return high.astype(BF16), (a - high).astype(BF16)


def dot32(a, b, dims):
    return lax.dot_general(a, b, (dims, ((), ())), preferred_element_type=F32)


def exact_dot(bf, full, dims):
    high, low = halves(full)
    return dot32(bf, high, dims) + dot32(bf, low, dims)


def exact_dot_left(full, bf, dims):
    high, low = halves(full)
    return dot32(high, bf, dims) + dot32(low, bf, dims)


def rotate(tensor, cosine, sine_part):
    half_width = tensor.shape[-1] // 2
    turned = jnp.concatenate([-tensor[..., half_width:], tensor[..., :half_width]], axis=-1)
    return tensor * cosine + turned * sine_part


MESH = pl.DeviceIdType.MESH
ANY = pl.BlockSpec(memory_space=pl.ANY)
VM = pl.BlockSpec(memory_space=pltpu.VMEM)
NEAR_LAST = (2, 1, 3)


def place():
    ctx = lax.axis_index("ctx")
    tp = lax.axis_index("tp")
    return ctx // 2, ctx % 2, tp // X, tp % X


def device(dz=0, dc=0, dy=0, dx=0):
    z, core, y, x = place()
    return (((z + dz) % Z) * 2 + (core + dc) % 2, ((y + dy) % Y) * X + (x + dx) % X)


def greet(devices):
    barrier = pltpu.get_barrier_semaphore()
    for d in devices:
        pl.semaphore_signal(barrier, inc=1, device_id=d, device_id_type=MESH)
    pl.semaphore_wait(barrier, len(devices))


def send(src, dst, send_sem, recv_sem, to):
    copy = pltpu.make_async_remote_copy(
        src_ref=src,
        dst_ref=dst,
        send_sem=send_sem,
        recv_sem=recv_sem,
        device_id=to,
        device_id_type=MESH,
    )
    copy.start()
    return copy


def keep(src, dst, sem):
    copy = pltpu.make_async_copy(src, dst, sem)
    copy.start()
    return copy


def dma(*shape):
    return pltpu.SemaphoreType.DMA(shape)


def call(kernel, outs, in_specs, out_specs, scratch, number, flops, moved):
    return pl.pallas_call(
        kernel,
        out_shape=outs,
        in_specs=in_specs,
        out_specs=out_specs,
        scratch_shapes=scratch,
        cost_estimate=pl.CostEstimate(flops=flops, bytes_accessed=moved, transcendentals=0),
        compiler_params=pltpu.CompilerParams(
            collective_id=number, has_side_effects=True, vmem_limit_bytes=58 * 2**20
        ),
    )


def mask_of(begin, spot_q, key_tag, key_spot):
    return ((key_tag >= begin) & (key_tag <= spot_q)) | (key_spot == spot_q)


KB = 512


def tiles(total, size):
    return [(s, min(size, total - s)) for s in range(0, total, size)]


PIECES = 3


def relay_plan(weights, send_a, recv_a, send_b, recv_b, send_s, recv_s, cols):
    def begin(p, own, start, size):
        return [
            send(own, weights(1, start, size), send_a.at[p, 0], recv_a.at[p, 0], device(dx=1)),
            send(own, weights(3, start, size), send_a.at[p, 1], recv_a.at[p, 1], device(dx=3)),
        ]

    def relay(p, copies, start, size):
        half = size // 2
        more = []
        for k, (slot, at, to) in enumerate(((1, start, 1), (3, start + half, 3))):
            copies[k].wait_recv()
            more.append(
                send(
                    weights(slot, at, half), weights(2, at, half),
                    send_b.at[p, k], recv_b.at[p, k], device(dx=to),
                )
            )
            there = weights(slot, start, size)
            more.append(send(there, there, send_s.at[p, k], recv_s.at[p, k], device(dc=1)))
        return more

    def relay_far(p, more, start, size):
        more[0].wait_recv()
        more[2].wait_recv()
        there = weights(2, start, size)
        return send(there, there, send_s.at[p, 2], recv_s.at[p, 2], device(dc=1))

    def finish(copies, more, last):
        more[1].wait_recv()
        more[3].wait_recv()
        last.wait_recv()
        for copy in copies + more + [last]:
            copy.wait_send()

    return begin, relay, relay_far, finish


def front_kernel(
    hid_ref, gain_ref, fa_ref, la_ref, ua_ref, maga_ref, thin_ref, fw_ref, aw_ref, bw_ref,
    mage_ref, mago_ref, el_ref, small_ref, cos_ref, sin_ref, begin_ref, tag_ref,
    mixed_out, soft_out, log_out, kv_out, weights_out, wq_out, q_out, pre_out, thr_out,
    cola_out, cole_out, sq_out, ina_out, ine_out, ino_out, n1_out, small_out,
    kv_all, score, soft, logs, mixed, mixed_x, joined, w_own, wq_all, normed, kv_own, small,
    sq_x, sq_y, sq_one, ja,
    kv_send, kv_recv, sib_send, sib_recv, a_send, a_recv, b_send, b_recv, ws_send, ws_recv,
    m_send, m_recv, sq_send, sq_recv, sm_send, sm_recv, local, n_local,
):
    z, core, y, x = place()
    me = z * 2 + core
    rows, here, width = hid_ref.shape
    length = Z * 2 * here
    count = fw_ref.shape[0]
    ff = (count - HD) // 3
    piece = here // Y
    cols = pl.ds(pl.multiple_of(core * (width // 2), width // 2), width // 2)
    greet(
        [device(dx=d) for d in (1, 2, 3)]
        + [device(dy=d) for d in (1, 2, 3)]
        + [device(dz=d) for d in (1, 2, 3)]
        + [device(dc=1)]
    )

    def join(matrix, start, size, at):
        low = dot32(aw_ref[start : start + size], bw_ref[matrix, :, at], ((1,), (0,)))
        return fw_ref[start : start + size, at].astype(F32) + adapter_scale * low

    for s, size in tiles(width, 512):
        at = slice(s, s + size)
        one = join(0, 0, HD, at)
        two = join(3, HD + 2 * ff, ff, at)
        sq_one[0:1, at] = jnp.sum(one * one, axis=0, keepdims=True)
        sq_one[1:2, at] = jnp.sum(two * two, axis=0, keepdims=True)
    sq_copies = [
        send(sq_one, sq_x.at[d - 1], sq_send.at[0, d - 1], sq_recv.at[0, d - 1], device(dx=d))
        for d in NEAR_LAST
    ]

    def there(slot, start, size):
        return weights_out.at[slot, pl.ds(start, size), cols]

    begin, relay, relay_far, finish = relay_plan(
        there, a_send, a_recv, b_send, b_recv, ws_send, ws_recv, cols
    )
    where = ((HD, ff), (HD + ff, ff), (0, HD))
    sent, more, last = {}, {}, {}
    for m in range(2):
        start = HD + m * ff
        total = jnp.zeros((ff, 1), F32)
        for s, size in tiles(width, 512):
            at = slice(s, s + size)
            value = join(1 + m, start, ff, at)
            joined[:, at] = value
            total = total + jnp.sum(value * value, axis=1, keepdims=True)
        column = jnp.sqrt(total)
        cole_out[m * ff : (m + 1) * ff] = column
        magnitude = mage_ref[m * ff : (m + 1) * ff]
        ratio = magnitude / column
        for s, size in tiles(width, 512):
            at = slice(s, s + size)
            w_own[start : start + ff, at] = (joined[:, at] * ratio).astype(BF16)
        sent[m] = begin(m, w_own.at[pl.ds(start, ff), cols], start, ff)
        inner = dot32(w_own[start : start + ff], el_ref[...], ((1,), (0,)))
        ine_out[m * ff : (m + 1) * ff] = inner / ratio
        source = small_ref[0:ff, m * 16 : (m + 1) * 16]
        small[0:ff, m * 16 : (m + 1) * 16] = (source * ratio).astype(BF16)
        small[0:ff, (3 + m) * 16 : (4 + m) * 16] = (source / (magnitude * column)).astype(BF16)
    small[0:ff, 32:48] = small_ref[0:ff, 32:48].astype(BF16)
    small[0:ff, 80:] = jnp.zeros((ff, HD - 80), BF16)
    small[ff:] = small_ref[ff:].astype(BF16)
    sm_copies = [
        send(small, small_out.at[d], sm_send.at[d - 1], sm_recv.at[d - 1], device(dx=d))
        for d in NEAR_LAST
    ]
    own = [keep(small, small_out.at[0], local.at[0])]
    for copy in sq_copies:
        copy.wait()
    sq_one[...] += sq_x[0] + sq_x[1] + sq_x[2]
    sq_copies = [
        send(sq_one, sq_y.at[d - 1], sq_send.at[1, d - 1], sq_recv.at[1, d - 1], device(dy=d))
        for d in NEAR_LAST
    ]
    for m in range(3):
        total = jnp.zeros((1, HD), F32)
        for s, size in tiles(width, 512):
            at = slice(s, s + size)
            value = fa_ref[m, at].astype(F32) + adapter_scale * dot32(
                la_ref[m, at], ua_ref[m], ((1,), (0,))
            )
            ja[at] = value
            total = total + jnp.sum(value * value, axis=0, keepdims=True)
        column = jnp.sqrt(total)
        cola_out[m : m + 1] = column
        ratio = maga_ref[m : m + 1] / column
        wq_all[:, m * HD : (m + 1) * HD] = (ja[...] * ratio).astype(BF16)
        inner = dot32(la_ref[m], ja[...].astype(BF16), ((0,), (0,)))
        ina_out[m] = inner[0:16] + inner[32:48]
    own.append(keep(wq_all, wq_out, local.at[1]))
    kv_copies, sib_copies, n_copies = [], [], []
    gain = gain_ref[...]
    for r in range(rows):
        inputs = hid_ref[r].astype(F32)
        inverse = lax.rsqrt(jnp.mean(inputs * inputs, axis=1, keepdims=True) + epsilon)
        if r >= 2:
            n_copies[r - 2].wait()
        normed[r % 2] = (inputs * inverse * gain).astype(BF16)
        n_copies.append(keep(normed.at[r % 2], n1_out.at[r], n_local.at[r]))
        pre = dot32(normed[r % 2], wq_all[...], ((1,), (0,)))
        pre_out[r] = pre
        thin = dot32(normed[r % 2], thin_ref[...], ((1,), (0,)))
        thr_out[r] = thin
        cosine, sine = cos_ref[r], sin_ref[r]
        q_out[r] = rotate(pre[:, :HD], cosine, sine).astype(BF16)
        kv_own[r, :, :HD] = rotate(pre[:, HD : 2 * HD], cosine, sine).astype(BF16)
        kv_own[r, :, HD:] = pre[:, 2 * HD :].astype(BF16)
        for d in NEAR_LAST:
            kv_copies.append(
                send(
                    kv_own.at[r], kv_all.at[me, r], kv_send.at[r, d - 1], kv_recv.at[r, d - 1],
                    device(dz=d),
                )
            )
        sib_copies.append(
            send(kv_own.at[r], kv_all.at[me, r], sib_send.at[r, 0], sib_recv.at[r, 0], device(dc=1))
        )
    own.append(keep(kv_own, kv_all.at[me], local.at[2]))
    for copy in sq_copies:
        copy.wait()
    squares = sq_one[...] + (sq_y[0] + sq_y[1] + sq_y[2])
    sq_out[...] = squares
    ratios = mago_ref[...] / jnp.sqrt(squares)
    for s, size in tiles(width, 512):
        at = slice(s, s + size)
        one = join(0, 0, HD, at)
        two = join(3, HD + 2 * ff, ff, at)
        w_own[0:HD, at] = (one * ratios[0:1, at]).astype(BF16)
        w_own[HD + 2 * ff :, at] = (two * ratios[1:2, at]).astype(BF16)
        ino_out[0:16, at] = dot32(small[ff:], one.astype(BF16), ((0,), (0,)))[0:16]
        ino_out[16:32, at] = dot32(small[0:ff], two.astype(BF16), ((0,), (0,)))[32:48]
    sent[2] = begin(2, w_own.at[pl.ds(0, HD), cols], 0, HD)
    own.append(keep(w_own, weights_out.at[0], local.at[3]))
    more[0] = relay(0, sent[0], *where[0])

    def pass_kv(r):
        for k, d in enumerate(NEAR_LAST):
            kv_copies[3 * r + k].wait_recv()
            slot = ((z + Z - d) % Z) * 2 + core
            at = kv_all.at[slot, r]
            sib_copies.append(send(at, at, sib_send.at[r, d], sib_recv.at[r, d], device(dc=1)))

    for r in range(rows):
        pass_kv(r)
    more[1] = relay(1, sent[1], *where[1])
    own[2].wait()
    for copy in sib_copies:
        copy.wait_recv()
    own.append(keep(kv_all, kv_out, local.at[4]))
    spot_q = lax.broadcasted_iota(jnp.int32, (here, 1), 0) + me * here
    m_copies = []
    for i in (2, 1, 3, 0):
        row = (x + i) % X
        query = q_out[row]
        first = begin_ref[row]
        peak = jnp.full((here, 1), -1e30, F32)
        for b in range(length // KB):
            keys = jnp.concatenate(
                [kv_all[b * (KB // here) + k, row, :, :HD] for k in range(KB // here)], axis=0
            )
            raw = dot32(query, keys, ((1,), (1,))) * (HD**-0.5)
            key_spot = lax.broadcasted_iota(jnp.int32, (1, KB), 1) + b * KB
            ok = mask_of(first, spot_q, tag_ref[row, :, b * KB : (b + 1) * KB], key_spot)
            raw = jnp.where(ok, raw, -1e30)
            score[:, b * KB : (b + 1) * KB] = raw
            peak = jnp.maximum(peak, jnp.max(raw, axis=1, keepdims=True))
        total = jnp.zeros((here, 1), F32)
        gathered = jnp.zeros((here, HD), F32)
        for b in range(length // KB):
            power = jnp.exp(score[:, b * KB : (b + 1) * KB] - peak)
            total = total + jnp.sum(power, axis=1, keepdims=True)
            values = jnp.concatenate(
                [kv_all[b * (KB // here) + k, row, :, HD:] for k in range(KB // here)], axis=0
            )
            gathered = gathered + dot32(power.astype(BF16), values, ((1,), (0,)))
        soft[row] = gathered / total
        logs[row] = peak + jnp.log(total)
        for j in range(Y):
            mixed[i, j * piece : (j + 1) * piece] = soft[
                row, pl.ds(pl.multiple_of(((y + j) % Y) * piece, piece), piece)
            ].astype(BF16)
        if i:
            m_copies.append(
                send(mixed.at[i], mixed_x.at[i], m_send.at[i - 1], m_recv.at[i - 1], device(dx=i))
            )
        else:
            mixed_x[0] = mixed[0]
        if i == 2:
            more[2] = relay(2, sent[2], *where[2])
        if i == 3:
            last[0] = relay_far(0, more[0], *where[0])
    own.append(keep(soft, soft_out, local.at[5]))
    own.append(keep(logs, log_out, local.at[6]))
    last[1] = relay_far(1, more[1], *where[1])
    last[2] = relay_far(2, more[2], *where[2])
    for copy in m_copies:
        copy.wait()
    own.append(keep(mixed_x, mixed_out, local.at[7]))
    for copy in kv_copies + sib_copies:
        copy.wait_send()
    for copy in sm_copies:
        copy.wait()
    for p in range(PIECES):
        finish(sent[p], more[p], last[p])
    for copy in n_copies[rows - 2 :]:
        copy.wait()
    own.pop(2)
    for copy in own:
        copy.wait()


def front(
    hidden, gain, fa, la, ua, maga, thin, fw, aw, bw, mage, mago, el, small, cos, sin, begin, tag
):
    rows, here, width = hidden.shape
    count = fw.shape[0]
    ff = (count - HD) // 3
    length = 2 * Z * here
    s = jax.ShapeDtypeStruct
    return call(
        front_kernel,
        (
            s((X, here, HD), BF16),
            s((rows, here, HD), F32),
            s((rows, here, 1), F32),
            s((2 * Z, rows, here, 2 * HD), BF16),
            s((X, count, width), BF16),
            s((width, 3 * HD), BF16),
            s((rows, here, HD), BF16),
            s((rows, here, 3 * HD), F32),
            s((rows, here, HD), F32),
            s((3, HD), F32),
            s((2 * ff, 1), F32),
            s((2, width), F32),
            s((3, 16, HD), F32),
            s((2 * ff, HD), F32),
            s((32, width), F32),
            s((rows, here, width), BF16),
            s((X, ff + HD, HD), BF16),
        ),
        [VM] * 18,
        (ANY,) * 6 + (VM,) * 9 + (ANY, ANY),
        [
            pltpu.VMEM((2 * Z, rows, here, 2 * HD), BF16),
            pltpu.VMEM((here, length), F32),
            pltpu.VMEM((rows, here, HD), F32),
            pltpu.VMEM((rows, here, 1), F32),
            pltpu.VMEM((X, here, HD), BF16),
            pltpu.VMEM((X, here, HD), BF16),
            pltpu.VMEM((ff, width), F32),
            pltpu.VMEM((count, width), BF16),
            pltpu.VMEM((width, 3 * HD), BF16),
            pltpu.VMEM((2, here, width), BF16),
            pltpu.VMEM((rows, here, 2 * HD), BF16),
            pltpu.VMEM((ff + HD, HD), BF16),
            pltpu.VMEM((3, 2, width), F32),
            pltpu.VMEM((3, 2, width), F32),
            pltpu.VMEM((2, width), F32),
            pltpu.VMEM((width, HD), F32),
            dma(rows, 3), dma(rows, 3), dma(rows, 4), dma(rows, 4),
            dma(PIECES, 2), dma(PIECES, 2), dma(PIECES, 2), dma(PIECES, 2),
            dma(PIECES, 3), dma(PIECES, 3),
            dma(3), dma(3), dma(2, 3), dma(2, 3), dma(3), dma(3), dma(8), dma(rows),
        ],
        0,
        2 * 2 * rows * here * length * HD + 2 * rows * here * width * 4 * HD,
        32 * 2**20,
    )(hidden, gain, fa, la, ua, maga, thin, fw, aw, bw, mage, mago, el, small, cos, sin, begin, tag)


def feed_kernel(
    mixed_ref, hid_ref, gain_ref, cot_ref, weights_ref, small_ref, el_ref, upper_ref, mago_ref,
    sq_ref,
    resid_grad_out, block_out, dmix_out, early_out, columns_out, lower_out,
    out_w, gate_w, up_w, down_w, normed, low, act, dgate, dup, sends, recvs, acc, resid_s, mags,
    load, s_send, s_recv, a_send, a_recv, b_send, b_recv, ws_send, ws_recv,
):
    z, core, y, x = place()
    width = hid_ref.shape[1]
    piece = hid_ref.shape[0]
    here = cot_ref.shape[0]
    ff = gate_w.shape[0] // X
    cols = pl.ds(pl.multiple_of(core * (width // 2), width // 2), width // 2)
    down_rows = pl.ds(HD + 2 * ff, ff)
    loads = [[], [], [], []]
    for w, (dst, start, size) in enumerate(((out_w, 0, HD), (gate_w, HD, ff), (up_w, HD + ff, ff))):
        for i in range(X):
            loads[w].append(
                keep(
                    weights_ref.at[i, pl.ds(start, size)], dst.at[pl.ds(i * size, size)],
                    load.at[w, i],
                )
            )
    loads[3].append(keep(weights_ref.at[0, down_rows], down_w.at[pl.ds(0, ff)], load.at[3, 0]))
    greet(
        [device(dy=d) for d in (1, 2, 3)] + [device(dx=1), device(dx=3), device(dc=1)]
    )

    def there(slot, start, size):
        return down_w.at[pl.ds(slot * ff + start, size), cols]

    begin, relay, relay_far, finish = relay_plan(
        there, a_send, a_recv, b_send, b_recv, ws_send, ws_recv, cols
    )
    sent = begin(0, weights_ref.at[0, down_rows, cols], 0, ff)

    def loaded(w):
        for copy in loads[w]:
            copy.wait()

    def start_scatter(k):
        return [
            send(
                sends.at[k, d - 1], recvs.at[k, d - 1], s_send.at[k, d - 1], s_recv.at[k, d - 1],
                device(dy=d),
            )
            for d in NEAR_LAST
        ]

    def put(k, part, start, size):
        acc[k, :, start : start + size] = part[:piece]
        for d in range(1, Y):
            sends[k, d - 1, :, start : start + size] = part[d * piece : (d + 1) * piece].astype(BF16)

    def summed(k, copies):
        for copy in copies:
            copy.wait()
        return acc[k] + (
            recvs[k, 0].astype(F32) + recvs[k, 1].astype(F32) + recvs[k, 2].astype(F32)
        )

    def start_gather(buffer, k):
        return [
            send(
                buffer.at[pl.ds(0, piece)], buffer.at[pl.ds((Y - d) * piece, piece)],
                s_send.at[k, d - 1], s_recv.at[k, d - 1], device(dy=d),
            )
            for d in NEAR_LAST
        ]

    loaded(0)
    mixed_cat = jnp.concatenate([mixed_ref[i] for i in range(X)], axis=1)
    for start, size in tiles(width, 512):
        put(0, dot32(mixed_cat, out_w[:, start : start + size], ((1,), (0,))), start, size)
    copies = start_scatter(0)
    ratios = mago_ref[...] / jnp.sqrt(sq_ref[...])
    upper_o = (upper_ref[0:16] * ratios[0:1]).astype(BF16)
    upper_d = (upper_ref[16:32] * ratios[1:2]).astype(BF16)
    through_down = dot32(cot_ref[...], upper_d, ((1,), (1,))).astype(BF16)
    small = jnp.concatenate([small_ref[i, 0:ff] for i in range(X)], axis=0)
    small_o = jnp.concatenate([small_ref[i, ff:] for i in range(X)], axis=0)
    from_mixed = dot32(mixed_cat, small_o, ((1,), (0,)))[:, 0:16].astype(BF16)
    attended = summed(0, copies)
    acc[0] = attended
    gain = gain_ref[...]
    resid = hid_ref[...].astype(F32) + attended
    inverse = lax.rsqrt(jnp.mean(resid * resid, axis=1, keepdims=True) + epsilon)
    resid_s[...] = resid
    normed[0:piece] = (resid * inverse * gain).astype(BF16)
    copies = start_gather(normed, 3)
    more = relay(0, sent, 0, ff)
    loaded(1)
    loaded(2)
    loaded(3)
    for copy in copies:
        copy.wait()
    far = relay_far(0, more, 0, ff)
    finish(sent, more, far)
    for start, size in tiles(X * ff, 256):
        at = slice(start, start + size)
        gate = dot32(normed[...], gate_w[at], ((1,), (1,)))
        up = dot32(normed[...], up_w[at], ((1,), (1,)))
        d_act = dot32(cot_ref[...], down_w[at], ((1,), (1,)))
        sig = 1.0 / (1.0 + jnp.exp(-gate))
        gated = gate * sig
        act[:, at] = (gated * up).astype(BF16)
        d_gate = (d_act * up * sig * (1.0 + gate * (1.0 - sig))).astype(BF16)
        d_up = (d_act * gated).astype(BF16)
        dgate[:, at] = d_gate
        dup[:, at] = d_up
        mags[0:1, at] = jnp.sum(d_gate.astype(F32) * gate, axis=0, keepdims=True)
        mags[1:2, at] = jnp.sum(d_up.astype(F32) * up, axis=0, keepdims=True)
    for start, size in tiles(width, 512):
        at = slice(start, start + size)
        part = dot32(dgate[...], gate_w[:, at], ((1,), (0,)))
        part = part + dot32(dup[...], up_w[:, at], ((1,), (0,)))
        put(1, part, start, size)
    two_copies = start_scatter(1)
    for start, size in tiles(width, 512):
        at = slice(start, start + size)
        put(2, dot32(act[...], down_w[:, at], ((1,), (0,))), start, size)
    ff_copies = start_scatter(2)
    through = dot32(normed[...], el_ref[...], ((1,), (0,)))
    through = (through[:, 0:32] + through[:, 32:64]).astype(BF16)
    gate_down = dot32(dgate[...], small, ((1,), (0,)))[:, 0:16].astype(BF16)
    up_down = dot32(dup[...], small, ((1,), (0,)))[:, 16:32].astype(BF16)
    from_act = dot32(act[...], small, ((1,), (0,)))[:, 32:48].astype(BF16)
    small_t = jnp.transpose(small.astype(F32))
    pull_gate = (small_t[48:64] * mags[0:1]).astype(BF16)
    pull_up = (small_t[64:80] * mags[1:2]).astype(BF16)

    def columns(row, value):
        for i in range(X):
            columns_out[i, row : row + value.shape[0]] = value[:, i * ff : (i + 1) * ff]

    columns(0, dot32(through[:, 0:16], dgate[...], ((0,), (0,))))
    columns(16, dot32(through[:, 16:32], dup[...], ((0,), (0,))))
    columns(32, dot32(through_down, act[...], ((0,), (0,))))
    columns(48, jnp.concatenate([mags[...], jnp.zeros((6, X * ff), F32)], axis=0))
    early_out[0:16] = dot32(gate_down, normed[...], ((0,), (0,))) - dot32(
        pull_gate, gate_w[...], ((1,), (0,))
    )
    early_out[16:32] = dot32(up_down, normed[...], ((0,), (0,))) - dot32(
        pull_up, up_w[...], ((1,), (0,))
    )
    early_out[48:64] = dot32(from_act, cot_ref[...], ((0,), (0,)))
    d_two = summed(1, two_copies)
    resid = resid_s[...]
    inverse = lax.rsqrt(jnp.mean(resid * resid, axis=1, keepdims=True) + epsilon)
    scaled = d_two * gain
    cot_own = cot_ref[0:piece].astype(F32)
    d_resid = cot_own + (
        inverse * scaled
        - resid * (inverse * inverse * inverse) * jnp.mean(resid * scaled, axis=1, keepdims=True)
    )
    resid_grad_out[...] = d_resid
    own_low = d_resid.astype(BF16)
    low[0:piece] = own_low
    copies = start_gather(low, 4)
    mag_out = jnp.sum(own_low.astype(F32) * acc[0], axis=0, keepdims=True)
    feedforward = summed(2, ff_copies)
    block_out[...] = (resid_s[...] + feedforward).astype(BF16)
    mag_down = jnp.sum(cot_own * feedforward, axis=0, keepdims=True)
    early_out[64:80] = jnp.concatenate(
        [mag_out, mag_down, jnp.zeros((14, width), F32)], axis=0
    )
    for copy in copies:
        copy.wait()
    d_mixed = dot32(low[...], out_w[...], ((1,), (1,))).astype(BF16)
    for i in range(X):
        dmix_out[i] = d_mixed[:, i * HD : (i + 1) * HD]
    through_out = dot32(low[...], upper_o, ((1,), (1,))).astype(BF16)
    value = dot32(through_out, mixed_cat, ((0,), (0,)))
    for i in range(X):
        lower_out[i] = value[:, i * HD : (i + 1) * HD]
    early_out[32:48] = dot32(from_mixed, low[...], ((0,), (0,)))


def feed(mixed_x, hid_own, gain, cot_row, weights, small_x, el, upper, mago, squares):
    here, width = cot_row.shape
    piece = here // Y
    hidden = (weights.shape[1] - HD) // 3 * X
    s = jax.ShapeDtypeStruct
    return call(
        feed_kernel,
        (
            s((piece, width), F32),
            s((piece, width), BF16),
            s((X, here, HD), BF16),
            s((80, width), F32),
            s((X, 56, hidden // X), F32),
            s((X, 16, HD), F32),
        ),
        [VM, VM, VM, VM, ANY, VM, VM, VM, VM, VM],
        (VM,) * 6,
        [
            pltpu.VMEM((X * HD, width), BF16),
            pltpu.VMEM((hidden, width), BF16),
            pltpu.VMEM((hidden, width), BF16),
            pltpu.VMEM((hidden, width), BF16),
            pltpu.VMEM((here, width), BF16),
            pltpu.VMEM((here, width), BF16),
            pltpu.VMEM((here, hidden), BF16),
            pltpu.VMEM((here, hidden), BF16),
            pltpu.VMEM((here, hidden), BF16),
            pltpu.VMEM((3, Y - 1, piece, width), BF16),
            pltpu.VMEM((3, Y - 1, piece, width), BF16),
            pltpu.VMEM((3, piece, width), F32),
            pltpu.VMEM((piece, width), F32),
            pltpu.VMEM((2, hidden), F32),
            dma(4, X), dma(5, 3), dma(5, 3), dma(1, 2), dma(1, 2), dma(1, 2), dma(1, 2),
            dma(1, 3), dma(1, 3),
        ],
        1,
        2 * here * hidden * width * 6,
        32 * 2**20,
    )(mixed_x, hid_own, gain, cot_row, weights, small_x, el, upper, mago, squares)


def attend_back_kernel(
    q_ref, kv_ref, dmix_ref, soft_ref, log_ref, begin_ref, tag_ref, cos_ref, sin_ref, block_ref,
    grads_out, block_out,
    kv_all, dmix_all, dmix_abs, part, own, sib_s, sib_r, z_own, z_s, z_r, dq_s,
    d_send, d_recv, b_send, b_recv, sib_send, sib_recv, z_send, z_recv, local,
):
    z, core, y, x = place()
    me = z * 2 + core
    rows, here = q_ref.shape[0], q_ref.shape[1]
    piece, width = block_ref.shape
    half = width // 2
    load = keep(kv_ref, kv_all, local.at[0])
    greet(
        [device(dx=d) for d in (1, 2, 3)]
        + [device(dy=d) for d in (1, 2, 3)]
        + [device(dz=d) for d in (1, 2, 3)]
        + [device(dc=1)]
    )
    d_copies = [
        send(
            dmix_ref.at[X - d], dmix_all.at[x], d_send.at[d - 1], d_recv.at[d - 1], device(dx=d)
        )
        for d in NEAR_LAST
    ]
    own_mix = keep(dmix_ref.at[0], dmix_all.at[x], local.at[1])
    tokens = pl.ds(pl.multiple_of(y * piece, piece), piece)
    left, right = pl.ds(0, half), pl.ds(half, half)
    own_block = keep(block_ref, block_out.at[x, tokens], local.at[2])
    block_one = []
    for d in NEAR_LAST:
        block_one.append(
            send(
                block_ref.at[:, left], block_out.at[x, tokens, left],
                b_send.at[0, d - 1], b_recv.at[0, d - 1], device(dx=d),
            )
        )
        block_one.append(
            send(
                block_ref.at[:, right], block_out.at[x, tokens, right],
                b_send.at[1, d - 1], b_recv.at[1, d - 1], device(dy=d),
            )
        )
    load.wait()
    own_mix.wait()
    for copy in d_copies:
        copy.wait()
    spot_q = lax.broadcasted_iota(jnp.int32, (here, 1), 0) + me * here
    sib_copies, z_copies, block_two = [], [], []

    def pass_on(r):
        sib_copies[r].wait()
        z_own[r] = own[r, z] + sib_r[r, z].astype(F32)
        for d in NEAR_LAST:
            to = (z + d) % Z
            z_s[r, d - 1] = (own[r, to] + sib_r[r, to].astype(F32)).astype(BF16)
            z_copies.append(
                send(
                    z_s.at[r, d - 1], z_r.at[r, d - 1], z_send.at[r, d - 1], z_recv.at[r, d - 1],
                    device(dz=d),
                )
            )

    def back(a, r):
        cosine, sine = cos_ref[r], sin_ref[r]
        weighted = a * sine
        turned = jnp.concatenate([weighted[:, HD // 2 :], -weighted[:, : HD // 2]], axis=1)
        return a * cosine + turned

    for r in range(rows):
        for j in range(Y):
            dmix_abs[pl.ds(pl.multiple_of(((y + j) % Y) * piece, piece), piece)] = dmix_all[
                r, j * piece : (j + 1) * piece
            ]
        query = q_ref[r]
        grad = dmix_abs[...]
        delta = jnp.sum(grad.astype(F32) * soft_ref[r], axis=1, keepdims=True)
        begin = begin_ref[r]
        log = log_ref[r]
        d_query = jnp.zeros((here, HD), F32)
        for b in range(Z):
            keys = jnp.concatenate([kv_all[2 * b + k, r, :, :HD] for k in range(2)], axis=0)
            values = jnp.concatenate([kv_all[2 * b + k, r, :, HD:] for k in range(2)], axis=0)
            raw = dot32(query, keys, ((1,), (1,))) * (HD**-0.5)
            key_spot = lax.broadcasted_iota(jnp.int32, (1, KB), 1) + b * KB
            ok = mask_of(begin, spot_q, tag_ref[r, :, b * KB : (b + 1) * KB], key_spot)
            probs = jnp.exp(jnp.where(ok, raw, -1e30) - log)
            d_probs = dot32(grad, values, ((1,), (1,)))
            d_scores = (probs * (d_probs - delta)).astype(BF16)
            d_query = d_query + dot32(d_scores, keys, ((1,), (0,)))
            d_keys = dot32(d_scores, query, ((0,), (0,))) * (HD**-0.5)
            d_values = dot32(probs.astype(BF16), grad, ((0,), (0,)))
            for k in range(2):
                part[b, k, :, :HD] = d_keys[k * here : (k + 1) * here]
                part[b, k, :, HD:] = d_values[k * here : (k + 1) * here]
        dq_s[r] = d_query * (HD**-0.5)
        for b in range(Z):
            sib_s[r, b] = part[b, 1 - core].astype(BF16)
            own[r, b] = part[b, core]
        sib_copies.append(
            send(sib_s.at[r], sib_r.at[r], sib_send.at[r], sib_recv.at[r], device(dc=1))
        )
        grads_out[r, :, :HD] = back(dq_s[r], r).astype(BF16)
        if r:
            pass_on(r - 1)
        if r == 1:
            own_block.wait()
            for copy in block_one:
                copy.wait()
            for d in NEAR_LAST:
                spread = block_out.at[:, tokens, left]
                block_two.append(
                    send(
                        spread, spread, b_send.at[2, d - 1], b_recv.at[2, d - 1], device(dy=d)
                    )
                )
                spread = block_out.at[x, :, right]
                block_two.append(
                    send(
                        spread, spread, b_send.at[3, d - 1], b_recv.at[3, d - 1], device(dx=d)
                    )
                )
    pass_on(rows - 1)
    for r in range(rows):
        for copy in z_copies[3 * r : 3 * r + 3]:
            copy.wait()
        total = z_own[r] + (
            z_r[r, 0].astype(F32) + z_r[r, 1].astype(F32) + z_r[r, 2].astype(F32)
        )
        grads_out[r, :, HD : 2 * HD] = back(total[:, :HD], r).astype(BF16)
        grads_out[r, :, 2 * HD :] = total[:, HD:].astype(BF16)
    for copy in block_two:
        copy.wait()


def attend_back(queries, kv, dmix, soft, log, begin, tag, cosine, sine, block):
    rows, here, _ = queries.shape
    piece, width = block.shape
    return call(
        attend_back_kernel,
        (
            jax.ShapeDtypeStruct((rows, here, 3 * HD), BF16),
            jax.ShapeDtypeStruct((rows, here, width), BF16),
        ),
        [VM, ANY, VM, VM, VM, VM, VM, VM, VM, VM],
        (VM, ANY),
        [
            pltpu.VMEM((2 * Z, rows, here, 2 * HD), BF16),
            pltpu.VMEM((rows, here, HD), BF16),
            pltpu.VMEM((here, HD), BF16),
            pltpu.VMEM((Z, 2, here, 2 * HD), F32),
            pltpu.VMEM((rows, Z, here, 2 * HD), F32),
            pltpu.VMEM((rows, Z, here, 2 * HD), BF16),
            pltpu.VMEM((rows, Z, here, 2 * HD), BF16),
            pltpu.VMEM((rows, here, 2 * HD), F32),
            pltpu.VMEM((rows, Z - 1, here, 2 * HD), BF16),
            pltpu.VMEM((rows, Z - 1, here, 2 * HD), BF16),
            pltpu.VMEM((rows, here, HD), F32),
            dma(3), dma(3), dma(4, 3), dma(4, 3), dma(rows), dma(rows), dma(rows, 3), dma(rows, 3),
            dma(3),
        ],
        2,
        2 * 5 * rows * here * 2 * Z * here * HD,
        32 * 2**20,
    )(queries, kv, dmix, soft, log, begin, tag, cosine, sine, block)


def input_grad_kernel(
    grads_ref, weight_ref, hid_ref, gain_ref, dres_ref,
    grad_out,
    rel, send_l, send_r, recv_l, recv_r, acc_l, acc_r, send_2, recv_2, d_one, spread,
    s_one, r_one, s_two, r_two, s_gat, r_gat, local,
):
    z, core, y, x = place()
    rows, here, deep = grads_ref.shape
    piece, width = hid_ref.shape
    half = width // 2
    for i in range(X):
        for j in range(Y):
            rel[i, j] = grads_ref[
                (x + i) % X, pl.ds(pl.multiple_of(((y + j) % Y) * piece, piece), piece)
            ]
    greet([device(dx=d) for d in (1, 2, 3)] + [device(dy=d) for d in (1, 2, 3)])
    one = []
    for d in (2, 1, 3, 0):
        lhs_l = rel[d].reshape(here, deep)
        lhs_r = jnp.concatenate([rel[i, d] for i in range(X)], axis=0)
        for start, size in tiles(half, 512):
            at = slice(start, start + size)
            part = dot32(lhs_l, weight_ref[at], ((1,), (1,)))
            if d:
                send_l[d - 1, :, at] = part.astype(BF16)
            else:
                acc_l[:, at] = part
        if d:
            one.append(
                send(send_l.at[d - 1], recv_l.at[d - 1], s_one.at[0, d - 1], r_one.at[0, d - 1],
                     device(dx=d))
            )
        for start, size in tiles(half, 512):
            at = slice(start, start + size)
            part = dot32(lhs_r, weight_ref[half + start : half + start + size], ((1,), (1,)))
            if d:
                send_r[d - 1, :, at] = part.astype(BF16)
            else:
                acc_r[:, at] = part
        if d:
            one.append(
                send(send_r.at[d - 1], recv_r.at[d - 1], s_one.at[1, d - 1], r_one.at[1, d - 1],
                     device(dy=d))
            )
    for copy in one:
        copy.wait()
    two = []
    for k, (acc, recv) in enumerate(((acc_l, recv_l), (acc_r, recv_r))):
        for d in (2, 1, 3, 0):
            at = slice(d * piece, (d + 1) * piece)
            part = acc[at] + (
                recv[0, at].astype(F32) + recv[1, at].astype(F32) + recv[2, at].astype(F32)
            )
            if d:
                send_2[k, d - 1] = part.astype(BF16)
                two.append(
                    send(send_2.at[k, d - 1], recv_2.at[k, d - 1], s_two.at[k, d - 1],
                         r_two.at[k, d - 1], device(dx=d) if k else device(dy=d))
                )
            else:
                d_one[:, k * half : (k + 1) * half] = part
    for copy in two:
        copy.wait()
    for k in range(2):
        d_one[:, k * half : (k + 1) * half] += (
            recv_2[k, 0].astype(F32) + recv_2[k, 1].astype(F32) + recv_2[k, 2].astype(F32)
        )
    inputs = hid_ref[...].astype(F32)
    inverse = lax.rsqrt(jnp.mean(inputs * inputs, axis=1, keepdims=True) + epsilon)
    scaled = d_one[...] * gain_ref[...]
    result = dres_ref[...] + (
        inverse * scaled
        - inputs * (inverse * inverse * inverse) * jnp.mean(inputs * scaled, axis=1, keepdims=True)
    )
    tokens = pl.ds(pl.multiple_of(y * piece, piece), piece)
    left, right = pl.ds(0, half), pl.ds(half, half)
    spread[x, tokens] = result.astype(BF16)
    gat = []
    for d in NEAR_LAST:
        for k, (cut, to) in enumerate(((left, device(dx=d)), (right, device(dy=d)))):
            at = spread.at[x, tokens, cut]
            gat.append(send(at, at, s_gat.at[k, d - 1], r_gat.at[k, d - 1], to))
    for copy in gat:
        copy.wait()
    gat = []
    for d in NEAR_LAST:
        at = spread.at[:, tokens, left]
        gat.append(send(at, at, s_gat.at[2, d - 1], r_gat.at[2, d - 1], device(dy=d)))
        at = spread.at[x, :, right]
        gat.append(send(at, at, s_gat.at[3, d - 1], r_gat.at[3, d - 1], device(dx=d)))
    for copy in gat:
        copy.wait()
    out = keep(spread, grad_out, local.at[0])
    out.wait()


def input_grad(grads, weight, hid_own, gain, d_resid):
    rows, here, deep = grads.shape
    piece, width = hid_own.shape
    half = width // 2
    return call(
        input_grad_kernel,
        jax.ShapeDtypeStruct((rows, here, width), BF16),
        [VM] * 5,
        ANY,
        [
            pltpu.VMEM((X, Y, piece, deep), BF16),
            pltpu.VMEM((3, here, half), BF16),
            pltpu.VMEM((3, here, half), BF16),
            pltpu.VMEM((3, here, half), BF16),
            pltpu.VMEM((3, here, half), BF16),
            pltpu.VMEM((here, half), F32),
            pltpu.VMEM((here, half), F32),
            pltpu.VMEM((2, 3, piece, half), BF16),
            pltpu.VMEM((2, 3, piece, half), BF16),
            pltpu.VMEM((piece, width), F32),
            pltpu.VMEM((rows, here, width), BF16),
            dma(2, 3), dma(2, 3), dma(2, 3), dma(2, 3), dma(4, 3), dma(4, 3), dma(1),
        ],
        3,
        2 * rows * here * deep * width,
        16 * 2**20,
    )(grads, weight, hid_own, gain, d_resid)


def sums_kernel(
    all_ref, block_ref, lower_ref, ctx_ref,
    all_out, block_out, ctx_out,
    c_r, z_s, z_r, x_s, x_r, y_s, y_r, gath, bx_r, lx_r, b_one, b_two, e_one, e_two, e_z, b_z,
    ss, rs,
):
    z, core, y, x = place()
    n, width = all_ref.shape
    nc, nz = n // 2, n // 2 // Z
    wx, wy = width // X, width // X // Y
    rank = lower_ref.shape[1]
    greet(
        [device(dx=d) for d in (1, 2, 3)]
        + [device(dy=d) for d in (1, 2, 3)]
        + [device(dz=d) for d in (1, 2, 3)]
        + [device(dc=1)]
    )

    def go(k, d, src, dst, to):
        return send(src, dst, ss.at[k, d], rs.at[k, d], to)

    def ds(index, size):
        return pl.ds(pl.multiple_of(index * size, size), size)

    def done(copies):
        for copy in copies:
            copy.wait()

    first = [go(0, 0, all_ref.at[ds(1 - core, nc)], c_r, device(dc=1))]
    slots = []
    for d in NEAR_LAST:
        slots.append(go(1, d, block_ref.at[X - d], bx_r.at[d - 1], device(dx=d)))
        slots.append(go(2, d, lower_ref.at[X - d], lx_r.at[d - 1], device(dx=d)))
    done(first)
    z_s[...] = all_ref[ds(core, nc)] + c_r[...]
    zc = [go(3, d, z_s.at[ds((z + d) % Z, nz)], z_r.at[d - 1], device(dz=d)) for d in NEAR_LAST]
    done(slots)
    b_one[...] = block_ref[0] + (bx_r[0] + bx_r[1] + bx_r[2])
    e_one[:rank] = lower_ref[0] + (lx_r[0] + lx_r[1] + lx_r[2])
    e_one[rank:] = ctx_ref[...]
    cc = [
        go(4, 0, b_one, b_two, device(dc=1)),
        go(5, 0, e_one, e_two, device(dc=1)),
    ]
    done(cc)
    b_two[...] += b_one[...]
    e_two[...] += e_one[...]
    cz = []
    for d in NEAR_LAST:
        cz.append(go(6, d, b_two, b_z.at[d - 1], device(dz=d)))
        cz.append(go(7, d, e_two, e_z.at[d - 1], device(dz=d)))
    done(zc)
    x_s[...] = z_s[ds(z, nz)] + (z_r[0] + z_r[1] + z_r[2])
    xc = [go(8, d, x_s.at[:, ds((x + d) % X, wx)], x_r.at[d - 1], device(dx=d)) for d in NEAR_LAST]
    done(xc)
    y_s[...] = x_s[:, ds(x, wx)] + (x_r[0] + x_r[1] + x_r[2])
    yc = [go(9, d, y_s.at[:, ds((y + d) % Y, wy)], y_r.at[d - 1], device(dy=d)) for d in NEAR_LAST]
    done(yc)
    mine = ds(core * Z + z, nz)
    at_y = x * Y + y
    gath[mine, ds(at_y, wy)] = y_s[:, ds(y, wy)] + (y_r[0] + y_r[1] + y_r[2])
    spot = gath.at[mine, ds(at_y, wy)]
    done([go(10, d, spot, spot, device(dy=d)) for d in NEAR_LAST])
    spot = gath.at[mine, ds(x, wx)]
    done([go(11, d, spot, spot, device(dx=d)) for d in NEAR_LAST])
    spot = gath.at[mine]
    done([go(12, d, spot, spot, device(dz=d)) for d in NEAR_LAST])
    spot = gath.at[ds(core, nc)]
    done([go(13, 0, spot, spot, device(dc=1))])
    all_out[...] = gath[...]
    done(cz)
    block_out[...] = b_two[...] + (b_z[0] + b_z[1] + b_z[2])
    ctx_out[...] = e_two[...] + (e_z[0] + e_z[1] + e_z[2])


def sums(everywhere, block, lower, local):
    n, width = everywhere.shape
    _, bn, bw = block.shape
    rank = lower.shape[1]
    en = local.shape[0] + rank
    nc, nz = n // 2, n // 2 // Z
    wx, wy = width // X, width // X // Y
    return call(
        sums_kernel,
        (
            jax.ShapeDtypeStruct((n, width), F32),
            jax.ShapeDtypeStruct((bn, bw), F32),
            jax.ShapeDtypeStruct((en, HD), F32),
        ),
        [VM] * 4,
        (VM,) * 3,
        [
            pltpu.VMEM((nc, width), F32),
            pltpu.VMEM((nc, width), F32),
            pltpu.VMEM((3, nz, width), F32),
            pltpu.VMEM((nz, width), F32),
            pltpu.VMEM((3, nz, wx), F32),
            pltpu.VMEM((nz, wx), F32),
            pltpu.VMEM((3, nz, wy), F32),
            pltpu.VMEM((n, width), F32),
            pltpu.VMEM((3, bn, bw), F32),
            pltpu.VMEM((3, rank, HD), F32),
            pltpu.VMEM((bn, bw), F32),
            pltpu.VMEM((bn, bw), F32),
            pltpu.VMEM((en, HD), F32),
            pltpu.VMEM((en, HD), F32),
            pltpu.VMEM((3, en, HD), F32),
            pltpu.VMEM((3, bn, bw), F32),
            dma(14, 4), dma(14, 4),
        ],
        4,
        2**20,
        2**22,
    )(everywhere, block, lower, local)


def on_device(
    hidden,
    segments,
    key_attendable,
    attention_gain,
    feedforward_gain,
    attend_frozen,
    output_frozen,
    expand_frozen,
    reduce_frozen,
    attend_lower,
    attend_upper,
    attend_magnitude,
    output_lower,
    output_upper,
    output_magnitude,
    expand_lower,
    expand_upper,
    expand_magnitude,
    reduce_lower,
    reduce_upper,
    reduce_magnitude,
    cotangent,
):
    rows, here, width = hidden.shape
    length = segments.shape[1]
    ff = reduce_frozen.shape[0]
    flat = rows * here
    piece = here // Y
    rank = output_lower.shape[1]
    ctx = lax.axis_index("ctx")
    tp = lax.axis_index("tp")
    y, x = tp // X, tp % X
    offset = ctx * here
    share = 1.0 / (2 * Z)

    def left_factor(a):
        high, low = halves(a)
        return jnp.concatenate([high, high, low], axis=-1)

    def right_factor(a):
        high, low = halves(a)
        return jnp.concatenate([high, low, high], axis=-2)

    fw = jnp.concatenate(
        [output_frozen, expand_frozen[0].T, expand_frozen[1].T, reduce_frozen], axis=0
    )
    expand_upper_t = expand_upper.transpose(0, 2, 1)
    aw = left_factor(
        jnp.concatenate([output_lower, expand_upper_t[0], expand_upper_t[1], reduce_lower], axis=0)
    )
    bw = right_factor(
        jnp.stack([output_upper, expand_lower[0].T, expand_lower[1].T, reduce_upper], axis=0)
    )
    la = left_factor(attend_lower)
    ua = right_factor(attend_upper)
    flat_lower = attend_lower.transpose(1, 0, 2).reshape(width, 3 * rank)
    high, low = halves(flat_lower)
    thin = jnp.concatenate([high, low, jnp.zeros((width, HD - 6 * rank), BF16)], axis=1)
    flat_lower = expand_lower.transpose(1, 0, 2).reshape(width, 2 * rank)
    high, low = halves(flat_lower)
    el = jnp.concatenate([high, low, jnp.zeros((width, HD - 4 * rank), BF16)], axis=1)
    small = jnp.concatenate([expand_upper_t[0], expand_upper_t[1], reduce_lower], axis=1)
    small = jnp.concatenate(
        [
            jnp.pad(small, ((0, 0), (0, HD - 3 * rank))),
            jnp.pad(output_lower, ((0, 0), (0, HD - rank))),
        ],
        axis=0,
    )
    mago = jnp.stack([output_magnitude, reduce_magnitude])
    upper = jnp.concatenate([output_upper, reduce_upper], axis=0)

    levels = jnp.arange(SEGS, dtype=jnp.int32)
    below_count = jnp.sum((segments[:, None, :] < levels[None, :, None]).astype(F32), axis=2)
    segments_here = lax.dynamic_slice_in_dim(segments, offset, here, 1)
    begin_here = jnp.sum(
        (segments_here[:, :, None] == levels[None, None, :]).astype(F32) * below_count[:, None, :],
        axis=2,
    )
    spot_here = offset + jnp.arange(here, dtype=jnp.int32)
    places = spot_here.astype(F32)[None, :] - begin_here
    frequency = rotary_base ** (-(2.0 * jnp.arange(HD // 2).astype(F32)) / HD)
    frequency = jnp.concatenate([frequency, frequency])
    angles = places[:, :, None] * frequency[None, None, :]
    cosine, sine_part = jnp.cos(angles), jnp.sin(angles)
    spots = jnp.arange(length, dtype=jnp.int32)[None]
    key_tag = jnp.where(key_attendable == 1, spots, -1)[:, None, :]
    begin = begin_here.astype(jnp.int32)[:, :, None]
    gain_one = attention_gain.astype(F32)
    gain_two = feedforward_gain.astype(F32)

    def take_row(a):
        mine = lax.dynamic_index_in_dim(a, x, 0, keepdims=False)
        return roll_blocks(mine.reshape(Y, piece, width), 0, y)

    (
        mixed_parts,
        soft,
        log_total,
        all_pairs,
        weights_x,
        weight_attend,
        queries,
        pre,
        through_three,
        column_attend,
        column_expand,
        squares,
        inner_attend,
        inner_expand,
        inner_both,
        normed_one,
        small_x,
    ) = front(
        hidden,
        gain_one[None],
        attend_frozen,
        la,
        ua,
        attend_magnitude,
        thin,
        fw,
        aw,
        bw,
        expand_magnitude.reshape(2 * ff, 1),
        mago,
        el,
        small,
        cosine,
        sine_part,
        begin,
        key_tag,
    )
    hid_own = take_row(hidden)[0]
    cot_row = take_row(cotangent).reshape(here, width)
    d_resid, block_own, d_mixed_parts, early, block_x, lower_out = feed(
        mixed_parts, hid_own, gain_two[None], cot_row, weights_x, small_x, el, upper, mago, squares
    )
    grads_low, block_output = attend_back(
        queries,
        all_pairs,
        d_mixed_parts,
        soft,
        log_total,
        begin,
        key_tag,
        cosine,
        sine_part,
        block_own,
    )
    hidden_grad = input_grad(grads_low, weight_attend, hid_own, gain_one[None], d_resid)
    hidden_grad = hidden_grad.astype(F32)
    pre = pre.reshape(flat, 3 * HD)
    through_three = through_three.reshape(flat, HD)
    normed_one = normed_one.reshape(flat, width)

    late = []
    local = []
    mags = []
    through_three = through_three[:, : 3 * rank] + through_three[:, 3 * rank : 6 * rank]
    flat_grads = grads_low.reshape(flat, 3, HD)
    flat_pre = pre.reshape(flat, 3, HD)
    downs = []
    for m in range(3):
        grad = flat_grads[:, m]
        ratio = attend_magnitude[m] / column_attend[m]
        mag = jnp.sum(grad.astype(F32) * flat_pre[:, m], axis=0)
        mags.append(mag / attend_magnitude[m])
        pull = attend_magnitude[m] * (mags[m] * column_attend[m]) / column_attend[m] ** 3
        upper_part = exact_dot_left(
            through_three[:, m * rank : (m + 1) * rank], grad, ((0,), (0,))
        )
        local.append(adapter_scale * (upper_part * ratio - inner_attend[m] * pull))
        downs.append(exact_dot(grad, attend_upper[m] * ratio, ((1,), (1,))))
        pulled = attend_upper[m] * pull
        outer = exact_dot_left(pulled, attend_frozen[m], ((1,), (1,)))
        outer = outer + adapter_scale * jnp.dot(
            jnp.dot(pulled, attend_upper[m].T, precision=lax.Precision.HIGHEST),
            attend_lower[m].T,
            precision=lax.Precision.HIGHEST,
        )
        late.append(outer)
    late = exact_dot_left(jnp.concatenate(downs, axis=1), normed_one, ((0,), (0,))) - (
        jnp.concatenate(late, axis=0)
    )
    local = jnp.concatenate(local + [jnp.stack(mags), jnp.zeros((5, HD), F32)], axis=0)
    everywhere, block_x, small_ctx = sums(
        jnp.concatenate(
            [early, inner_both * share, late, jnp.zeros((32, width), F32)], axis=0
        ),
        block_x,
        lower_out,
        local,
    )
    lower_out, local = small_ctx[:rank], small_ctx[rank:]
    late = adapter_scale * everywhere[7 * rank : 10 * rank]
    early = everywhere[: 7 * rank]

    attend_lower_grad = late.reshape(3, rank, width).transpose(0, 2, 1)
    attend_upper_grad = local[: 3 * rank].reshape(3, rank, HD)
    attend_magnitude_grad = local[3 * rank : 3 * rank + 3]
    column_expand = column_expand.reshape(2, ff)
    inner_expand = inner_expand.reshape(2, ff, HD)
    inner_expand = inner_expand[..., : 2 * rank] + inner_expand[..., 2 * rank : 4 * rank]
    expand_magnitude_grad = block_x[3 * rank : 3 * rank + 2] / expand_magnitude
    pull_expand = expand_magnitude * expand_magnitude_grad / column_expand**2
    ratio_expand = expand_magnitude / column_expand
    expand_upper_grad = jnp.stack(
        [
            adapter_scale
            * (
                block_x[m * rank : (m + 1) * rank] * ratio_expand[m]
                - inner_expand[m, :, m * rank : (m + 1) * rank].T * pull_expand[m]
            )
            for m in range(2)
        ]
    )
    expand_lower_grad = adapter_scale * early[: 2 * rank].reshape(2, rank, width).transpose(0, 2, 1)
    columns = jnp.sqrt(squares)
    magnitude_grads = early[4 * rank : 4 * rank + 2] / mago
    pulls = mago * magnitude_grads / squares
    ratios = mago / columns
    output_magnitude_grad = magnitude_grads[0]
    reduce_magnitude_grad = magnitude_grads[1]
    output_upper_grad = adapter_scale * (
        early[2 * rank : 3 * rank] * ratios[0] - early[5 * rank : 6 * rank] * pulls[0]
    )
    reduce_upper_grad = adapter_scale * (
        early[3 * rank : 4 * rank] * ratios[1] - early[6 * rank : 7 * rank] * pulls[1]
    )

    def pulled_rows(frozen, lower, upper, pull):
        pulled = upper * pull
        rows_part = exact_dot(frozen, pulled, ((1,), (1,)))
        return rows_part + adapter_scale * jnp.dot(
            lower,
            jnp.dot(upper, pulled.T, precision=lax.Precision.HIGHEST),
            precision=lax.Precision.HIGHEST,
        )

    output_lower_grad = adapter_scale * (
        lower_out.T - pulled_rows(output_frozen, output_lower, output_upper, pulls[0])
    )
    reduce_lower_grad = adapter_scale * (
        block_x[2 * rank : 3 * rank].T
        - pulled_rows(reduce_frozen, reduce_lower, reduce_upper, pulls[1])
    )
    return (
        block_output,
        hidden_grad,
        attend_lower_grad,
        attend_upper_grad,
        attend_magnitude_grad,
        output_lower_grad,
        output_upper_grad,
        output_magnitude_grad,
        expand_lower_grad,
        expand_upper_grad,
        expand_magnitude_grad,
        reduce_lower_grad,
        reduce_upper_grad,
        reduce_magnitude_grad,
    )


def solution(mesh):
    placed = (
        P(None, "ctx", None),
        P(),
        P(),
        P(),
        P(),
        P(None, None, "tp"),
        P("tp", None),
        P(None, None, "tp"),
        P("tp", None),
        P(),
        P(None, None, "tp"),
        P(None, "tp"),
        P("tp", None),
        P(),
        P(),
        P(),
        P(None, None, "tp"),
        P(None, "tp"),
        P("tp", None),
        P(),
        P(),
        P(None, "ctx", None),
    )
    return jax.shard_map(
        on_device,
        mesh=mesh,
        in_specs=placed,
        out_specs=(
            P(None, "ctx", None),
            P(None, "ctx", None),
            P(),
            P(None, None, "tp"),
            P(None, "tp"),
            P("tp", None),
            P(),
            P(),
            P(),
            P(None, None, "tp"),
            P(None, "tp"),
            P("tp", None),
            P(),
            P(),
        ),
        check_vma=False,
    )
```

```python
import jax
import jax.numpy as jnp
from jax import lax
from jax.experimental import pallas as pl
from jax.experimental.pallas import tpu as pltpu
from jax.sharding import PartitionSpec as P

HD = 128
SEGS = 4
X = 4
Y = 4
Z = 4

epsilon = 1e-05
adapter_scale = 2.0
rotary_base = 10000.0
F32 = jnp.float32
BF16 = jnp.bfloat16


def roll_blocks(a, axis, start):
    n = a.shape[axis]
    return lax.dynamic_slice_in_dim(jnp.concatenate([a, a], axis=axis), start, n, axis)


def halves(a):
    high = lax.reduce_precision(a, 8, 7)
    return high.astype(BF16), (a - high).astype(BF16)


def dot32(a, b, dims):
    return lax.dot_general(a, b, (dims, ((), ())), preferred_element_type=F32)


def exact_dot(bf, full, dims):
    high, low = halves(full)
    return dot32(bf, high, dims) + dot32(bf, low, dims)


def rotate(tensor, cosine, sine_part):
    half_width = tensor.shape[-1] // 2
    turned = jnp.concatenate([-tensor[..., half_width:], tensor[..., :half_width]], axis=-1)
    return tensor * cosine + turned * sine_part


MESH = pl.DeviceIdType.MESH
ANY = pl.BlockSpec(memory_space=pl.ANY)
VM = pl.BlockSpec(memory_space=pltpu.VMEM)
NEAR_LAST = (2, 1, 3)


def place():
    ctx = lax.axis_index("ctx")
    tp = lax.axis_index("tp")
    return ctx // 2, ctx % 2, tp // X, tp % X


def device(dz=0, dc=0, dy=0, dx=0):
    z, core, y, x = place()
    return (((z + dz) % Z) * 2 + (core + dc) % 2, ((y + dy) % Y) * X + (x + dx) % X)


def greet(devices):
    barrier = pltpu.get_barrier_semaphore()
    for d in devices:
        pl.semaphore_signal(barrier, inc=1, device_id=d, device_id_type=MESH)
    pl.semaphore_wait(barrier, len(devices))


def send(src, dst, send_sem, recv_sem, to):
    copy = pltpu.make_async_remote_copy(
        src_ref=src,
        dst_ref=dst,
        send_sem=send_sem,
        recv_sem=recv_sem,
        device_id=to,
        device_id_type=MESH,
    )
    copy.start()
    return copy


def keep(src, dst, sem):
    copy = pltpu.make_async_copy(src, dst, sem)
    copy.start()
    return copy


def dma(*shape):
    return pltpu.SemaphoreType.DMA(shape)


def call(kernel, outs, in_specs, out_specs, scratch, number, flops, moved):
    return pl.pallas_call(
        kernel,
        out_shape=outs,
        in_specs=in_specs,
        out_specs=out_specs,
        scratch_shapes=scratch,
        cost_estimate=pl.CostEstimate(flops=flops, bytes_accessed=moved, transcendentals=0),
        compiler_params=pltpu.CompilerParams(
            collective_id=number, has_side_effects=True, vmem_limit_bytes=58 * 2**20
        ),
    )


def mask_of(begin, spot_q, key_tag, key_spot):
    return ((key_tag >= begin) & (key_tag <= spot_q)) | (key_spot == spot_q)


KB = 512


def tiles(total, size):
    return [(s, min(size, total - s)) for s in range(0, total, size)]


PIECES = 3


def relay_plan(weights, send_a, recv_a, send_b, recv_b, send_s, recv_s, cols):
    def begin(p, own, start, size):
        return [
            send(own, weights(1, start, size), send_a.at[p, 0], recv_a.at[p, 0], device(dx=1)),
            send(own, weights(3, start, size), send_a.at[p, 1], recv_a.at[p, 1], device(dx=3)),
        ]

    def relay(p, copies, start, size):
        half = size // 2
        more = []
        for k, (slot, at, to) in enumerate(((1, start, 1), (3, start + half, 3))):
            copies[k].wait_recv()
            more.append(
                send(
                    weights(slot, at, half), weights(2, at, half),
                    send_b.at[p, k], recv_b.at[p, k], device(dx=to),
                )
            )
            there = weights(slot, start, size)
            more.append(send(there, there, send_s.at[p, k], recv_s.at[p, k], device(dc=1)))
        return more

    def relay_far(p, more, start, size):
        more[0].wait_recv()
        more[2].wait_recv()
        there = weights(2, start, size)
        return send(there, there, send_s.at[p, 2], recv_s.at[p, 2], device(dc=1))

    def finish(copies, more, last):
        more[1].wait_recv()
        more[3].wait_recv()
        last.wait_recv()
        for copy in copies + more + [last]:
            copy.wait_send()

    return begin, relay, relay_far, finish


def front_kernel(
    hid_ref, gain_ref, fa_ref, la_ref, ua_ref, maga_ref, thin_ref, fw_ref, aw_ref, bw_ref,
    mage_ref, mago_ref, el_ref, small_ref, cos_ref, sin_ref, begin_ref, tag_ref,
    mixed_out, soft_out, log_out, kv_out, weights_out, wq_out, q_out, pre_out, thr_out,
    cola_out, cole_out, sq_out, ina_out, ine_out, ino_out, n1_out, small_out,
    kv_all, score, soft, logs, mixed, mixed_x, joined, w_own, wq_all, normed, kv_own, small,
    sq_x, sq_y, sq_one, ja,
    kv_send, kv_recv, sib_send, sib_recv, a_send, a_recv, b_send, b_recv, ws_send, ws_recv,
    m_send, m_recv, sq_send, sq_recv, sm_send, sm_recv, local, n_local,
):
    z, core, y, x = place()
    me = z * 2 + core
    rows, here, width = hid_ref.shape
    length = Z * 2 * here
    count = fw_ref.shape[0]
    ff = (count - HD) // 3
    piece = here // Y
    cols = pl.ds(pl.multiple_of(core * (width // 2), width // 2), width // 2)
    greet(
        [device(dx=d) for d in (1, 2, 3)]
        + [device(dy=d) for d in (1, 2, 3)]
        + [device(dz=d) for d in (1, 2, 3)]
        + [device(dc=1)]
    )

    def join(matrix, start, size, at):
        low = dot32(aw_ref[start : start + size], bw_ref[matrix, :, at], ((1,), (0,)))
        return fw_ref[start : start + size, at].astype(F32) + adapter_scale * low

    for s, size in tiles(width, 512):
        at = slice(s, s + size)
        one = join(0, 0, HD, at)
        two = join(3, HD + 2 * ff, ff, at)
        sq_one[0:1, at] = jnp.sum(one * one, axis=0, keepdims=True)
        sq_one[1:2, at] = jnp.sum(two * two, axis=0, keepdims=True)
    sq_copies = [
        send(sq_one, sq_x.at[d - 1], sq_send.at[0, d - 1], sq_recv.at[0, d - 1], device(dx=d))
        for d in NEAR_LAST
    ]

    def there(slot, start, size):
        return weights_out.at[slot, pl.ds(start, size), cols]

    begin, relay, relay_far, finish = relay_plan(
        there, a_send, a_recv, b_send, b_recv, ws_send, ws_recv, cols
    )
    where = ((HD, ff), (HD + ff, ff), (0, HD))
    sent, more, last = {}, {}, {}
    for m in range(2):
        start = HD + m * ff
        total = jnp.zeros((ff, 1), F32)
        for s, size in tiles(width, 512):
            at = slice(s, s + size)
            value = join(1 + m, start, ff, at)
            joined[:, at] = value
            total = total + jnp.sum(value * value, axis=1, keepdims=True)
        column = jnp.sqrt(total)
        cole_out[m * ff : (m + 1) * ff] = column
        magnitude = mage_ref[m * ff : (m + 1) * ff]
        ratio = magnitude / column
        for s, size in tiles(width, 512):
            at = slice(s, s + size)
            w_own[start : start + ff, at] = (joined[:, at] * ratio).astype(BF16)
        sent[m] = begin(m, w_own.at[pl.ds(start, ff), cols], start, ff)
        inner = dot32(w_own[start : start + ff], el_ref[...], ((1,), (0,)))
        ine_out[m * ff : (m + 1) * ff] = inner / ratio
        source = small_ref[0:ff, m * 16 : (m + 1) * 16]
        small[0:ff, m * 16 : (m + 1) * 16] = (source * ratio).astype(BF16)
        small[0:ff, (3 + m) * 16 : (4 + m) * 16] = (source / (magnitude * column)).astype(BF16)
    small[0:ff, 32:48] = small_ref[0:ff, 32:48].astype(BF16)
    small[0:ff, 80:] = jnp.zeros((ff, HD - 80), BF16)
    small[ff:] = small_ref[ff:].astype(BF16)
    sm_copies = [
        send(small, small_out.at[d], sm_send.at[d - 1], sm_recv.at[d - 1], device(dx=d))
        for d in NEAR_LAST
    ]
    own = [keep(small, small_out.at[0], local.at[0])]
    for copy in sq_copies:
        copy.wait()
    sq_one[...] += sq_x[0] + sq_x[1] + sq_x[2]
    sq_copies = [
        send(sq_one, sq_y.at[d - 1], sq_send.at[1, d - 1], sq_recv.at[1, d - 1], device(dy=d))
        for d in NEAR_LAST
    ]
    for m in range(3):
        total = jnp.zeros((1, HD), F32)
        for s, size in tiles(width, 512):
            at = slice(s, s + size)
            value = fa_ref[m, at].astype(F32) + adapter_scale * dot32(
                la_ref[m, at], ua_ref[m], ((1,), (0,))
            )
            ja[at] = value
            total = total + jnp.sum(value * value, axis=0, keepdims=True)
        column = jnp.sqrt(total)
        cola_out[m : m + 1] = column
        ratio = maga_ref[m : m + 1] / column
        wq_all[:, m * HD : (m + 1) * HD] = (ja[...] * ratio).astype(BF16)
        inner = dot32(la_ref[m], ja[...].astype(BF16), ((0,), (0,)))
        ina_out[m] = inner[0:16] + inner[32:48]
    own.append(keep(wq_all, wq_out, local.at[1]))
    kv_copies, sib_copies, n_copies = [], [], []
    gain = gain_ref[...]
    for r in range(rows):
        inputs = hid_ref[r].astype(F32)
        inverse = lax.rsqrt(jnp.mean(inputs * inputs, axis=1, keepdims=True) + epsilon)
        if r >= 2:
            n_copies[r - 2].wait()
        normed[r % 2] = (inputs * inverse * gain).astype(BF16)
        n_copies.append(keep(normed.at[r % 2], n1_out.at[r], n_local.at[r]))
        pre = dot32(normed[r % 2], wq_all[...], ((1,), (0,)))
        pre_out[r] = pre
        thin = dot32(normed[r % 2], thin_ref[...], ((1,), (0,)))
        thr_out[r] = thin
        cosine, sine = cos_ref[r], sin_ref[r]
        q_out[r] = rotate(pre[:, :HD], cosine, sine).astype(BF16)
        kv_own[r, :, :HD] = rotate(pre[:, HD : 2 * HD], cosine, sine).astype(BF16)
        kv_own[r, :, HD:] = pre[:, 2 * HD :].astype(BF16)
        for d in NEAR_LAST:
            kv_copies.append(
                send(
                    kv_own.at[r], kv_all.at[me, r], kv_send.at[r, d - 1], kv_recv.at[r, d - 1],
                    device(dz=d),
                )
            )
        sib_copies.append(
            send(kv_own.at[r], kv_all.at[me, r], sib_send.at[r, 0], sib_recv.at[r, 0], device(dc=1))
        )
    own.append(keep(kv_own, kv_all.at[me], local.at[2]))
    for copy in sq_copies:
        copy.wait()
    squares = sq_one[...] + (sq_y[0] + sq_y[1] + sq_y[2])
    sq_out[...] = squares
    ratios = mago_ref[...] / jnp.sqrt(squares)
    for s, size in tiles(width, 512):
        at = slice(s, s + size)
        one = join(0, 0, HD, at)
        two = join(3, HD + 2 * ff, ff, at)
        w_own[0:HD, at] = (one * ratios[0:1, at]).astype(BF16)
        w_own[HD + 2 * ff :, at] = (two * ratios[1:2, at]).astype(BF16)
        ino_out[0:16, at] = dot32(small[ff:], one.astype(BF16), ((0,), (0,)))[0:16]
        ino_out[16:32, at] = dot32(small[0:ff], two.astype(BF16), ((0,), (0,)))[32:48]
    sent[2] = begin(2, w_own.at[pl.ds(0, HD), cols], 0, HD)
    own.append(keep(w_own, weights_out.at[0], local.at[3]))
    more[0] = relay(0, sent[0], *where[0])

    def pass_kv(r):
        for k, d in enumerate(NEAR_LAST):
            kv_copies[3 * r + k].wait_recv()
            slot = ((z + Z - d) % Z) * 2 + core
            at = kv_all.at[slot, r]
            sib_copies.append(send(at, at, sib_send.at[r, d], sib_recv.at[r, d], device(dc=1)))

    for r in range(rows):
        pass_kv(r)
    more[1] = relay(1, sent[1], *where[1])
    own[2].wait()
    for copy in sib_copies:
        copy.wait_recv()
    own.append(keep(kv_all, kv_out, local.at[4]))
    spot_q = lax.broadcasted_iota(jnp.int32, (here, 1), 0) + me * here
    m_copies = []
    for i in (2, 1, 3, 0):
        row = (x + i) % X
        query = q_out[row]
        first = begin_ref[row]
        peak = jnp.full((here, 1), -1e30, F32)
        for b in range(length // KB):
            keys = jnp.concatenate(
                [kv_all[b * (KB // here) + k, row, :, :HD] for k in range(KB // here)], axis=0
            )
            raw = dot32(query, keys, ((1,), (1,))) * (HD**-0.5)
            key_spot = lax.broadcasted_iota(jnp.int32, (1, KB), 1) + b * KB
            ok = mask_of(first, spot_q, tag_ref[row, :, b * KB : (b + 1) * KB], key_spot)
            raw = jnp.where(ok, raw, -1e30)
            score[:, b * KB : (b + 1) * KB] = raw
            peak = jnp.maximum(peak, jnp.max(raw, axis=1, keepdims=True))
        total = jnp.zeros((here, 1), F32)
        gathered = jnp.zeros((here, HD), F32)
        for b in range(length // KB):
            power = jnp.exp(score[:, b * KB : (b + 1) * KB] - peak)
            total = total + jnp.sum(power, axis=1, keepdims=True)
            values = jnp.concatenate(
                [kv_all[b * (KB // here) + k, row, :, HD:] for k in range(KB // here)], axis=0
            )
            gathered = gathered + dot32(power.astype(BF16), values, ((1,), (0,)))
        soft[row] = gathered / total
        logs[row] = peak + jnp.log(total)
        for j in range(Y):
            mixed[i, j * piece : (j + 1) * piece] = soft[
                row, pl.ds(pl.multiple_of(((y + j) % Y) * piece, piece), piece)
            ].astype(BF16)
        if i:
            m_copies.append(
                send(mixed.at[i], mixed_x.at[i], m_send.at[i - 1], m_recv.at[i - 1], device(dx=i))
            )
        else:
            mixed_x[0] = mixed[0]
        if i == 2:
            more[2] = relay(2, sent[2], *where[2])
        if i == 3:
            last[0] = relay_far(0, more[0], *where[0])
    own.append(keep(soft, soft_out, local.at[5]))
    own.append(keep(logs, log_out, local.at[6]))
    last[1] = relay_far(1, more[1], *where[1])
    last[2] = relay_far(2, more[2], *where[2])
    for copy in m_copies:
        copy.wait()
    own.append(keep(mixed_x, mixed_out, local.at[7]))
    for copy in kv_copies + sib_copies:
        copy.wait_send()
    for copy in sm_copies:
        copy.wait()
    for p in range(PIECES):
        finish(sent[p], more[p], last[p])
    for copy in n_copies[rows - 2 :]:
        copy.wait()
    own.pop(2)
    for copy in own:
        copy.wait()


def front(
    hidden, gain, fa, la, ua, maga, thin, fw, aw, bw, mage, mago, el, small, cos, sin, begin, tag
):
    rows, here, width = hidden.shape
    count = fw.shape[0]
    ff = (count - HD) // 3
    length = 2 * Z * here
    s = jax.ShapeDtypeStruct
    return call(
        front_kernel,
        (
            s((X, here, HD), BF16),
            s((rows, here, HD), F32),
            s((rows, here, 1), F32),
            s((2 * Z, rows, here, 2 * HD), BF16),
            s((X, count, width), BF16),
            s((width, 3 * HD), BF16),
            s((rows, here, HD), BF16),
            s((rows, here, 3 * HD), F32),
            s((rows, here, HD), F32),
            s((3, HD), F32),
            s((2 * ff, 1), F32),
            s((2, width), F32),
            s((3, 16, HD), F32),
            s((2 * ff, HD), F32),
            s((32, width), F32),
            s((rows, here, width), BF16),
            s((X, ff + HD, HD), BF16),
        ),
        [VM] * 18,
        (ANY,) * 6 + (VM,) * 9 + (ANY, ANY),
        [
            pltpu.VMEM((2 * Z, rows, here, 2 * HD), BF16),
            pltpu.VMEM((here, length), F32),
            pltpu.VMEM((rows, here, HD), F32),
            pltpu.VMEM((rows, here, 1), F32),
            pltpu.VMEM((X, here, HD), BF16),
            pltpu.VMEM((X, here, HD), BF16),
            pltpu.VMEM((ff, width), F32),
            pltpu.VMEM((count, width), BF16),
            pltpu.VMEM((width, 3 * HD), BF16),
            pltpu.VMEM((2, here, width), BF16),
            pltpu.VMEM((rows, here, 2 * HD), BF16),
            pltpu.VMEM((ff + HD, HD), BF16),
            pltpu.VMEM((3, 2, width), F32),
            pltpu.VMEM((3, 2, width), F32),
            pltpu.VMEM((2, width), F32),
            pltpu.VMEM((width, HD), F32),
            dma(rows, 3), dma(rows, 3), dma(rows, 4), dma(rows, 4),
            dma(PIECES, 2), dma(PIECES, 2), dma(PIECES, 2), dma(PIECES, 2),
            dma(PIECES, 3), dma(PIECES, 3),
            dma(3), dma(3), dma(2, 3), dma(2, 3), dma(3), dma(3), dma(8), dma(rows),
        ],
        0,
        2 * 2 * rows * here * length * HD + 2 * rows * here * width * 4 * HD,
        32 * 2**20,
    )(hidden, gain, fa, la, ua, maga, thin, fw, aw, bw, mage, mago, el, small, cos, sin, begin, tag)


def feed_kernel(
    mixed_ref, hid_ref, gain_ref, cot_ref, weights_ref, small_ref, el_ref, upper_ref, mago_ref,
    sq_ref,
    resid_grad_out, block_out, dmix_out, early_out, columns_out, lower_out,
    out_w, gate_w, up_w, down_w, normed, low, act, dgate, dup, sends, recvs, acc, resid_s, mags,
    load, s_send, s_recv, a_send, a_recv, b_send, b_recv, ws_send, ws_recv,
):
    z, core, y, x = place()
    width = hid_ref.shape[1]
    piece = hid_ref.shape[0]
    here = cot_ref.shape[0]
    ff = gate_w.shape[0] // X
    cols = pl.ds(pl.multiple_of(core * (width // 2), width // 2), width // 2)
    down_rows = pl.ds(HD + 2 * ff, ff)
    loads = [[], [], [], []]
    for w, (dst, start, size) in enumerate(((out_w, 0, HD), (gate_w, HD, ff), (up_w, HD + ff, ff))):
        for i in range(X):
            loads[w].append(
                keep(
                    weights_ref.at[i, pl.ds(start, size)], dst.at[pl.ds(i * size, size)],
                    load.at[w, i],
                )
            )
    loads[3].append(keep(weights_ref.at[0, down_rows], down_w.at[pl.ds(0, ff)], load.at[3, 0]))
    greet(
        [device(dy=d) for d in (1, 2, 3)] + [device(dx=1), device(dx=3), device(dc=1)]
    )

    def there(slot, start, size):
        return down_w.at[pl.ds(slot * ff + start, size), cols]

    begin, relay, relay_far, finish = relay_plan(
        there, a_send, a_recv, b_send, b_recv, ws_send, ws_recv, cols
    )
    sent = begin(0, weights_ref.at[0, down_rows, cols], 0, ff)

    def loaded(w):
        for copy in loads[w]:
            copy.wait()

    def start_scatter(k):
        return [
            send(
                sends.at[k, d - 1], recvs.at[k, d - 1], s_send.at[k, d - 1], s_recv.at[k, d - 1],
                device(dy=d),
            )
            for d in NEAR_LAST
        ]

    def put(k, part, start, size):
        acc[k, :, start : start + size] = part[:piece]
        for d in range(1, Y):
            sends[k, d - 1, :, start : start + size] = part[d * piece : (d + 1) * piece].astype(BF16)

    def summed(k, copies):
        for copy in copies:
            copy.wait()
        return acc[k] + (
            recvs[k, 0].astype(F32) + recvs[k, 1].astype(F32) + recvs[k, 2].astype(F32)
        )

    def start_gather(buffer, k):
        return [
            send(
                buffer.at[pl.ds(0, piece)], buffer.at[pl.ds((Y - d) * piece, piece)],
                s_send.at[k, d - 1], s_recv.at[k, d - 1], device(dy=d),
            )
            for d in NEAR_LAST
        ]

    loaded(0)
    mixed_cat = jnp.concatenate([mixed_ref[i] for i in range(X)], axis=1)
    for start, size in tiles(width, 512):
        put(0, dot32(mixed_cat, out_w[:, start : start + size], ((1,), (0,))), start, size)
    copies = start_scatter(0)
    ratios = mago_ref[...] / jnp.sqrt(sq_ref[...])
    upper_o = (upper_ref[0:16] * ratios[0:1]).astype(BF16)
    upper_d = (upper_ref[16:32] * ratios[1:2]).astype(BF16)
    through_down = dot32(cot_ref[...], upper_d, ((1,), (1,))).astype(BF16)
    small = jnp.concatenate([small_ref[i, 0:ff] for i in range(X)], axis=0)
    small_o = jnp.concatenate([small_ref[i, ff:] for i in range(X)], axis=0)
    from_mixed = dot32(mixed_cat, small_o, ((1,), (0,)))[:, 0:16].astype(BF16)
    attended = summed(0, copies)
    acc[0] = attended
    gain = gain_ref[...]
    resid = hid_ref[...].astype(F32) + attended
    inverse = lax.rsqrt(jnp.mean(resid * resid, axis=1, keepdims=True) + epsilon)
    resid_s[...] = resid
    normed[0:piece] = (resid * inverse * gain).astype(BF16)
    copies = start_gather(normed, 3)
    more = relay(0, sent, 0, ff)
    loaded(1)
    loaded(2)
    loaded(3)
    for copy in copies:
        copy.wait()
    far = relay_far(0, more, 0, ff)
    finish(sent, more, far)
    for start, size in tiles(X * ff, 256):
        at = slice(start, start + size)
        gate = dot32(normed[...], gate_w[at], ((1,), (1,)))
        up = dot32(normed[...], up_w[at], ((1,), (1,)))
        d_act = dot32(cot_ref[...], down_w[at], ((1,), (1,)))
        sig = 1.0 / (1.0 + jnp.exp(-gate))
        gated = gate * sig
        act[:, at] = (gated * up).astype(BF16)
        d_gate = (d_act * up * sig * (1.0 + gate * (1.0 - sig))).astype(BF16)
        d_up = (d_act * gated).astype(BF16)
        dgate[:, at] = d_gate
        dup[:, at] = d_up
        mags[0:1, at] = jnp.sum(d_gate.astype(F32) * gate, axis=0, keepdims=True)
        mags[1:2, at] = jnp.sum(d_up.astype(F32) * up, axis=0, keepdims=True)
    for start, size in tiles(width, 512):
        at = slice(start, start + size)
        part = dot32(dgate[...], gate_w[:, at], ((1,), (0,)))
        part = part + dot32(dup[...], up_w[:, at], ((1,), (0,)))
        put(1, part, start, size)
    two_copies = start_scatter(1)
    for start, size in tiles(width, 512):
        at = slice(start, start + size)
        put(2, dot32(act[...], down_w[:, at], ((1,), (0,))), start, size)
    ff_copies = start_scatter(2)
    through = dot32(normed[...], el_ref[...], ((1,), (0,)))
    through = (through[:, 0:32] + through[:, 32:64]).astype(BF16)
    gate_down = dot32(dgate[...], small, ((1,), (0,)))[:, 0:16].astype(BF16)
    up_down = dot32(dup[...], small, ((1,), (0,)))[:, 16:32].astype(BF16)
    from_act = dot32(act[...], small, ((1,), (0,)))[:, 32:48].astype(BF16)
    small_t = jnp.transpose(small.astype(F32))
    pull_gate = (small_t[48:64] * mags[0:1]).astype(BF16)
    pull_up = (small_t[64:80] * mags[1:2]).astype(BF16)

    def columns(row, value):
        for i in range(X):
            columns_out[i, row : row + value.shape[0]] = value[:, i * ff : (i + 1) * ff]

    columns(0, dot32(through[:, 0:16], dgate[...], ((0,), (0,))))
    columns(16, dot32(through[:, 16:32], dup[...], ((0,), (0,))))
    columns(32, dot32(through_down, act[...], ((0,), (0,))))
    columns(48, jnp.concatenate([mags[...], jnp.zeros((6, X * ff), F32)], axis=0))
    early_out[0:16] = dot32(gate_down, normed[...], ((0,), (0,))) - dot32(
        pull_gate, gate_w[...], ((1,), (0,))
    )
    early_out[16:32] = dot32(up_down, normed[...], ((0,), (0,))) - dot32(
        pull_up, up_w[...], ((1,), (0,))
    )
    early_out[48:64] = dot32(from_act, cot_ref[...], ((0,), (0,)))
    d_two = summed(1, two_copies)
    resid = resid_s[...]
    inverse = lax.rsqrt(jnp.mean(resid * resid, axis=1, keepdims=True) + epsilon)
    scaled = d_two * gain
    cot_own = cot_ref[0:piece].astype(F32)
    d_resid = cot_own + (
        inverse * scaled
        - resid * (inverse * inverse * inverse) * jnp.mean(resid * scaled, axis=1, keepdims=True)
    )
    resid_grad_out[...] = d_resid
    own_low = d_resid.astype(BF16)
    low[0:piece] = own_low
    copies = start_gather(low, 4)
    mag_out = jnp.sum(own_low.astype(F32) * acc[0], axis=0, keepdims=True)
    feedforward = summed(2, ff_copies)
    block_out[...] = (resid_s[...] + feedforward).astype(BF16)
    mag_down = jnp.sum(cot_own * feedforward, axis=0, keepdims=True)
    early_out[64:80] = jnp.concatenate(
        [mag_out, mag_down, jnp.zeros((14, width), F32)], axis=0
    )
    for copy in copies:
        copy.wait()
    d_mixed = dot32(low[...], out_w[...], ((1,), (1,))).astype(BF16)
    for i in range(X):
        dmix_out[i] = d_mixed[:, i * HD : (i + 1) * HD]
    through_out = dot32(low[...], upper_o, ((1,), (1,))).astype(BF16)
    value = dot32(through_out, mixed_cat, ((0,), (0,)))
    for i in range(X):
        lower_out[i] = value[:, i * HD : (i + 1) * HD]
    early_out[32:48] = dot32(from_mixed, low[...], ((0,), (0,)))


def feed(mixed_x, hid_own, gain, cot_row, weights, small_x, el, upper, mago, squares):
    here, width = cot_row.shape
    piece = here // Y
    hidden = (weights.shape[1] - HD) // 3 * X
    s = jax.ShapeDtypeStruct
    return call(
        feed_kernel,
        (
            s((piece, width), F32),
            s((piece, width), BF16),
            s((X, here, HD), BF16),
            s((80, width), F32),
            s((X, 56, hidden // X), F32),
            s((X, 16, HD), F32),
        ),
        [VM, VM, VM, VM, ANY, VM, VM, VM, VM, VM],
        (VM,) * 6,
        [
            pltpu.VMEM((X * HD, width), BF16),
            pltpu.VMEM((hidden, width), BF16),
            pltpu.VMEM((hidden, width), BF16),
            pltpu.VMEM((hidden, width), BF16),
            pltpu.VMEM((here, width), BF16),
            pltpu.VMEM((here, width), BF16),
            pltpu.VMEM((here, hidden), BF16),
            pltpu.VMEM((here, hidden), BF16),
            pltpu.VMEM((here, hidden), BF16),
            pltpu.VMEM((3, Y - 1, piece, width), BF16),
            pltpu.VMEM((3, Y - 1, piece, width), BF16),
            pltpu.VMEM((3, piece, width), F32),
            pltpu.VMEM((piece, width), F32),
            pltpu.VMEM((2, hidden), F32),
            dma(4, X), dma(5, 3), dma(5, 3), dma(1, 2), dma(1, 2), dma(1, 2), dma(1, 2),
            dma(1, 3), dma(1, 3),
        ],
        1,
        2 * here * hidden * width * 6,
        32 * 2**20,
    )(mixed_x, hid_own, gain, cot_row, weights, small_x, el, upper, mago, squares)


def attend_back_kernel(
    q_ref, kv_ref, dmix_ref, soft_ref, log_ref, begin_ref, tag_ref, cos_ref, sin_ref, block_ref,
    grads_out, block_out,
    kv_all, dmix_all, dmix_abs, part, own, sib_s, sib_r, z_own, z_s, z_r, dq_s,
    d_send, d_recv, b_send, b_recv, sib_send, sib_recv, z_send, z_recv, local,
):
    z, core, y, x = place()
    me = z * 2 + core
    rows, here = q_ref.shape[0], q_ref.shape[1]
    piece, width = block_ref.shape
    half = width // 2
    load = keep(kv_ref, kv_all, local.at[0])
    greet(
        [device(dx=d) for d in (1, 2, 3)]
        + [device(dy=d) for d in (1, 2, 3)]
        + [device(dz=d) for d in (1, 2, 3)]
        + [device(dc=1)]
    )
    d_copies = [
        send(
            dmix_ref.at[X - d], dmix_all.at[x], d_send.at[d - 1], d_recv.at[d - 1], device(dx=d)
        )
        for d in NEAR_LAST
    ]
    own_mix = keep(dmix_ref.at[0], dmix_all.at[x], local.at[1])
    tokens = pl.ds(pl.multiple_of(y * piece, piece), piece)
    left, right = pl.ds(0, half), pl.ds(half, half)
    own_block = keep(block_ref, block_out.at[x, tokens], local.at[2])
    block_one = []
    for d in NEAR_LAST:
        block_one.append(
            send(
                block_ref.at[:, left], block_out.at[x, tokens, left],
                b_send.at[0, d - 1], b_recv.at[0, d - 1], device(dx=d),
            )
        )
        block_one.append(
            send(
                block_ref.at[:, right], block_out.at[x, tokens, right],
                b_send.at[1, d - 1], b_recv.at[1, d - 1], device(dy=d),
            )
        )
    load.wait()
    own_mix.wait()
    for copy in d_copies:
        copy.wait()
    spot_q = lax.broadcasted_iota(jnp.int32, (here, 1), 0) + me * here
    sib_copies, z_copies, block_two = [], [], []

    def pass_on(r):
        sib_copies[r].wait()
        z_own[r] = own[r, z] + sib_r[r, z].astype(F32)
        for d in NEAR_LAST:
            to = (z + d) % Z
            z_s[r, d - 1] = (own[r, to] + sib_r[r, to].astype(F32)).astype(BF16)
            z_copies.append(
                send(
                    z_s.at[r, d - 1], z_r.at[r, d - 1], z_send.at[r, d - 1], z_recv.at[r, d - 1],
                    device(dz=d),
                )
            )

    def back(a, r):
        cosine, sine = cos_ref[r], sin_ref[r]
        weighted = a * sine
        turned = jnp.concatenate([weighted[:, HD // 2 :], -weighted[:, : HD // 2]], axis=1)
        return a * cosine + turned

    for r in range(rows):
        for j in range(Y):
            dmix_abs[pl.ds(pl.multiple_of(((y + j) % Y) * piece, piece), piece)] = dmix_all[
                r, j * piece : (j + 1) * piece
            ]
        query = q_ref[r]
        grad = dmix_abs[...]
        delta = jnp.sum(grad.astype(F32) * soft_ref[r], axis=1, keepdims=True)
        begin = begin_ref[r]
        log = log_ref[r]
        d_query = jnp.zeros((here, HD), F32)
        for b in range(Z):
            keys = jnp.concatenate([kv_all[2 * b + k, r, :, :HD] for k in range(2)], axis=0)
            values = jnp.concatenate([kv_all[2 * b + k, r, :, HD:] for k in range(2)], axis=0)
            raw = dot32(query, keys, ((1,), (1,))) * (HD**-0.5)
            key_spot = lax.broadcasted_iota(jnp.int32, (1, KB), 1) + b * KB
            ok = mask_of(begin, spot_q, tag_ref[r, :, b * KB : (b + 1) * KB], key_spot)
            probs = jnp.exp(jnp.where(ok, raw, -1e30) - log)
            d_probs = dot32(grad, values, ((1,), (1,)))
            d_scores = (probs * (d_probs - delta)).astype(BF16)
            d_query = d_query + dot32(d_scores, keys, ((1,), (0,)))
            d_keys = dot32(d_scores, query, ((0,), (0,))) * (HD**-0.5)
            d_values = dot32(probs.astype(BF16), grad, ((0,), (0,)))
            for k in range(2):
                part[b, k, :, :HD] = d_keys[k * here : (k + 1) * here]
                part[b, k, :, HD:] = d_values[k * here : (k + 1) * here]
        dq_s[r] = d_query * (HD**-0.5)
        for b in range(Z):
            sib_s[r, b] = part[b, 1 - core].astype(BF16)
            own[r, b] = part[b, core]
        sib_copies.append(
            send(sib_s.at[r], sib_r.at[r], sib_send.at[r], sib_recv.at[r], device(dc=1))
        )
        grads_out[r, :, :HD] = back(dq_s[r], r).astype(BF16)
        if r:
            pass_on(r - 1)
        if r == 1:
            own_block.wait()
            for copy in block_one:
                copy.wait()
            for d in NEAR_LAST:
                spread = block_out.at[:, tokens, left]
                block_two.append(
                    send(
                        spread, spread, b_send.at[2, d - 1], b_recv.at[2, d - 1], device(dy=d)
                    )
                )
                spread = block_out.at[x, :, right]
                block_two.append(
                    send(
                        spread, spread, b_send.at[3, d - 1], b_recv.at[3, d - 1], device(dx=d)
                    )
                )
    pass_on(rows - 1)
    for r in range(rows):
        for copy in z_copies[3 * r : 3 * r + 3]:
            copy.wait()
        total = z_own[r] + (
            z_r[r, 0].astype(F32) + z_r[r, 1].astype(F32) + z_r[r, 2].astype(F32)
        )
        grads_out[r, :, HD : 2 * HD] = back(total[:, :HD], r).astype(BF16)
        grads_out[r, :, 2 * HD :] = total[:, HD:].astype(BF16)
    for copy in block_two:
        copy.wait()


def attend_back(queries, kv, dmix, soft, log, begin, tag, cosine, sine, block):
    rows, here, _ = queries.shape
    piece, width = block.shape
    return call(
        attend_back_kernel,
        (
            jax.ShapeDtypeStruct((rows, here, 3 * HD), BF16),
            jax.ShapeDtypeStruct((rows, here, width), BF16),
        ),
        [VM, ANY, VM, VM, VM, VM, VM, VM, VM, VM],
        (VM, ANY),
        [
            pltpu.VMEM((2 * Z, rows, here, 2 * HD), BF16),
            pltpu.VMEM((rows, here, HD), BF16),
            pltpu.VMEM((here, HD), BF16),
            pltpu.VMEM((Z, 2, here, 2 * HD), F32),
            pltpu.VMEM((rows, Z, here, 2 * HD), F32),
            pltpu.VMEM((rows, Z, here, 2 * HD), BF16),
            pltpu.VMEM((rows, Z, here, 2 * HD), BF16),
            pltpu.VMEM((rows, here, 2 * HD), F32),
            pltpu.VMEM((rows, Z - 1, here, 2 * HD), BF16),
            pltpu.VMEM((rows, Z - 1, here, 2 * HD), BF16),
            pltpu.VMEM((rows, here, HD), F32),
            dma(3), dma(3), dma(4, 3), dma(4, 3), dma(rows), dma(rows), dma(rows, 3), dma(rows, 3),
            dma(3),
        ],
        2,
        2 * 5 * rows * here * 2 * Z * here * HD,
        32 * 2**20,
    )(queries, kv, dmix, soft, log, begin, tag, cosine, sine, block)


def tail_kernel(
    grads_ref, weight_ref, hid_ref, gain_ref, dres_ref, pre_ref, thr_ref, n1_ref, inner_ref,
    cola_ref, maga_ref, uppera_ref, early_ref, both_ref, block_ref, lower_ref,
    grad_out, all_out, block_out, ctx_out,
    rel, two, near, held, hop, came, acc, send_2, recv_2, d_one, spread, n1, down, all_s,
    c_r, z_s, z_r, x_s, x_r, y_s, y_r, bx_r, lx_r, b_one, b_two, e_one, e_two, e_z, b_z,
    s_one, r_one, s_two, r_two, s_gat, r_gat, ss, rs, local,
):
    z, core, y, x = place()
    rows, here, deep = grads_ref.shape
    piece, width = hid_ref.shape
    half = width // 2
    mid = here // 2
    n = all_s.shape[0]
    nc, nz = n // 2, n // 2 // Z
    wx, wy = width // X, width // X // Y
    rank = 16
    load = keep(n1_ref, n1, local.at[0])
    for i in range(X):
        for j in range(Y):
            rel[i, j] = grads_ref[
                (x + i) % X, pl.ds(pl.multiple_of(((y + j) % Y) * piece, piece), piece)
            ]
    greet(
        [device(dx=d) for d in (1, 2, 3)]
        + [device(dy=d) for d in (1, 2, 3)]
        + [device(dz=d) for d in (1, 2, 3)]
        + [device(dc=1)]
    )

    def to(k, d):
        return device(dy=d) if k else device(dx=d)

    def ds(index, size):
        return pl.ds(pl.multiple_of(index * size, size), size)

    def done(copies):
        for copy in copies:
            copy.wait()

    def term(k, d, begin, size):
        if k:
            lhs = jnp.concatenate([rel[i, d] for i in range(X)], axis=0)
        else:
            lhs = rel[d].reshape(here, deep)
        return dot32(lhs, weight_ref[k * half + begin : k * half + begin + size], ((1,), (1,)))

    one = {}
    for k in range(2):
        for start, size in tiles(half, 512):
            two[k, :, start : start + size] = term(k, 2, start, size).astype(BF16)
        one[k, 0] = send(
            two.at[k, pl.ds(0, mid)], hop.at[k, 0], s_one.at[k, 0], r_one.at[k, 0], to(k, 1)
        )
        one[k, 1] = send(
            two.at[k, pl.ds(mid, mid)], hop.at[k, 1], s_one.at[k, 1], r_one.at[k, 1], to(k, 3)
        )
    for k in range(2):
        for side, d in enumerate((1, 3)):
            plain = mid if side == 0 else 0
            other = mid - plain
            for start, size in tiles(half, 512):
                at = slice(start, start + size)
                part = term(k, d, start, size)
                near[k, side, plain : plain + mid, at] = part[plain : plain + mid].astype(BF16)
                held[k, side, :, at] = part[other : other + mid]
            one[k, 2 + side] = send(
                near.at[k, side, pl.ds(plain, mid)], came.at[k, side, pl.ds(plain, mid)],
                s_one.at[k, 2 + side], r_one.at[k, 2 + side], to(k, d),
            )
    for k in range(2):
        for start, size in tiles(half, 512):
            acc[k, :, start : start + size] = term(k, 0, start, size)

    for m in range(3):
        at = slice(m * HD, (m + 1) * HD)
        grad = grads_ref[:, :, at].reshape(rows * here, HD)
        before = pre_ref[:, :, at].reshape(rows * here, HD)
        column, magnitude = cola_ref[m : m + 1], maga_ref[m : m + 1]
        ratio = magnitude / column
        mag = jnp.sum(grad.astype(F32) * before, axis=0, keepdims=True) / magnitude
        pull = magnitude * mag / (column * column)
        thin = thr_ref[:, :, m * rank : (m + 1) * rank] + thr_ref[
            :, :, (3 + m) * rank : (4 + m) * rank
        ]
        thin = thin.reshape(rows * here, rank).astype(BF16)
        part = dot32(thin, grad, ((0,), (0,)))
        e_one[(1 + m) * rank : (2 + m) * rank] = adapter_scale * (
            part * ratio - inner_ref[m] * pull
        )
        e_one[4 * rank + m : 4 * rank + m + 1] = mag
        upper = uppera_ref[m]
        down[:, m * rank : (m + 1) * rank] = dot32(
            grad, (upper * ratio).astype(BF16), ((1,), (1,))
        ).astype(BF16)
        pulled = (upper * (mag / column)).astype(BF16)
        for start, size in tiles(width, 512):
            all_s[(7 + m) * rank : (8 + m) * rank, start : start + size] = dot32(
                pulled, weight_ref[start : start + size, at], ((1,), (1,))
            )
    e_one[4 * rank + 3 :] = jnp.zeros((e_one.shape[0] - 4 * rank - 3, HD), F32)
    load.wait()
    for start, size in tiles(width, 512):
        at = slice(start, start + size)
        value = dot32(
            down[...], n1[:, :, at].reshape(rows * here, size), ((0,), (0,))
        )
        all_s[7 * rank : 10 * rank, at] = value - all_s[7 * rank : 10 * rank, at]
    all_s[0 : 5 * rank] = early_ref[...]
    all_s[5 * rank : 7 * rank] = both_ref[...] * (1.0 / (2 * Z))
    all_s[10 * rank :] = jnp.zeros((n - 10 * rank, width), F32)

    def go(k, d, src, dst, where):
        return send(src, dst, ss.at[k, d], rs.at[k, d], where)

    first = [go(0, 0, all_s.at[ds(1 - core, nc)], c_r, device(dc=1))]
    slots = []
    for d in NEAR_LAST:
        slots.append(go(1, d, block_ref.at[X - d], bx_r.at[d - 1], device(dx=d)))
        slots.append(go(2, d, lower_ref.at[X - d], lx_r.at[d - 1], device(dx=d)))
    for k in range(2):
        for side, d in enumerate((1, 3)):
            one[k, side].wait_recv()
            other = 0 if side == 0 else mid
            near[k, side, other : other + mid] = (
                held[k, side] + hop[k, side].astype(F32)
            ).astype(BF16)
            one[k, 4 + side] = send(
                near.at[k, side, pl.ds(other, mid)], came.at[k, side, pl.ds(other, mid)],
                s_one.at[k, 4 + side], r_one.at[k, 4 + side], to(k, d),
            )
    done(first)
    z_s[...] = all_s[ds(core, nc)] + c_r[...]
    zc = [go(3, d, z_s.at[ds((z + d) % Z, nz)], z_r.at[d - 1], device(dz=d)) for d in NEAR_LAST]
    done(slots)
    b_one[...] = block_ref[0] + (bx_r[0] + bx_r[1] + bx_r[2])
    e_one[:rank] = lower_ref[0] + (lx_r[0] + lx_r[1] + lx_r[2])
    cc = [go(4, 0, b_one, b_two, device(dc=1)), go(5, 0, e_one, e_two, device(dc=1))]
    for index in range(2):
        for k in range(2):
            one[k, index].wait_send()
    for k in range(2):
        for index in (2, 3, 4, 5):
            one[k, index].wait()
    seconds = []
    for k in range(2):
        for d in (2, 1, 3, 0):
            at = slice(d * piece, (d + 1) * piece)
            part = acc[k, at] + (came[k, 0, at].astype(F32) + came[k, 1, at].astype(F32))
            if d:
                send_2[k, d - 1] = part.astype(BF16)
                seconds.append(
                    send(
                        send_2.at[k, d - 1], recv_2.at[k, d - 1], s_two.at[k, d - 1],
                        r_two.at[k, d - 1], to(1 - k, d),
                    )
                )
            else:
                d_one[:, k * half : (k + 1) * half] = part
    done(cc)
    b_two[...] += b_one[...]
    e_two[...] += e_one[...]
    done(zc)
    x_s[...] = z_s[ds(z, nz)] + (z_r[0] + z_r[1] + z_r[2])
    cz = []
    for d in NEAR_LAST:
        cz.append(go(6, d, b_two, b_z.at[d - 1], device(dz=d)))
        cz.append(go(7, d, e_two, e_z.at[d - 1], device(dz=d)))
    xc = [go(8, d, x_s.at[:, ds((x + d) % X, wx)], x_r.at[d - 1], device(dx=d)) for d in NEAR_LAST]
    done(seconds)
    for k in range(2):
        d_one[:, k * half : (k + 1) * half] += (
            recv_2[k, 0].astype(F32) + recv_2[k, 1].astype(F32) + recv_2[k, 2].astype(F32)
        )
    inputs = hid_ref[...].astype(F32)
    inverse = lax.rsqrt(jnp.mean(inputs * inputs, axis=1, keepdims=True) + epsilon)
    scaled = d_one[...] * gain_ref[...]
    result = dres_ref[...] + (
        inverse * scaled
        - inputs * (inverse * inverse * inverse) * jnp.mean(inputs * scaled, axis=1, keepdims=True)
    )
    tokens = ds(y, piece)
    left, right = pl.ds(0, half), pl.ds(half, half)
    spread[x, tokens] = result.astype(BF16)
    gat = []
    for d in NEAR_LAST:
        for k, cut in enumerate((left, right)):
            at = spread.at[x, tokens, cut]
            gat.append(send(at, at, s_gat.at[k, d - 1], r_gat.at[k, d - 1], to(k, d)))
    done(xc)
    y_s[...] = x_s[:, ds(x, wx)] + (x_r[0] + x_r[1] + x_r[2])
    yc = [go(9, d, y_s.at[:, ds((y + d) % Y, wy)], y_r.at[d - 1], device(dy=d)) for d in NEAR_LAST]
    done(gat)

    def block_of(k, d):
        if k:
            return spread.at[(x + d) % X, :, right]
        return spread.at[:, ds((y + d) % Y, piece), left]

    def part_of(k, d, second):
        if k:
            return spread.at[(x + d) % X, pl.ds(second * mid, mid), right]
        return spread.at[pl.ds(second * 2, 2), ds((y + d) % Y, piece), left]

    last = {}
    for k in range(2):
        for side, d in enumerate((1, 3)):
            last[k, side] = send(
                block_of(k, 0), block_of(k, 0), s_gat.at[2 + k, side], r_gat.at[2 + k, side],
                to(1 - k, d),
            )
    mine = ds(core * Z + z, nz)
    done(yc)
    all_out[mine, ds(x * Y + y, wy)] = y_s[:, ds(y, wy)] + (y_r[0] + y_r[1] + y_r[2])
    spot = all_out.at[mine, ds(x * Y + y, wy)]
    done([go(10, d, spot, spot, device(dy=d)) for d in NEAR_LAST])
    spot = all_out.at[mine, ds(x, wx)]
    sx = [go(11, d, spot, spot, device(dx=d)) for d in NEAR_LAST]
    for k in range(2):
        for side, d in enumerate((1, 3)):
            last[k, side].wait_recv()
            at = part_of(k, -d % 4, side)
            last[k, 2 + side] = send(
                at, at, s_gat.at[4 + k, side], r_gat.at[4 + k, side], to(1 - k, d)
            )
    done(sx)
    spot = all_out.at[mine]
    done([go(12, d, spot, spot, device(dz=d)) for d in NEAR_LAST])
    spot = all_out.at[ds(core, nc)]
    sc = [go(13, 0, spot, spot, device(dc=1))]
    done(cz)
    block_out[...] = b_two[...] + (b_z[0] + b_z[1] + b_z[2])
    ctx_out[...] = e_two[...] + (e_z[0] + e_z[1] + e_z[2])
    for k in range(2):
        for side in range(2):
            last[k, side].wait_send()
            last[k, 2 + side].wait()
    out = keep(spread, grad_out, local.at[1])
    done(sc)
    out.wait()


def tail(
    grads, weight, hid_own, gain, d_resid, pre, thr, n1, inner, cola, maga, uppera, early, both,
    block, lower,
):
    rows, here, deep = grads.shape
    piece, width = hid_own.shape
    half = width // 2
    mid = here // 2
    _, bn, bw = block.shape
    n = 192
    en = 72
    nc, nz = n // 2, n // 2 // Z
    wx, wy = width // X, width // X // Y
    s = jax.ShapeDtypeStruct
    v = pltpu.VMEM
    return call(
        tail_kernel,
        (s((rows, here, width), BF16), s((n, width), F32), s((bn, bw), F32), s((en, HD), F32)),
        [VM] * 7 + [ANY] + [VM] * 8,
        (ANY, VM, VM, VM),
        [
            v((X, Y, piece, deep), BF16),
            v((2, here, half), BF16),
            v((2, 2, here, half), BF16),
            v((2, 2, mid, half), F32),
            v((2, 2, mid, half), BF16),
            v((2, 2, here, half), BF16),
            v((2, here, half), F32),
            v((2, 3, piece, half), BF16),
            v((2, 3, piece, half), BF16),
            v((piece, width), F32),
            v((rows, here, width), BF16),
            v((rows, here, width), BF16),
            v((rows * here, 48), BF16),
            v((n, width), F32),
            v((nc, width), F32),
            v((nc, width), F32),
            v((3, nz, width), F32),
            v((nz, width), F32),
            v((3, nz, wx), F32),
            v((nz, wx), F32),
            v((3, nz, wy), F32),
            v((3, bn, bw), F32),
            v((3, 16, HD), F32),
            v((bn, bw), F32),
            v((bn, bw), F32),
            v((en, HD), F32),
            v((en, HD), F32),
            v((3, en, HD), F32),
            v((3, bn, bw), F32),
            dma(2, 6), dma(2, 6), dma(2, 3), dma(2, 3), dma(6, 3), dma(6, 3),
            dma(14, 4), dma(14, 4), dma(2),
        ],
        3,
        2 * rows * here * deep * width,
        16 * 2**20,
    )(
        grads, weight, hid_own, gain, d_resid, pre, thr, n1, inner, cola, maga, uppera, early, both,
        block, lower,
    )


def on_device(
    hidden,
    segments,
    key_attendable,
    attention_gain,
    feedforward_gain,
    attend_frozen,
    output_frozen,
    expand_frozen,
    reduce_frozen,
    attend_lower,
    attend_upper,
    attend_magnitude,
    output_lower,
    output_upper,
    output_magnitude,
    expand_lower,
    expand_upper,
    expand_magnitude,
    reduce_lower,
    reduce_upper,
    reduce_magnitude,
    cotangent,
):
    rows, here, width = hidden.shape
    length = segments.shape[1]
    ff = reduce_frozen.shape[0]
    piece = here // Y
    rank = output_lower.shape[1]
    ctx = lax.axis_index("ctx")
    tp = lax.axis_index("tp")
    y, x = tp // X, tp % X
    offset = ctx * here

    def left_factor(a):
        high, low = halves(a)
        return jnp.concatenate([high, high, low], axis=-1)

    def right_factor(a):
        high, low = halves(a)
        return jnp.concatenate([high, low, high], axis=-2)

    fw = jnp.concatenate(
        [output_frozen, expand_frozen[0].T, expand_frozen[1].T, reduce_frozen], axis=0
    )
    expand_upper_t = expand_upper.transpose(0, 2, 1)
    aw = left_factor(
        jnp.concatenate([output_lower, expand_upper_t[0], expand_upper_t[1], reduce_lower], axis=0)
    )
    bw = right_factor(
        jnp.stack([output_upper, expand_lower[0].T, expand_lower[1].T, reduce_upper], axis=0)
    )
    la = left_factor(attend_lower)
    ua = right_factor(attend_upper)
    flat_lower = attend_lower.transpose(1, 0, 2).reshape(width, 3 * rank)
    high, low = halves(flat_lower)
    thin = jnp.concatenate([high, low, jnp.zeros((width, HD - 6 * rank), BF16)], axis=1)
    flat_lower = expand_lower.transpose(1, 0, 2).reshape(width, 2 * rank)
    high, low = halves(flat_lower)
    el = jnp.concatenate([high, low, jnp.zeros((width, HD - 4 * rank), BF16)], axis=1)
    small = jnp.concatenate([expand_upper_t[0], expand_upper_t[1], reduce_lower], axis=1)
    small = jnp.concatenate(
        [
            jnp.pad(small, ((0, 0), (0, HD - 3 * rank))),
            jnp.pad(output_lower, ((0, 0), (0, HD - rank))),
        ],
        axis=0,
    )
    mago = jnp.stack([output_magnitude, reduce_magnitude])
    upper = jnp.concatenate([output_upper, reduce_upper], axis=0)

    levels = jnp.arange(SEGS, dtype=jnp.int32)
    below_count = jnp.sum((segments[:, None, :] < levels[None, :, None]).astype(F32), axis=2)
    segments_here = lax.dynamic_slice_in_dim(segments, offset, here, 1)
    begin_here = jnp.sum(
        (segments_here[:, :, None] == levels[None, None, :]).astype(F32) * below_count[:, None, :],
        axis=2,
    )
    spot_here = offset + jnp.arange(here, dtype=jnp.int32)
    places = spot_here.astype(F32)[None, :] - begin_here
    frequency = rotary_base ** (-(2.0 * jnp.arange(HD // 2).astype(F32)) / HD)
    frequency = jnp.concatenate([frequency, frequency])
    angles = places[:, :, None] * frequency[None, None, :]
    cosine, sine_part = jnp.cos(angles), jnp.sin(angles)
    spots = jnp.arange(length, dtype=jnp.int32)[None]
    key_tag = jnp.where(key_attendable == 1, spots, -1)[:, None, :]
    begin = begin_here.astype(jnp.int32)[:, :, None]
    gain_one = attention_gain.astype(F32)
    gain_two = feedforward_gain.astype(F32)

    def take_row(a):
        mine = lax.dynamic_index_in_dim(a, x, 0, keepdims=False)
        return roll_blocks(mine.reshape(Y, piece, width), 0, y)

    (
        mixed_parts,
        soft,
        log_total,
        all_pairs,
        weights_x,
        weight_attend,
        queries,
        pre,
        through_three,
        column_attend,
        column_expand,
        squares,
        inner_attend,
        inner_expand,
        inner_both,
        normed_one,
        small_x,
    ) = front(
        hidden,
        gain_one[None],
        attend_frozen,
        la,
        ua,
        attend_magnitude,
        thin,
        fw,
        aw,
        bw,
        expand_magnitude.reshape(2 * ff, 1),
        mago,
        el,
        small,
        cosine,
        sine_part,
        begin,
        key_tag,
    )
    hid_own = take_row(hidden)[0]
    cot_row = take_row(cotangent).reshape(here, width)
    d_resid, block_own, d_mixed_parts, early, block_x, lower_out = feed(
        mixed_parts, hid_own, gain_two[None], cot_row, weights_x, small_x, el, upper, mago, squares
    )
    grads_low, block_output = attend_back(
        queries,
        all_pairs,
        d_mixed_parts,
        soft,
        log_total,
        begin,
        key_tag,
        cosine,
        sine_part,
        block_own,
    )
    hidden_grad, everywhere, block_x, small_ctx = tail(
        grads_low,
        weight_attend,
        hid_own,
        gain_one[None],
        d_resid,
        pre,
        through_three,
        normed_one,
        inner_attend,
        column_attend,
        attend_magnitude,
        attend_upper,
        early,
        inner_both,
        block_x,
        lower_out,
    )
    hidden_grad = hidden_grad.astype(F32)
    lower_out, local = small_ctx[:rank], small_ctx[rank:]
    late = adapter_scale * everywhere[7 * rank : 10 * rank]
    early = everywhere[: 7 * rank]

    attend_lower_grad = late.reshape(3, rank, width).transpose(0, 2, 1)
    attend_upper_grad = local[: 3 * rank].reshape(3, rank, HD)
    attend_magnitude_grad = local[3 * rank : 3 * rank + 3]
    column_expand = column_expand.reshape(2, ff)
    inner_expand = inner_expand.reshape(2, ff, HD)
    inner_expand = inner_expand[..., : 2 * rank] + inner_expand[..., 2 * rank : 4 * rank]
    expand_magnitude_grad = block_x[3 * rank : 3 * rank + 2] / expand_magnitude
    pull_expand = expand_magnitude * expand_magnitude_grad / column_expand**2
    ratio_expand = expand_magnitude / column_expand
    expand_upper_grad = jnp.stack(
        [
            adapter_scale
            * (
                block_x[m * rank : (m + 1) * rank] * ratio_expand[m]
                - inner_expand[m, :, m * rank : (m + 1) * rank].T * pull_expand[m]
            )
            for m in range(2)
        ]
    )
    expand_lower_grad = adapter_scale * early[: 2 * rank].reshape(2, rank, width).transpose(0, 2, 1)
    columns = jnp.sqrt(squares)
    magnitude_grads = early[4 * rank : 4 * rank + 2] / mago
    pulls = mago * magnitude_grads / squares
    ratios = mago / columns
    output_magnitude_grad = magnitude_grads[0]
    reduce_magnitude_grad = magnitude_grads[1]
    output_upper_grad = adapter_scale * (
        early[2 * rank : 3 * rank] * ratios[0] - early[5 * rank : 6 * rank] * pulls[0]
    )
    reduce_upper_grad = adapter_scale * (
        early[3 * rank : 4 * rank] * ratios[1] - early[6 * rank : 7 * rank] * pulls[1]
    )

    def pulled_rows(frozen, lower, upper, pull):
        pulled = upper * pull
        rows_part = exact_dot(frozen, pulled, ((1,), (1,)))
        return rows_part + adapter_scale * jnp.dot(
            lower,
            jnp.dot(upper, pulled.T, precision=lax.Precision.HIGHEST),
            precision=lax.Precision.HIGHEST,
        )

    output_lower_grad = adapter_scale * (
        lower_out.T - pulled_rows(output_frozen, output_lower, output_upper, pulls[0])
    )
    reduce_lower_grad = adapter_scale * (
        block_x[2 * rank : 3 * rank].T
        - pulled_rows(reduce_frozen, reduce_lower, reduce_upper, pulls[1])
    )
    return (
        block_output,
        hidden_grad,
        attend_lower_grad,
        attend_upper_grad,
        attend_magnitude_grad,
        output_lower_grad,
        output_upper_grad,
        output_magnitude_grad,
        expand_lower_grad,
        expand_upper_grad,
        expand_magnitude_grad,
        reduce_lower_grad,
        reduce_upper_grad,
        reduce_magnitude_grad,
    )


def solution(mesh):
    placed = (
        P(None, "ctx", None),
        P(),
        P(),
        P(),
        P(),
        P(None, None, "tp"),
        P("tp", None),
        P(None, None, "tp"),
        P("tp", None),
        P(),
        P(None, None, "tp"),
        P(None, "tp"),
        P("tp", None),
        P(),
        P(),
        P(),
        P(None, None, "tp"),
        P(None, "tp"),
        P("tp", None),
        P(),
        P(),
        P(None, "ctx", None),
    )
    return jax.shard_map(
        on_device,
        mesh=mesh,
        in_specs=placed,
        out_specs=(
            P(None, "ctx", None),
            P(None, "ctx", None),
            P(),
            P(None, None, "tp"),
            P(None, "tp"),
            P("tp", None),
            P(),
            P(),
            P(),
            P(None, None, "tp"),
            P(None, "tp"),
            P("tp", None),
            P(),
            P(),
        ),
        check_vma=False,
    )
```

```python
import jax
import jax.numpy as jnp
from jax import lax
from jax.experimental import pallas as pl
from jax.experimental.pallas import tpu as pltpu
from jax.sharding import PartitionSpec as P

HD = 128
SEGS = 4
X = 4
Y = 4
Z = 4

epsilon = 1e-05
adapter_scale = 2.0
rotary_base = 10000.0
F32 = jnp.float32
BF16 = jnp.bfloat16


def halves(a):
    high = lax.reduce_precision(a, 8, 7)
    return high.astype(BF16), (a - high).astype(BF16)


def dot32(a, b, dims):
    return lax.dot_general(a, b, (dims, ((), ())), preferred_element_type=F32)


def exact_dot(bf, full, dims):
    high, low = halves(full)
    return dot32(bf, high, dims) + dot32(bf, low, dims)


def rotate(tensor, cosine, sine_part):
    half_width = tensor.shape[-1] // 2
    turned = jnp.concatenate([-tensor[..., half_width:], tensor[..., :half_width]], axis=-1)
    return tensor * cosine + turned * sine_part


MESH = pl.DeviceIdType.MESH
ANY = pl.BlockSpec(memory_space=pl.ANY)
VM = pl.BlockSpec(memory_space=pltpu.VMEM)
NEAR_LAST = (2, 1, 3)


def place():
    ctx = lax.axis_index("ctx")
    tp = lax.axis_index("tp")
    return ctx // 2, ctx % 2, tp // X, tp % X


def device(dz=0, dc=0, dy=0, dx=0):
    z, core, y, x = place()
    return (((z + dz) % Z) * 2 + (core + dc) % 2, ((y + dy) % Y) * X + (x + dx) % X)


def greet(devices):
    barrier = pltpu.get_barrier_semaphore()
    for d in devices:
        pl.semaphore_signal(barrier, inc=1, device_id=d, device_id_type=MESH)
    pl.semaphore_wait(barrier, len(devices))


def send(src, dst, send_sem, recv_sem, to):
    copy = pltpu.make_async_remote_copy(
        src_ref=src,
        dst_ref=dst,
        send_sem=send_sem,
        recv_sem=recv_sem,
        device_id=to,
        device_id_type=MESH,
    )
    copy.start()
    return copy


def keep(src, dst, sem):
    copy = pltpu.make_async_copy(src, dst, sem)
    copy.start()
    return copy


def dma(*shape):
    return pltpu.SemaphoreType.DMA(shape)


def call(kernel, outs, in_specs, out_specs, scratch, number, flops, moved):
    return pl.pallas_call(
        kernel,
        out_shape=outs,
        in_specs=in_specs,
        out_specs=out_specs,
        scratch_shapes=scratch,
        cost_estimate=pl.CostEstimate(flops=flops, bytes_accessed=moved, transcendentals=0),
        compiler_params=pltpu.CompilerParams(
            collective_id=number, has_side_effects=True, vmem_limit_bytes=58 * 2**20
        ),
    )


def mask_of(begin, spot_q, key_tag, key_spot):
    return ((key_tag >= begin) & (key_tag <= spot_q)) | (key_spot == spot_q)


KB = 512


def tiles(total, size):
    return [(s, min(size, total - s)) for s in range(0, total, size)]


PIECES = 3


def relay_plan(weights, send_a, recv_a, send_b, recv_b, send_s, recv_s, cols):
    def begin(p, own, start, size):
        return [
            send(own, weights(1, start, size), send_a.at[p, 0], recv_a.at[p, 0], device(dx=1)),
            send(own, weights(3, start, size), send_a.at[p, 1], recv_a.at[p, 1], device(dx=3)),
        ]

    def relay(p, copies, start, size):
        half = size // 2
        more = []
        for k, (slot, at, to) in enumerate(((1, start, 1), (3, start + half, 3))):
            copies[k].wait_recv()
            more.append(
                send(
                    weights(slot, at, half), weights(2, at, half),
                    send_b.at[p, k], recv_b.at[p, k], device(dx=to),
                )
            )
            there = weights(slot, start, size)
            more.append(send(there, there, send_s.at[p, k], recv_s.at[p, k], device(dc=1)))
        return more

    def relay_far(p, more, start, size):
        more[0].wait_recv()
        more[2].wait_recv()
        there = weights(2, start, size)
        return send(there, there, send_s.at[p, 2], recv_s.at[p, 2], device(dc=1))

    def finish(copies, more, last):
        more[1].wait_recv()
        more[3].wait_recv()
        last.wait_recv()
        for copy in copies + more + [last]:
            copy.wait_send()

    return begin, relay, relay_far, finish


def front_kernel(
    hid_ref, gain_ref, fa_ref, la_ref, ua_ref, maga_ref, thin_ref, fo_ref, fe_ref, fr_ref, aw_ref, bw_ref,
    mage_ref, mago_ref, el_ref, small_ref, cos_ref, sin_ref, begin_ref, tag_ref,
    mixed_out, soft_out, log_out, kv_out, weights_out, wq_out, q_out, pre_out, thr_out,
    cola_out, cole_out, sq_out, ina_out, ine_out, ino_out, n1_out, small,
    kv_all, score, soft, logs, mixed, mixed_x, joined, w_own, wq_all, normed, kv_own,
    sq_x, sq_y, sq_one, ja,
    kv_send, kv_recv, sib_send, sib_recv, a_send, a_recv, b_send, b_recv, ws_send, ws_recv,
    wz_send, wz_recv, wo_send, wo_recv, m_send, m_recv, sq_send, sq_recv, local, n_local,
):
    z, core, y, x = place()
    me = z * 2 + core
    rows, here, width = hid_ref.shape
    length = Z * 2 * here
    ff = fr_ref.shape[0]
    piece = here // Y
    step = width // 16
    odd = z % 2
    xcols = pl.ds(pl.multiple_of((core * 8 + odd * 3) * step, step), 5 * step)
    zmine = pl.ds(pl.multiple_of((core * 8 + odd * 5) * step, step), 3 * step)
    zother = pl.ds(pl.multiple_of((core * 8 + (1 - odd) * 5) * step, step), 3 * step)
    greet(
        [device(dx=d) for d in (1, 2, 3)]
        + [device(dy=d) for d in (1, 2, 3)]
        + [device(dz=d) for d in (1, 2, 3)]
        + [device(dc=1)]
    )

    def join(matrix, start, size, at):
        low = dot32(aw_ref[start : start + size], bw_ref[matrix, :, at], ((1,), (0,)))
        if matrix in (1, 2):
            frozen = fe_ref[matrix - 1, :, at]
        else:
            frozen = fr_ref[:, at] if matrix else fo_ref[:, at]
        return frozen.astype(F32) + adapter_scale * low

    for s, size in tiles(width, 512):
        at = slice(s, s + size)
        one = join(0, 0, HD, at)
        two = join(3, HD + 2 * ff, ff, at)
        sq_one[0:1, at] = jnp.sum(one * one, axis=0, keepdims=True)
        sq_one[1:2, at] = jnp.sum(two * two, axis=0, keepdims=True)
    sq_copies = [
        send(sq_one, sq_x.at[d - 1], sq_send.at[0, d - 1], sq_recv.at[0, d - 1], device(dx=d))
        for d in NEAR_LAST
    ]

    where = ((HD, ff), (HD + ff, ff), (0, HD))
    moves = [{}, {}, {}]

    def there(slot, start, size, cols):
        return weights_out.at[slot, pl.ds(start, size), cols]

    def begin(p):
        start, size = where[p]
        for k, (slot, d) in enumerate(((1, 1), (3, 3))):
            moves[p]["a", k] = send(
                w_own.at[pl.ds(start, size), xcols], there(slot, start, size, xcols),
                a_send.at[p, k], a_recv.at[p, k], device(dx=d),
            )

    def share(p, slot):
        start, size = where[p]
        half = size // 2
        at = there(slot, start, size, xcols)
        moves[p]["s", slot] = send(
            at, at, ws_send.at[p, slot - 1], ws_recv.at[p, slot - 1], device(dc=1)
        )
        for k, (first, d) in enumerate(((start, 1), (start + half, 3))):
            at = there(slot, first, half, zmine)
            moves[p]["z", slot, k] = send(
                at, at, wz_send.at[p, slot - 1, k], wz_recv.at[p, slot - 1, k], device(dz=d)
            )

    def relay(p):
        start, size = where[p]
        half = size // 2
        for k, (slot, first) in enumerate(((1, start), (3, start + half))):
            moves[p]["a", k].wait_recv()
            moves[p]["b", k] = send(
                there(slot, first, half, xcols), there(2, first, half, xcols),
                b_send.at[p, k], b_recv.at[p, k], device(dx=slot),
            )
            share(p, slot)

    def relay_far(p):
        moves[p]["b", 0].wait_recv()
        moves[p]["b", 1].wait_recv()
        share(p, 2)

    def relay_z(p, slot):
        start, size = where[p]
        moves[p]["z", slot, 0].wait_recv()
        moves[p]["z", slot, 1].wait_recv()
        at = there(slot, start, size, zother)
        moves[p]["o", slot] = send(
            at, at, wo_send.at[p, slot - 1], wo_recv.at[p, slot - 1], device(dc=1)
        )

    def finish(p):
        for slot in (1, 2, 3):
            moves[p]["s", slot].wait_recv()
            moves[p]["o", slot].wait_recv()
        for copy in moves[p].values():
            copy.wait_send()

    for m in range(2):
        start = HD + m * ff
        total = jnp.zeros((ff, 1), F32)
        for s, size in tiles(width, 512):
            at = slice(s, s + size)
            value = join(1 + m, start, ff, at)
            joined[:, at] = value
            total = total + jnp.sum(value * value, axis=1, keepdims=True)
        column = jnp.sqrt(total)
        cole_out[m * ff : (m + 1) * ff] = column
        magnitude = mage_ref[m * ff : (m + 1) * ff]
        ratio = magnitude / column
        for s, size in tiles(width, 512):
            at = slice(s, s + size)
            w_own[start : start + ff, at] = (joined[:, at] * ratio).astype(BF16)
        begin(m)
        inner = dot32(w_own[start : start + ff], el_ref[...], ((1,), (0,)))
        ine_out[m * ff : (m + 1) * ff] = inner / ratio
        source = small_ref[0:ff, m * 16 : (m + 1) * 16]
        small[0:ff, m * 16 : (m + 1) * 16] = (source * ratio).astype(BF16)
        small[0:ff, (3 + m) * 16 : (4 + m) * 16] = (source / (magnitude * column)).astype(BF16)
    small[0:ff, 32:48] = small_ref[0:ff, 32:48].astype(BF16)
    small[0:ff, 80:] = jnp.zeros((ff, HD - 80), BF16)
    small[ff:] = small_ref[ff:].astype(BF16)
    own = []
    for copy in sq_copies:
        copy.wait()
    sq_one[...] += sq_x[0] + sq_x[1] + sq_x[2]
    sq_copies = [
        send(sq_one, sq_y.at[d - 1], sq_send.at[1, d - 1], sq_recv.at[1, d - 1], device(dy=d))
        for d in NEAR_LAST
    ]
    for m in range(3):
        total = jnp.zeros((1, HD), F32)
        for s, size in tiles(width, 512):
            at = slice(s, s + size)
            value = fa_ref[m, at].astype(F32) + adapter_scale * dot32(
                la_ref[m, at], ua_ref[m], ((1,), (0,))
            )
            ja[at] = value
            total = total + jnp.sum(value * value, axis=0, keepdims=True)
        column = jnp.sqrt(total)
        cola_out[m : m + 1] = column
        ratio = maga_ref[m : m + 1] / column
        wq_all[:, m * HD : (m + 1) * HD] = (ja[...] * ratio).astype(BF16)
        inner = dot32(la_ref[m], ja[...].astype(BF16), ((0,), (0,)))
        ina_out[m] = inner[0:16] + inner[32:48]
    own.append(keep(wq_all, wq_out, local.at[1]))
    kv_copies, sib_copies, n_copies = {}, [], []
    gain = gain_ref[...]
    for r in range(rows):
        inputs = hid_ref[r].astype(F32)
        inverse = lax.rsqrt(jnp.mean(inputs * inputs, axis=1, keepdims=True) + epsilon)
        if r >= 2:
            n_copies[r - 2].wait()
        normed[r % 2] = (inputs * inverse * gain).astype(BF16)
        n_copies.append(keep(normed.at[r % 2], n1_out.at[r], n_local.at[r]))
        pre = dot32(normed[r % 2], wq_all[...], ((1,), (0,)))
        pre_out[r] = pre
        thin = dot32(normed[r % 2], thin_ref[...], ((1,), (0,)))
        thr_out[r] = thin
        cosine, sine = cos_ref[r], sin_ref[r]
        q_out[r] = rotate(pre[:, :HD], cosine, sine).astype(BF16)
        kv_own[r, :, :HD] = rotate(pre[:, HD : 2 * HD], cosine, sine).astype(BF16)
        kv_own[r, :, HD:] = pre[:, 2 * HD :].astype(BF16)
        for k, d in enumerate((1, 3)):
            kv_copies[r, k] = send(
                kv_own.at[r], kv_all.at[me, r], kv_send.at[r, k], kv_recv.at[r, k], device(dz=d)
            )
        sib_copies.append(
            send(kv_own.at[r], kv_all.at[me, r], sib_send.at[r, 0], sib_recv.at[r, 0], device(dc=1))
        )
    own.append(keep(kv_own, kv_all.at[me], local.at[2]))
    for copy in sq_copies:
        copy.wait()
    squares = sq_one[...] + (sq_y[0] + sq_y[1] + sq_y[2])
    sq_out[...] = squares
    ratios = mago_ref[...] / jnp.sqrt(squares)
    for s, size in tiles(width, 512):
        at = slice(s, s + size)
        one = join(0, 0, HD, at)
        two = join(3, HD + 2 * ff, ff, at)
        w_own[0:HD, at] = (one * ratios[0:1, at]).astype(BF16)
        w_own[HD + 2 * ff :, at] = (two * ratios[1:2, at]).astype(BF16)
        ino_out[0:16, at] = dot32(small[ff:], one.astype(BF16), ((0,), (0,)))[0:16]
        ino_out[16:32, at] = dot32(small[0:ff], two.astype(BF16), ((0,), (0,)))[32:48]
    begin(2)
    own.append(keep(w_own, weights_out.at[0], local.at[3]))

    def pass_kv(r):
        for k, d in enumerate((1, 3)):
            kv_copies[r, k].wait_recv()
            at = kv_all.at[((z + Z - d) % Z) * 2 + core, r]
            if (k == 0) == (r < rows // 2):
                kv_copies[r, 2] = send(at, at, kv_send.at[r, 2], kv_recv.at[r, 2], device(dz=d))
            sib_copies.append(
                send(at, at, sib_send.at[r, 1 + k], sib_recv.at[r, 1 + k], device(dc=1))
            )

    def pass_far(r):
        kv_copies[r, 2].wait_recv()
        at = kv_all.at[((z + 2) % Z) * 2 + core, r]
        sib_copies.append(send(at, at, sib_send.at[r, 3], sib_recv.at[r, 3], device(dc=1)))

    for r in range(rows):
        pass_kv(r)
    relay(0)
    for r in range(rows):
        pass_far(r)
    relay(1)
    own[1].wait()
    for copy in sib_copies:
        copy.wait_recv()
    own.append(keep(kv_all, kv_out, local.at[4]))
    spot_q = lax.broadcasted_iota(jnp.int32, (here, 1), 0) + me * here
    m_copies = []
    for i in (2, 1, 3, 0):
        row = (x + i) % X
        query = q_out[row]
        first = begin_ref[row]
        peak = jnp.full((here, 1), -1e30, F32)
        for b in range(length // KB):
            keys = jnp.concatenate(
                [kv_all[b * (KB // here) + k, row, :, :HD] for k in range(KB // here)], axis=0
            )
            raw = dot32(query, keys, ((1,), (1,))) * (HD**-0.5)
            key_spot = lax.broadcasted_iota(jnp.int32, (1, KB), 1) + b * KB
            ok = mask_of(first, spot_q, tag_ref[row, :, b * KB : (b + 1) * KB], key_spot)
            raw = jnp.where(ok, raw, -1e30)
            score[:, b * KB : (b + 1) * KB] = raw
            peak = jnp.maximum(peak, jnp.max(raw, axis=1, keepdims=True))
        total = jnp.zeros((here, 1), F32)
        gathered = jnp.zeros((here, HD), F32)
        for b in range(length // KB):
            power = jnp.exp(score[:, b * KB : (b + 1) * KB] - peak)
            total = total + jnp.sum(power, axis=1, keepdims=True)
            values = jnp.concatenate(
                [kv_all[b * (KB // here) + k, row, :, HD:] for k in range(KB // here)], axis=0
            )
            gathered = gathered + dot32(power.astype(BF16), values, ((1,), (0,)))
        soft[row] = gathered / total
        logs[row] = peak + jnp.log(total)
        for j in range(Y):
            mixed[i, j * piece : (j + 1) * piece] = soft[
                row, pl.ds(pl.multiple_of(((y + j) % Y) * piece, piece), piece)
            ].astype(BF16)
        if i:
            m_copies.append(
                send(mixed.at[i], mixed_x.at[i], m_send.at[i - 1], m_recv.at[i - 1], device(dx=i))
            )
        else:
            mixed_x[0] = mixed[0]
        if i == 2:
            relay(2)
        if i == 1:
            relay_far(0)
            relay_z(0, 1)
            relay_z(0, 3)
        if i == 3:
            relay_far(1)
            relay_z(1, 1)
            relay_z(1, 3)
    own.append(keep(soft, soft_out, local.at[5]))
    own.append(keep(logs, log_out, local.at[6]))
    relay_far(2)
    relay_z(2, 1)
    relay_z(2, 3)
    for p in range(PIECES):
        relay_z(p, 2)
    for copy in m_copies:
        copy.wait()
    own.append(keep(mixed_x, mixed_out, local.at[7]))
    for copy in list(kv_copies.values()) + sib_copies:
        copy.wait_send()
    for p in range(PIECES):
        finish(p)
    for copy in n_copies[rows - 2 :]:
        copy.wait()
    own.pop(1)
    for copy in own:
        copy.wait()


def front(
    hidden, gain, fa, la, ua, maga, thin, fo, fe, fr, aw, bw, mage, mago, el, small, cos, sin,
    begin, tag,
):
    rows, here, width = hidden.shape
    ff = fr.shape[0]
    count = HD + 3 * ff
    length = 2 * Z * here
    s = jax.ShapeDtypeStruct
    return call(
        front_kernel,
        (
            s((X, here, HD), BF16),
            s((rows, here, HD), F32),
            s((rows, here, 1), F32),
            s((2 * Z, rows, here, 2 * HD), BF16),
            s((X, count, width), BF16),
            s((width, 3 * HD), BF16),
            s((rows, here, HD), BF16),
            s((rows, here, 3 * HD), F32),
            s((rows, here, HD), F32),
            s((3, HD), F32),
            s((2 * ff, 1), F32),
            s((2, width), F32),
            s((3, 16, HD), F32),
            s((2 * ff, HD), F32),
            s((32, width), F32),
            s((rows, here, width), BF16),
            s((ff + HD, HD), BF16),
        ),
        [VM] * 20,
        (ANY,) * 6 + (VM,) * 9 + (ANY, VM),
        [
            pltpu.VMEM((2 * Z, rows, here, 2 * HD), BF16),
            pltpu.VMEM((here, length), F32),
            pltpu.VMEM((rows, here, HD), F32),
            pltpu.VMEM((rows, here, 1), F32),
            pltpu.VMEM((X, here, HD), BF16),
            pltpu.VMEM((X, here, HD), BF16),
            pltpu.VMEM((ff, width), F32),
            pltpu.VMEM((count, width), BF16),
            pltpu.VMEM((width, 3 * HD), BF16),
            pltpu.VMEM((2, here, width), BF16),
            pltpu.VMEM((rows, here, 2 * HD), BF16),
            pltpu.VMEM((3, 2, width), F32),
            pltpu.VMEM((3, 2, width), F32),
            pltpu.VMEM((2, width), F32),
            pltpu.VMEM((width, HD), F32),
            dma(rows, 3), dma(rows, 3), dma(rows, 4), dma(rows, 4),
            dma(PIECES, 2), dma(PIECES, 2), dma(PIECES, 2), dma(PIECES, 2),
            dma(PIECES, 3), dma(PIECES, 3), dma(PIECES, 3, 2), dma(PIECES, 3, 2),
            dma(PIECES, 3), dma(PIECES, 3),
            dma(3), dma(3), dma(2, 3), dma(2, 3), dma(8), dma(rows),
        ],
        0,
        2 * 2 * rows * here * length * HD + 2 * rows * here * width * 4 * HD,
        32 * 2**20,
    )(
        hidden, gain, fa, la, ua, maga, thin, fo, fe, fr, aw, bw, mage, mago, el, small, cos, sin,
        begin, tag,
    )


def feed_kernel(
    mixed_ref, hidden_ref, gain_ref, cotangent_ref, weights_ref, small_ref, el_ref, upper_ref, mago_ref,
    sq_ref,
    resid_grad_out, resid_s, ff_own, ff_send, dmix_out, early_out, columns_out, lower_out,
    out_w, gate_w, up_w, down_w, normed, low, act, dgate, dup, sends, recvs, acc, mags,
    hid_ref, cot_ref,
    small_x, load, s_send, s_recv, local, sm_send, sm_recv, a_send, a_recv, b_send, b_recv, ws_send, ws_recv,
):
    z, core, y, x = place()
    width = hid_ref.shape[1]
    piece = hid_ref.shape[0]
    here = cot_ref.shape[0]
    ff = gate_w.shape[0] // X
    cols = pl.ds(pl.multiple_of(core * (width // 2), width // 2), width // 2)
    down_rows = pl.ds(HD + 2 * ff, ff)
    tokens = pl.ds(pl.multiple_of(y * piece, piece), piece)
    loads = [[], [], [], [], [keep(hidden_ref.at[x, tokens], hid_ref, local.at[0])]]
    for j in range(Y):
        block = pl.ds(pl.multiple_of(((y + j) % Y) * piece, piece), piece)
        loads[4].append(
            keep(
                cotangent_ref.at[x, block], cot_ref.at[pl.ds(j * piece, piece)], local.at[1 + j]
            )
        )
    for w, (dst, start, size) in enumerate(((out_w, 0, HD), (gate_w, HD, ff), (up_w, HD + ff, ff))):
        for i in range(X):
            loads[w].append(
                keep(
                    weights_ref.at[i, pl.ds(start, size)], dst.at[pl.ds(i * size, size)],
                    load.at[w, i],
                )
            )
    loads[3].append(keep(weights_ref.at[0, down_rows], down_w.at[pl.ds(0, ff)], load.at[3, 0]))
    greet(
        [device(dy=d) for d in (1, 2, 3)] + [device(dx=1), device(dx=2), device(dx=3), device(dc=1)]
    )

    def there(slot, start, size):
        return down_w.at[pl.ds(slot * ff + start, size), cols]

    begin, relay, relay_far, finish = relay_plan(
        there, a_send, a_recv, b_send, b_recv, ws_send, ws_recv, cols
    )
    sent = begin(0, weights_ref.at[0, down_rows, cols], 0, ff)
    sm_copies = [
        send(small_ref, small_x.at[d], sm_send.at[d - 1], sm_recv.at[d - 1], device(dx=d))
        for d in NEAR_LAST
    ]

    def loaded(w):
        for copy in loads[w]:
            copy.wait()

    def start_scatter(k):
        return [
            send(
                sends.at[k, d - 1], recvs.at[k, d - 1], s_send.at[k, d - 1], s_recv.at[k, d - 1],
                device(dy=d),
            )
            for d in NEAR_LAST
        ]

    def put(k, part, start, size):
        at = slice(start, start + size)
        acc[k, :, at] = part[:piece]
        for d in range(1, Y):
            sends[k, d - 1, :, at] = part[d * piece : (d + 1) * piece].astype(BF16)

    def summed(k, copies):
        for copy in copies:
            copy.wait()
        return acc[k] + (
            recvs[k, 0].astype(F32) + recvs[k, 1].astype(F32) + recvs[k, 2].astype(F32)
        )

    def start_gather(buffer, k):
        return [
            send(
                buffer.at[pl.ds(0, piece)], buffer.at[pl.ds((Y - d) * piece, piece)],
                s_send.at[k, d - 1], s_recv.at[k, d - 1], device(dy=d),
            )
            for d in NEAR_LAST
        ]

    loaded(0)
    mixed_cat = jnp.concatenate([mixed_ref[i] for i in range(X)], axis=1)
    for start, size in tiles(width, 512):
        put(0, dot32(mixed_cat, out_w[:, start : start + size], ((1,), (0,))), start, size)
    copies = start_scatter(0)
    ratios = mago_ref[...] / jnp.sqrt(sq_ref[...])
    upper_o = (upper_ref[0:16] * ratios[0:1]).astype(BF16)
    upper_d = (upper_ref[16:32] * ratios[1:2]).astype(BF16)
    loaded(4)
    through_down = dot32(cot_ref[...], upper_d, ((1,), (1,))).astype(BF16)
    attended = summed(0, copies)
    acc[0] = attended
    gain = gain_ref[...]
    resid = hid_ref[...].astype(F32) + attended
    inverse = lax.rsqrt(jnp.mean(resid * resid, axis=1, keepdims=True) + epsilon)
    resid_s[...] = resid
    normed[0:piece] = (resid * inverse * gain).astype(BF16)
    copies = start_gather(normed, 3)
    more = relay(0, sent, 0, ff)
    loaded(1)
    loaded(2)
    loaded(3)
    for copy in copies:
        copy.wait()
    far = relay_far(0, more, 0, ff)
    finish(sent, more, far)
    for start, size in tiles(X * ff, 256):
        at = slice(start, start + size)
        gate = dot32(normed[...], gate_w[at], ((1,), (1,)))
        up = dot32(normed[...], up_w[at], ((1,), (1,)))
        d_act = dot32(cot_ref[...], down_w[at], ((1,), (1,)))
        sig = 1.0 / (1.0 + jnp.exp(-gate))
        gated = gate * sig
        act[:, at] = (gated * up).astype(BF16)
        d_gate = (d_act * up * sig * (1.0 + gate * (1.0 - sig))).astype(BF16)
        d_up = (d_act * gated).astype(BF16)
        dgate[:, at] = d_gate
        dup[:, at] = d_up
        mags[0:1, at] = jnp.sum(d_gate.astype(F32) * gate, axis=0, keepdims=True)
        mags[1:2, at] = jnp.sum(d_up.astype(F32) * up, axis=0, keepdims=True)
    for start, size in tiles(width, 512):
        at = slice(start, start + size)
        part = dot32(dgate[...], gate_w[:, at], ((1,), (0,)))
        part = part + dot32(dup[...], up_w[:, at], ((1,), (0,)))
        put(1, part, start, size)
    two_copies = start_scatter(1)
    for start, size in tiles(width, 512):
        at = slice(start, start + size)
        part = dot32(act[...], down_w[:, at], ((1,), (0,)))
        ff_own[:, at] = part[:piece]
        for d in range(1, Y):
            ff_send[d - 1, :, at] = part[d * piece : (d + 1) * piece].astype(BF16)
    for copy in sm_copies:
        copy.wait()
    small = jnp.concatenate([small_ref[0:ff]] + [small_x[i, 0:ff] for i in range(1, X)], axis=0)
    small_o = jnp.concatenate([small_ref[ff:]] + [small_x[i, ff:] for i in range(1, X)], axis=0)
    from_mixed = dot32(mixed_cat, small_o, ((1,), (0,)))[:, 0:16].astype(BF16)
    through = dot32(normed[...], el_ref[...], ((1,), (0,)))
    through = (through[:, 0:32] + through[:, 32:64]).astype(BF16)
    gate_down = dot32(dgate[...], small, ((1,), (0,)))[:, 0:16].astype(BF16)
    up_down = dot32(dup[...], small, ((1,), (0,)))[:, 16:32].astype(BF16)
    from_act = dot32(act[...], small, ((1,), (0,)))[:, 32:48].astype(BF16)
    small_t = jnp.transpose(small.astype(F32))
    pull_gate = (small_t[48:64] * mags[0:1]).astype(BF16)
    pull_up = (small_t[64:80] * mags[1:2]).astype(BF16)

    def columns(row, value):
        for i in range(X):
            columns_out[i, row : row + value.shape[0]] = value[:, i * ff : (i + 1) * ff]

    columns(0, dot32(through[:, 0:16], dgate[...], ((0,), (0,))))
    columns(16, dot32(through[:, 16:32], dup[...], ((0,), (0,))))
    columns(32, dot32(through_down, act[...], ((0,), (0,))))
    columns(48, jnp.concatenate([mags[...], jnp.zeros((6, X * ff), F32)], axis=0))
    early_out[0:16] = dot32(gate_down, normed[...], ((0,), (0,))) - dot32(
        pull_gate, gate_w[...], ((1,), (0,))
    )
    early_out[16:32] = dot32(up_down, normed[...], ((0,), (0,))) - dot32(
        pull_up, up_w[...], ((1,), (0,))
    )
    early_out[48:64] = dot32(from_act, cot_ref[...], ((0,), (0,)))
    d_two = summed(1, two_copies)
    resid = resid_s[...]
    inverse = lax.rsqrt(jnp.mean(resid * resid, axis=1, keepdims=True) + epsilon)
    scaled = d_two * gain
    cot_own = cot_ref[0:piece].astype(F32)
    d_resid = cot_own + (
        inverse * scaled
        - resid * (inverse * inverse * inverse) * jnp.mean(resid * scaled, axis=1, keepdims=True)
    )
    resid_grad_out[...] = d_resid
    own_low = d_resid.astype(BF16)
    low[0:piece] = own_low
    copies = start_gather(low, 4)
    mag_out = jnp.sum(own_low.astype(F32) * acc[0], axis=0, keepdims=True)
    early_out[64:80] = jnp.concatenate([mag_out, jnp.zeros((15, width), F32)], axis=0)
    for copy in copies:
        copy.wait()
    d_mixed = dot32(low[...], out_w[...], ((1,), (1,))).astype(BF16)
    for i in range(X):
        dmix_out[i] = d_mixed[:, i * HD : (i + 1) * HD]
    through_out = dot32(low[...], upper_o, ((1,), (1,))).astype(BF16)
    value = dot32(through_out, mixed_cat, ((0,), (0,)))
    for i in range(X):
        lower_out[i] = value[:, i * HD : (i + 1) * HD]
    early_out[32:48] = dot32(from_mixed, low[...], ((0,), (0,)))


def feed(mixed_x, hidden, gain, cotangent, weights, small, el, upper, mago, squares):
    _, here, width = hidden.shape
    piece = here // Y
    many = (weights.shape[1] - HD) // 3 * X
    s = jax.ShapeDtypeStruct
    return call(
        feed_kernel,
        (
            s((piece, width), F32),
            s((piece, width), F32),
            s((piece, width), F32),
            s((Y - 1, piece, width), BF16),
            s((X, here, HD), BF16),
            s((80, width), F32),
            s((X, 56, many // X), F32),
            s((X, 16, HD), F32),
        ),
        [VM, ANY, VM, ANY, ANY, VM, VM, VM, VM, VM],
        (VM,) * 8,
        [
            pltpu.VMEM((X * HD, width), BF16),
            pltpu.VMEM((many, width), BF16),
            pltpu.VMEM((many, width), BF16),
            pltpu.VMEM((many, width), BF16),
            pltpu.VMEM((here, width), BF16),
            pltpu.VMEM((here, width), BF16),
            pltpu.VMEM((here, many), BF16),
            pltpu.VMEM((here, many), BF16),
            pltpu.VMEM((here, many), BF16),
            pltpu.VMEM((2, Y - 1, piece, width), BF16),
            pltpu.VMEM((2, Y - 1, piece, width), BF16),
            pltpu.VMEM((2, piece, width), F32),
            pltpu.VMEM((2, many), F32),
            pltpu.VMEM((piece, width), BF16),
            pltpu.VMEM((here, width), BF16),
            pltpu.VMEM((X,) + small.shape, BF16),
            dma(4, X), dma(5, 3), dma(5, 3), dma(1 + Y), dma(3), dma(3), dma(1, 2), dma(1, 2), dma(1, 2), dma(1, 2),
            dma(1, 3), dma(1, 3),
        ],
        1,
        2 * here * many * width * 6,
        32 * 2**20,
    )(mixed_x, hidden, gain, cotangent, weights, small, el, upper, mago, squares)


def attend_back_kernel(
    q_ref, kv_ref, dmix_ref, soft_ref, log_ref, begin_ref, tag_ref, cos_ref, sin_ref, resid_ref,
    ff_own, ff_send, cot_ref,
    grads_out, block_out, mag_out,
    kv_all, dmix_all, dmix_abs, part, own, sib_s, sib_r, z_own, z_s, z_r, dq_s, ff_r, block_ref,
    cot_own, f_send, f_recv, d_send, d_recv, b_send, b_recv, sib_send, sib_recv, z_send, z_recv, local,
):
    z, core, y, x = place()
    me = z * 2 + core
    rows, here = q_ref.shape[0], q_ref.shape[1]
    piece, width = resid_ref.shape
    half = width // 2
    load = keep(kv_ref, kv_all, local.at[0])
    greet(
        [device(dx=d) for d in (1, 2, 3)]
        + [device(dy=d) for d in (1, 2, 3)]
        + [device(dz=d) for d in (1, 2, 3)]
        + [device(dc=1)]
    )
    d_copies = [
        send(
            dmix_ref.at[X - d], dmix_all.at[x], d_send.at[d - 1], d_recv.at[d - 1], device(dx=d)
        )
        for d in NEAR_LAST
    ]
    own_mix = keep(dmix_ref.at[0], dmix_all.at[x], local.at[1])
    tokens = pl.ds(pl.multiple_of(y * piece, piece), piece)
    left, right = pl.ds(0, half), pl.ds(half, half)
    load_cot = keep(cot_ref.at[x, tokens], cot_own, local.at[2])
    f_copies = [
        send(ff_send.at[d - 1], ff_r.at[d - 1], f_send.at[d - 1], f_recv.at[d - 1], device(dy=d))
        for d in NEAR_LAST
    ]
    block_one, block_two = [], {}
    load.wait()
    own_mix.wait()
    for copy in d_copies:
        copy.wait()
    spot_q = lax.broadcasted_iota(jnp.int32, (here, 1), 0) + me * here
    sib_copies, z_copies = [], []

    def pass_on(r):
        sib_copies[r].wait()
        z_own[r] = own[r, z] + sib_r[r, z].astype(F32)
        for d in NEAR_LAST:
            to = (z + d) % Z
            z_s[r, d - 1] = (own[r, to] + sib_r[r, to].astype(F32)).astype(BF16)
            z_copies.append(
                send(
                    z_s.at[r, d - 1], z_r.at[r, d - 1], z_send.at[r, d - 1], z_recv.at[r, d - 1],
                    device(dz=d),
                )
            )

    def back(a, r):
        cosine, sine = cos_ref[r], sin_ref[r]
        weighted = a * sine
        turned = jnp.concatenate([weighted[:, HD // 2 :], -weighted[:, : HD // 2]], axis=1)
        return a * cosine + turned

    for r in range(rows):
        for j in range(Y):
            dmix_abs[pl.ds(pl.multiple_of(((y + j) % Y) * piece, piece), piece)] = dmix_all[
                r, j * piece : (j + 1) * piece
            ]
        query = q_ref[r]
        grad = dmix_abs[...]
        delta = jnp.sum(grad.astype(F32) * soft_ref[r], axis=1, keepdims=True)
        begin = begin_ref[r]
        log = log_ref[r]
        d_query = jnp.zeros((here, HD), F32)
        for b in range(Z):
            keys = jnp.concatenate([kv_all[2 * b + k, r, :, :HD] for k in range(2)], axis=0)
            values = jnp.concatenate([kv_all[2 * b + k, r, :, HD:] for k in range(2)], axis=0)
            raw = dot32(query, keys, ((1,), (1,))) * (HD**-0.5)
            key_spot = lax.broadcasted_iota(jnp.int32, (1, KB), 1) + b * KB
            ok = mask_of(begin, spot_q, tag_ref[r, :, b * KB : (b + 1) * KB], key_spot)
            probs = jnp.exp(jnp.where(ok, raw, -1e30) - log)
            d_probs = dot32(grad, values, ((1,), (1,)))
            d_scores = (probs * (d_probs - delta)).astype(BF16)
            d_query = d_query + dot32(d_scores, keys, ((1,), (0,)))
            d_keys = dot32(d_scores, query, ((0,), (0,))) * (HD**-0.5)
            d_values = dot32(probs.astype(BF16), grad, ((0,), (0,)))
            for k in range(2):
                part[b, k, :, :HD] = d_keys[k * here : (k + 1) * here]
                part[b, k, :, HD:] = d_values[k * here : (k + 1) * here]
        dq_s[r] = d_query * (HD**-0.5)
        for b in range(Z):
            sib_s[r, b] = part[b, 1 - core].astype(BF16)
            own[r, b] = part[b, core]
        sib_copies.append(
            send(sib_s.at[r], sib_r.at[r], sib_send.at[r], sib_recv.at[r], device(dc=1))
        )
        grads_out[r, :, :HD] = back(dq_s[r], r).astype(BF16)
        if r:
            pass_on(r - 1)
        if r == 0:
            load_cot.wait()
            for copy in f_copies:
                copy.wait()
            feedforward = ff_own[...] + (
                ff_r[0].astype(F32) + ff_r[1].astype(F32) + ff_r[2].astype(F32)
            )
            mag_out[...] = jnp.zeros(mag_out.shape, F32) + jnp.sum(
                cot_own[...].astype(F32) * feedforward, axis=0, keepdims=True
            )
            block_ref[...] = (resid_ref[...] + feedforward).astype(BF16)
            own_block = keep(block_ref, block_out.at[x, tokens], local.at[3])
            for d in NEAR_LAST:
                for k, cut in enumerate((left, right)):
                    block_one.append(
                        send(
                            block_ref.at[:, cut], block_out.at[x, tokens, cut],
                            b_send.at[k, d - 1], b_recv.at[k, d - 1],
                            device(dy=d) if k else device(dx=d),
                        )
                    )
        if r == 1:
            own_block.wait()
            for copy in block_one:
                copy.wait()
            for k in range(2):
                for side, d in enumerate((1, 3)):
                    at = block_out.at[x, :, right] if k else block_out.at[:, tokens, left]
                    block_two[k, side] = send(
                        at, at, b_send.at[2 + k, side], b_recv.at[2 + k, side],
                        device(dx=d) if k else device(dy=d),
                    )
        if r == 3:
            for k in range(2):
                for side, d in enumerate((1, 3)):
                    block_two[k, side].wait_recv()
                    if k:
                        at = block_out.at[
                            (x + X - d) % X, pl.ds(side * (here // 2), here // 2), right
                        ]
                    else:
                        block = pl.ds(pl.multiple_of(((y + Y - d) % Y) * piece, piece), piece)
                        at = block_out.at[pl.ds(side * (rows // 2), rows // 2), block, left]
                    block_two[k, 2 + side] = send(
                        at, at, b_send.at[4 + k, side], b_recv.at[4 + k, side],
                        device(dx=d) if k else device(dy=d),
                    )
    pass_on(rows - 1)
    for r in range(rows):
        for copy in z_copies[3 * r : 3 * r + 3]:
            copy.wait()
        total = z_own[r] + (
            z_r[r, 0].astype(F32) + z_r[r, 1].astype(F32) + z_r[r, 2].astype(F32)
        )
        grads_out[r, :, HD : 2 * HD] = back(total[:, :HD], r).astype(BF16)
        grads_out[r, :, 2 * HD :] = total[:, HD:].astype(BF16)
    for k in range(2):
        for side in range(2):
            block_two[k, side].wait_send()
            block_two[k, 2 + side].wait()


def attend_back(
    queries, kv, dmix, soft, log, begin, tag, cosine, sine, resid, ff_own, ff_send, cotangent
):
    rows, here, _ = queries.shape
    piece, width = resid.shape
    return call(
        attend_back_kernel,
        (
            jax.ShapeDtypeStruct((rows, here, 3 * HD), BF16),
            jax.ShapeDtypeStruct((rows, here, width), BF16),
            jax.ShapeDtypeStruct((8, width), F32),
        ),
        [VM, ANY] + [VM] * 9 + [ANY, ANY],
        (VM, ANY, VM),
        [
            pltpu.VMEM((2 * Z, rows, here, 2 * HD), BF16),
            pltpu.VMEM((rows, here, HD), BF16),
            pltpu.VMEM((here, HD), BF16),
            pltpu.VMEM((Z, 2, here, 2 * HD), F32),
            pltpu.VMEM((rows, Z, here, 2 * HD), F32),
            pltpu.VMEM((rows, Z, here, 2 * HD), BF16),
            pltpu.VMEM((rows, Z, here, 2 * HD), BF16),
            pltpu.VMEM((rows, here, 2 * HD), F32),
            pltpu.VMEM((rows, Z - 1, here, 2 * HD), BF16),
            pltpu.VMEM((rows, Z - 1, here, 2 * HD), BF16),
            pltpu.VMEM((rows, here, HD), F32),
            pltpu.VMEM((Y - 1, piece, width), BF16),
            pltpu.VMEM((piece, width), BF16),
            pltpu.VMEM((piece, width), BF16),
            dma(3), dma(3), dma(3), dma(3), dma(6, 3), dma(6, 3), dma(rows), dma(rows),
            dma(rows, 3), dma(rows, 3), dma(4),
        ],
        2,
        2 * 5 * rows * here * 2 * Z * here * HD,
        32 * 2**20,
    )(
        queries, kv, dmix, soft, log, begin, tag, cosine, sine, resid, ff_own, ff_send, cotangent
    )


def tail_kernel(
    grads_ref, weight_ref, hidden_ref, gain_ref, dres_ref, pre_ref, thr_ref, n1_ref, inner_ref,
    cola_ref, maga_ref, uppera_ref, early_ref, both_ref, block_ref, lower_ref,
    magd_ref, grad_out, all_out, block_out, ctx_out,
    rel, two, near, held, hop, came, acc, send_2, recv_2, d_one, spread, n1, down, all_s,
    hid_ref, gath, c_r, z_s, z_b, z_r, x_s, x_r, y_v, bx_r, lx_r, b_one, b_two, e_one, e_two, e_z, b_z,
    s_one, r_one, s_two, r_two, s_gat, r_gat, ss, rs, local,
):
    z, core, y, x = place()
    rows, here, deep = grads_ref.shape
    piece, width = dres_ref.shape
    half = width // 2
    sub = piece // 2
    mid = here // 4
    n = all_s.shape[0]
    nc = n // 2
    wz, wx = width // Z, width // Z // X
    rank = 16
    load_hid = keep(
        hidden_ref.at[x, pl.ds(pl.multiple_of(y * piece, piece), piece)], hid_ref, local.at[2]
    )
    load = keep(n1_ref, n1, local.at[0])
    for i in range(X):
        for j in range(Y):
            rel[i, j] = grads_ref[
                (x + i) % X, pl.ds(pl.multiple_of(((y + j) % Y) * piece, piece), piece)
            ]
    greet(
        [device(dx=d) for d in (1, 2, 3)]
        + [device(dy=d) for d in (1, 2, 3)]
        + [device(dz=d) for d in (1, 2, 3)]
        + [device(dc=1)]
    )

    def to(k, d):
        return device(dy=d) if k else device(dx=d)

    def ds(index, size):
        return pl.ds(pl.multiple_of(index * size, size), size)

    def done(copies):
        for copy in copies:
            copy.wait()

    def term(k, d, begin, size):
        if k:
            lhs = jnp.concatenate([rel[i, d] for i in range(X)], axis=0)
        else:
            lhs = rel[d].reshape(here, deep)
        return dot32(lhs, weight_ref[k * half + begin : k * half + begin + size], ((1,), (1,)))

    def cut(part, u, first, count):
        return jnp.concatenate(
            [
                part[b * piece + u * sub : b * piece + (u + 1) * sub]
                for b in range(first, first + count)
            ],
            axis=0,
        )

    one = {}

    def start_far(u):
        for k in range(2):
            for side, d in enumerate((1, 3)):
                one[k, u, side] = send(
                    two.at[k, u, pl.ds(side * mid, mid)], hop.at[k, u, side],
                    s_one.at[k, u, side], r_one.at[k, u, side], to(k, d),
                )

    def start_near(u):
        for k in range(2):
            for side, d in enumerate((1, 3)):
                plain = pl.ds((1 - side) * mid, mid)
                one[k, u, 2 + side] = send(
                    near.at[k, u, side, plain], came.at[k, u, side, plain],
                    s_one.at[k, u, 2 + side], r_one.at[k, u, 2 + side], to(k, d),
                )

    for k in range(2):
        for start, size in tiles(half, 512):
            part = term(k, 2, start, size)
            for u in range(2):
                two[k, u, :, start : start + size] = cut(part, u, 0, 4).astype(BF16)
    start_far(0)
    for k in range(2):
        for side, d in enumerate((1, 3)):
            for start, size in tiles(half, 512):
                at = slice(start, start + size)
                part = term(k, d, start, size)
                rest = (1 - side) * mid
                for u in range(2):
                    near[k, u, side, rest : rest + mid, at] = cut(
                        part, u, 2 * (1 - side), 2
                    ).astype(BF16)
                    held[k, u, side, :, at] = cut(part, u, 2 * side, 2)
    start_near(0)
    start_far(1)
    start_near(1)
    for k in range(2):
        for start, size in tiles(half, 512):
            part = term(k, 0, start, size)
            for u in range(2):
                acc[k, u, :, start : start + size] = cut(part, u, 0, 4)

    for m in range(3):
        at = slice(m * HD, (m + 1) * HD)
        grad = grads_ref[:, :, at].reshape(rows * here, HD)
        before = pre_ref[:, :, at].reshape(rows * here, HD)
        column, magnitude = cola_ref[m : m + 1], maga_ref[m : m + 1]
        ratio = magnitude / column
        mag = jnp.sum(grad.astype(F32) * before, axis=0, keepdims=True) / magnitude
        pull = magnitude * mag / (column * column)
        thin = thr_ref[:, :, m * rank : (m + 1) * rank] + thr_ref[
            :, :, (3 + m) * rank : (4 + m) * rank
        ]
        thin = thin.reshape(rows * here, rank).astype(BF16)
        part = dot32(thin, grad, ((0,), (0,)))
        e_one[(1 + m) * rank : (2 + m) * rank] = adapter_scale * (
            part * ratio - inner_ref[m] * pull
        )
        e_one[4 * rank + m : 4 * rank + m + 1] = mag
        upper = uppera_ref[m]
        down[:, m * rank : (m + 1) * rank] = dot32(
            grad, (upper * ratio).astype(BF16), ((1,), (1,))
        ).astype(BF16)
        pulled = (upper * (mag / column)).astype(BF16)
        for start, size in tiles(width, 512):
            all_s[(7 + m) * rank : (8 + m) * rank, start : start + size] = dot32(
                pulled, weight_ref[start : start + size, at], ((1,), (1,))
            )
    e_one[4 * rank + 3 :] = jnp.zeros((e_one.shape[0] - 4 * rank - 3, HD), F32)
    load.wait()
    for start, size in tiles(width, 512):
        at = slice(start, start + size)
        value = dot32(
            down[...], n1[:, :, at].reshape(rows * here, size), ((0,), (0,))
        )
        all_s[7 * rank : 10 * rank, at] = value - all_s[7 * rank : 10 * rank, at]
    all_s[0 : 5 * rank] = early_ref[...]
    all_s[4 * rank + 1 : 4 * rank + 2] = magd_ref[0:1]
    all_s[5 * rank : 7 * rank] = both_ref[...] * (1.0 / (2 * Z))
    all_s[10 * rank :] = jnp.zeros((n - 10 * rank, width), F32)

    def go(k, d, src, dst, where):
        return send(src, dst, ss.at[k, d], rs.at[k, d], where)

    first = [go(0, 0, all_s.at[ds(1 - core, nc)], c_r, device(dc=1))]
    slots = []
    for d in NEAR_LAST:
        slots.append(go(1, d, block_ref.at[X - d], bx_r.at[d - 1], device(dx=d)))
        slots.append(go(2, d, lower_ref.at[X - d], lx_r.at[d - 1], device(dx=d)))
    for u in range(2):
        for k in range(2):
            for side, d in enumerate((1, 3)):
                one[k, u, side].wait_recv()
                other = pl.ds(side * mid, mid)
                near[k, u, side, side * mid : (side + 1) * mid] = (
                    held[k, u, side] + hop[k, u, side].astype(F32)
                ).astype(BF16)
                one[k, u, 4 + side] = send(
                    near.at[k, u, side, other], came.at[k, u, side, other],
                    s_one.at[k, u, 4 + side], r_one.at[k, u, 4 + side], to(k, d),
                )
    done(first)
    z_s[...] = all_s[ds(core, nc)] + c_r[...]
    z_b[...] = z_s[...].astype(BF16)
    zc = [
        go(3, d, z_b.at[:, ds((z + d) % Z, wz)], z_r.at[d - 1], device(dz=d)) for d in NEAR_LAST
    ]
    done(slots)
    b_one[...] = block_ref[0] + (bx_r[0] + bx_r[1] + bx_r[2])
    e_one[:rank] = lower_ref[0] + (lx_r[0] + lx_r[1] + lx_r[2])
    cc = [go(4, 0, b_one, b_two, device(dc=1)), go(5, 0, e_one, e_two, device(dc=1))]
    seconds = [[], []]
    for u in range(2):
        for k in range(2):
            for index in range(2):
                one[k, u, index].wait_send()
            for index in (2, 3, 4, 5):
                one[k, u, index].wait()
        for k in range(2):
            for d in (2, 1, 3, 0):
                at = slice(d * sub, (d + 1) * sub)
                part = acc[k, u, at] + (
                    came[k, u, 0, at].astype(F32) + came[k, u, 1, at].astype(F32)
                )
                if d:
                    send_2[u, k, d - 1] = part.astype(BF16)
                    seconds[u].append(
                        send(
                            send_2.at[u, k, d - 1], recv_2.at[u, k, d - 1], s_two.at[u, k, d - 1],
                            r_two.at[u, k, d - 1], to(1 - k, d),
                        )
                    )
                else:
                    d_one[u, :, k * half : (k + 1) * half] = part
    done(cc)
    b_two[...] += b_one[...]
    e_two[...] += e_one[...]
    done(zc)
    x_s[...] = z_s[:, ds(z, wz)] + (
        z_r[0].astype(F32) + z_r[1].astype(F32) + z_r[2].astype(F32)
    )
    cz = []
    b_z[z] = b_two[...]
    e_z[z] = e_two[...]
    for d in NEAR_LAST:
        cz.append(go(6, d, b_two, b_z.at[z], device(dz=d)))
        cz.append(go(7, d, e_two, e_z.at[z], device(dz=d)))
    xc = [go(8, d, x_s.at[:, ds((x + d) % X, wx)], x_r.at[d - 1], device(dx=d)) for d in NEAR_LAST]
    left, right = pl.ds(0, half), pl.ds(half, half)
    load_hid.wait()
    gat = [[], []]
    for u in range(2):
        done(seconds[u])
        for k in range(2):
            d_one[u, :, k * half : (k + 1) * half] += (
                recv_2[u, k, 0].astype(F32)
                + recv_2[u, k, 1].astype(F32)
                + recv_2[u, k, 2].astype(F32)
            )
        own = slice(u * sub, (u + 1) * sub)
        inputs = hid_ref[own].astype(F32)
        inverse = lax.rsqrt(jnp.mean(inputs * inputs, axis=1, keepdims=True) + epsilon)
        scaled = d_one[u] * gain_ref[...]
        result = dres_ref[own] + (
            inverse * scaled
            - inputs
            * (inverse * inverse * inverse)
            * jnp.mean(inputs * scaled, axis=1, keepdims=True)
        )
        spread[x, y, own] = result.astype(BF16)
        for d in NEAR_LAST:
            for k, side in enumerate((left, right)):
                at = spread.at[x, y, pl.ds(u * sub, sub), side]
                gat[u].append(
                    send(at, at, s_gat.at[u, k, d - 1], r_gat.at[u, k, d - 1], to(k, d))
                )
        if u == 0:
            done(xc)
            y_v[y] = x_s[:, ds(x, wx)] + (x_r[0] + x_r[1] + x_r[2])
            yc = [go(9, d, y_v.at[y], y_v.at[y], device(dy=d)) for d in NEAR_LAST]
    done(yc)
    mine = ds(core, nc)
    at_x = ds(z * X + x, wx)
    gath[mine, at_x] = (((y_v[0] + y_v[1]) + y_v[2]) + y_v[3]).astype(BF16)
    sx = [go(10, d, gath.at[mine, at_x], gath.at[mine, at_x], device(dx=d)) for d in NEAR_LAST]

    def part_of(k, u, d, first, count):
        tokens = pl.ds(u * sub, sub)
        if k:
            return spread.at[(x + d) % X, pl.ds(first, count), tokens, right]
        return spread.at[pl.ds(first, count), (y + d) % Y, tokens, left]

    last = {}
    for u in range(2):
        done(gat[u])
        for k in range(2):
            for side, d in enumerate((1, 3)):
                at = part_of(k, u, 0, 0, 4)
                last[k, u, side] = send(
                    at, at, s_gat.at[u, 2 + k, side], r_gat.at[u, 2 + k, side], to(1 - k, d)
                )
    done(sx)
    spot = gath.at[mine, ds(z, wz)]
    sz = [go(11, d, spot, spot, device(dz=d)) for d in NEAR_LAST]
    done(cz)
    block_out[...] = ((b_z[0] + b_z[1]) + b_z[2]) + b_z[3]
    ctx_out[...] = ((e_z[0] + e_z[1]) + e_z[2]) + e_z[3]
    done(sz)
    spot = gath.at[mine]
    sc = go(12, 0, spot, spot, device(dc=1))
    for u in range(2):
        for k in range(2):
            for side, d in enumerate((1, 3)):
                last[k, u, side].wait_recv()
                at = part_of(k, u, 4 - d, 2 * side, 2)
                last[k, u, 2 + side] = send(
                    at, at, s_gat.at[u, 4 + k, side], r_gat.at[u, 4 + k, side], to(1 - k, d)
                )
    for u in range(2):
        for k in range(2):
            for side in range(2):
                last[k, u, side].wait_send()
                last[k, u, 2 + side].wait()
    out = keep(spread, grad_out, local.at[1])
    sc.wait()
    all_out[...] = gath[...]
    out.wait()


def tail(
    grads, weight, hidden, gain, d_resid, pre, thr, n1, inner, cola, maga, uppera, early, both,
    block, lower, magd,
):
    rows, here, deep = grads.shape
    piece, width = d_resid.shape
    half = width // 2
    mid = here // 4
    sub = piece // 2
    _, bn, bw = block.shape
    n = 192
    en = 72
    nc = n // 2
    wz, wx = width // Z, width // Z // X
    s = jax.ShapeDtypeStruct
    v = pltpu.VMEM
    return call(
        tail_kernel,
        (s((rows, Y, piece, width), BF16), s((n, width), BF16), s((bn, bw), F32), s((en, HD), F32)),
        [VM] * 2 + [ANY] + [VM] * 4 + [ANY] + [VM] * 9,
        (ANY, VM, VM, VM),
        [
            v((X, Y, piece, deep), BF16),
            v((2, 2, 2 * mid, half), BF16),
            v((2, 2, 2, 2 * mid, half), BF16),
            v((2, 2, 2, mid, half), F32),
            v((2, 2, 2, mid, half), BF16),
            v((2, 2, 2, 2 * mid, half), BF16),
            v((2, 2, 2 * mid, half), F32),
            v((2, 2, 3, sub, half), BF16),
            v((2, 2, 3, sub, half), BF16),
            v((2, sub, width), F32),
            v((X, Y, piece, width), BF16),
            v((rows, here, width), BF16),
            v((rows * here, 48), BF16),
            v((n, width), F32),
            v((piece, width), BF16),
            v((n, width), BF16),
            v((nc, width), F32),
            v((nc, width), F32),
            v((nc, width), BF16),
            v((3, nc, wz), BF16),
            v((nc, wz), F32),
            v((3, nc, wx), F32),
            v((Y, nc, wx), F32),
            v((3, bn, bw), F32),
            v((3, 16, HD), F32),
            v((bn, bw), F32),
            v((bn, bw), F32),
            v((en, HD), F32),
            v((en, HD), F32),
            v((Z, en, HD), F32),
            v((Z, bn, bw), F32),
            dma(2, 2, 6), dma(2, 2, 6), dma(2, 2, 3), dma(2, 2, 3), dma(2, 6, 3), dma(2, 6, 3),
            dma(13, 4), dma(13, 4), dma(3),
        ],
        3,
        2 * rows * here * deep * width,
        16 * 2**20,
    )(
        grads, weight, hidden, gain, d_resid, pre, thr, n1, inner, cola, maga, uppera, early, both,
        block, lower, magd,
    )


def widen_kernel(a_ref, b_ref, wide_out, same_out, narrow, wide, passed, loads, stores):
    rows = a_ref.shape[0]
    copies = [keep(a_ref.at[r], narrow.at[r], loads.at[0, r]) for r in range(rows)]
    others = [keep(b_ref.at[r], passed.at[r], loads.at[1, r]) for r in range(rows)]
    outs = []
    for r in range(rows):
        copies[r].wait()
        wide[r] = narrow[r].astype(F32)
        outs.append(keep(wide.at[r], wide_out.at[r], stores.at[0, r]))
    for r in range(rows):
        others[r].wait()
        outs.append(keep(passed.at[r], same_out.at[r], stores.at[1, r]))
    for copy in outs:
        copy.wait()


def widen(a, b):
    parts = 16
    many, width = a.shape[0] * a.shape[1] * a.shape[2] // parts, a.shape[3]
    wide, same = pl.pallas_call(
        widen_kernel,
        out_shape=(
            jax.ShapeDtypeStruct((parts, many, width), F32),
            jax.ShapeDtypeStruct((parts, many, width), BF16),
        ),
        in_specs=[ANY, ANY],
        out_specs=(ANY, ANY),
        scratch_shapes=[
            pltpu.VMEM((parts, many, width), BF16),
            pltpu.VMEM((parts, many, width), F32),
            pltpu.VMEM((parts, many, width), BF16),
            dma(2, parts), dma(2, parts),
        ],
        compiler_params=pltpu.CompilerParams(vmem_limit_bytes=58 * 2**20),
    )(a.reshape(parts, many, width), b.reshape(parts, many, width))
    return wide.reshape(b.shape), same.reshape(b.shape)


def on_device(
    hidden,
    segments,
    key_attendable,
    attention_gain,
    feedforward_gain,
    attend_frozen,
    output_frozen,
    expand_frozen,
    reduce_frozen,
    attend_lower,
    attend_upper,
    attend_magnitude,
    output_lower,
    output_upper,
    output_magnitude,
    expand_lower,
    expand_upper,
    expand_magnitude,
    reduce_lower,
    reduce_upper,
    reduce_magnitude,
    cotangent,
):
    rows, here, width = hidden.shape
    length = segments.shape[1]
    ff = reduce_frozen.shape[0]
    rank = output_lower.shape[1]
    ctx = lax.axis_index("ctx")
    offset = ctx * here

    def left_factor(a):
        high, low = halves(a)
        return jnp.concatenate([high, high, low], axis=-1)

    def right_factor(a):
        high, low = halves(a)
        return jnp.concatenate([high, low, high], axis=-2)

    expand_upper_t = expand_upper.transpose(0, 2, 1)
    aw = left_factor(
        jnp.concatenate([output_lower, expand_upper_t[0], expand_upper_t[1], reduce_lower], axis=0)
    )
    bw = right_factor(
        jnp.stack([output_upper, expand_lower[0].T, expand_lower[1].T, reduce_upper], axis=0)
    )
    la = left_factor(attend_lower)
    ua = right_factor(attend_upper)
    flat_lower = attend_lower.transpose(1, 0, 2).reshape(width, 3 * rank)
    high, low = halves(flat_lower)
    thin = jnp.concatenate([high, low, jnp.zeros((width, HD - 6 * rank), BF16)], axis=1)
    flat_lower = expand_lower.transpose(1, 0, 2).reshape(width, 2 * rank)
    high, low = halves(flat_lower)
    el = jnp.concatenate([high, low, jnp.zeros((width, HD - 4 * rank), BF16)], axis=1)
    small = jnp.concatenate([expand_upper_t[0], expand_upper_t[1], reduce_lower], axis=1)
    small = jnp.concatenate(
        [
            jnp.pad(small, ((0, 0), (0, HD - 3 * rank))),
            jnp.pad(output_lower, ((0, 0), (0, HD - rank))),
        ],
        axis=0,
    )
    mago = jnp.stack([output_magnitude, reduce_magnitude])
    upper = jnp.concatenate([output_upper, reduce_upper], axis=0)

    levels = jnp.arange(SEGS, dtype=jnp.int32)
    below_count = jnp.sum((segments[:, None, :] < levels[None, :, None]).astype(F32), axis=2)
    segments_here = lax.dynamic_slice_in_dim(segments, offset, here, 1)
    begin_here = jnp.sum(
        (segments_here[:, :, None] == levels[None, None, :]).astype(F32) * below_count[:, None, :],
        axis=2,
    )
    spot_here = offset + jnp.arange(here, dtype=jnp.int32)
    places = spot_here.astype(F32)[None, :] - begin_here
    frequency = rotary_base ** (-(2.0 * jnp.arange(HD // 2).astype(F32)) / HD)
    frequency = jnp.concatenate([frequency, frequency])
    angles = places[:, :, None] * frequency[None, None, :]
    cosine, sine_part = jnp.cos(angles), jnp.sin(angles)
    spots = jnp.arange(length, dtype=jnp.int32)[None]
    key_tag = jnp.where(key_attendable == 1, spots, -1)[:, None, :]
    begin = begin_here.astype(jnp.int32)[:, :, None]
    gain_one = attention_gain.astype(F32)
    gain_two = feedforward_gain.astype(F32)

    (
        mixed_parts,
        soft,
        log_total,
        all_pairs,
        weights_x,
        weight_attend,
        queries,
        pre,
        through_three,
        column_attend,
        column_expand,
        squares,
        inner_attend,
        inner_expand,
        inner_both,
        normed_one,
        small_own,
    ) = front(
        hidden,
        gain_one[None],
        attend_frozen,
        la,
        ua,
        attend_magnitude,
        thin,
        output_frozen,
        expand_frozen.transpose(0, 2, 1),
        reduce_frozen,
        aw,
        bw,
        expand_magnitude.reshape(2 * ff, 1),
        mago,
        el,
        small,
        cosine,
        sine_part,
        begin,
        key_tag,
    )
    d_resid, resid, ff_own, ff_send, d_mixed_parts, early, block_x, lower_out = feed(
        mixed_parts, hidden, gain_two[None], cotangent, weights_x, small_own, el, upper, mago, squares
    )
    grads_low, block_output, mag_down = attend_back(
        queries,
        all_pairs,
        d_mixed_parts,
        soft,
        log_total,
        begin,
        key_tag,
        cosine,
        sine_part,
        resid,
        ff_own,
        ff_send,
        cotangent,
    )
    hidden_grad, everywhere, block_x, small_ctx = tail(
        grads_low,
        weight_attend,
        hidden,
        gain_one[None],
        d_resid,
        pre,
        through_three,
        normed_one,
        inner_attend,
        column_attend,
        attend_magnitude,
        attend_upper,
        early,
        inner_both,
        block_x,
        lower_out,
        mag_down,
    )
    hidden_grad, block_output = widen(hidden_grad, block_output)
    everywhere = everywhere.astype(F32)
    lower_out, local = small_ctx[:rank], small_ctx[rank:]
    late = adapter_scale * everywhere[7 * rank : 10 * rank]
    early = everywhere[: 7 * rank]

    attend_lower_grad = late.reshape(3, rank, width).transpose(0, 2, 1)
    attend_upper_grad = local[: 3 * rank].reshape(3, rank, HD)
    attend_magnitude_grad = local[3 * rank : 3 * rank + 3]
    column_expand = column_expand.reshape(2, ff)
    inner_expand = inner_expand.reshape(2, ff, HD)
    inner_expand = inner_expand[..., : 2 * rank] + inner_expand[..., 2 * rank : 4 * rank]
    expand_magnitude_grad = block_x[3 * rank : 3 * rank + 2] / expand_magnitude
    pull_expand = expand_magnitude * expand_magnitude_grad / column_expand**2
    ratio_expand = expand_magnitude / column_expand
    expand_upper_grad = jnp.stack(
        [
            adapter_scale
            * (
                block_x[m * rank : (m + 1) * rank] * ratio_expand[m]
                - inner_expand[m, :, m * rank : (m + 1) * rank].T * pull_expand[m]
            )
            for m in range(2)
        ]
    )
    expand_lower_grad = adapter_scale * early[: 2 * rank].reshape(2, rank, width).transpose(0, 2, 1)
    columns = jnp.sqrt(squares)
    magnitude_grads = early[4 * rank : 4 * rank + 2] / mago
    pulls = mago * magnitude_grads / squares
    ratios = mago / columns
    output_magnitude_grad = magnitude_grads[0]
    reduce_magnitude_grad = magnitude_grads[1]
    output_upper_grad = adapter_scale * (
        early[2 * rank : 3 * rank] * ratios[0] - early[5 * rank : 6 * rank] * pulls[0]
    )
    reduce_upper_grad = adapter_scale * (
        early[3 * rank : 4 * rank] * ratios[1] - early[6 * rank : 7 * rank] * pulls[1]
    )

    def pulled_rows(frozen, lower, upper, pull):
        pulled = upper * pull
        rows_part = exact_dot(frozen, pulled, ((1,), (1,)))
        return rows_part + adapter_scale * jnp.dot(
            lower,
            jnp.dot(upper, pulled.T, precision=lax.Precision.HIGHEST),
            precision=lax.Precision.HIGHEST,
        )

    output_lower_grad = adapter_scale * (
        lower_out.T - pulled_rows(output_frozen, output_lower, output_upper, pulls[0])
    )
    reduce_lower_grad = adapter_scale * (
        block_x[2 * rank : 3 * rank].T
        - pulled_rows(reduce_frozen, reduce_lower, reduce_upper, pulls[1])
    )
    return (
        block_output,
        hidden_grad,
        attend_lower_grad,
        attend_upper_grad,
        attend_magnitude_grad,
        output_lower_grad,
        output_upper_grad,
        output_magnitude_grad,
        expand_lower_grad,
        expand_upper_grad,
        expand_magnitude_grad,
        reduce_lower_grad,
        reduce_upper_grad,
        reduce_magnitude_grad,
    )


def solution(mesh):
    placed = (
        P(None, "ctx", None),
        P(),
        P(),
        P(),
        P(),
        P(None, None, "tp"),
        P("tp", None),
        P(None, None, "tp"),
        P("tp", None),
        P(),
        P(None, None, "tp"),
        P(None, "tp"),
        P("tp", None),
        P(),
        P(),
        P(),
        P(None, None, "tp"),
        P(None, "tp"),
        P("tp", None),
        P(),
        P(),
        P(None, "ctx", None),
    )
    return jax.shard_map(
        on_device,
        mesh=mesh,
        in_specs=placed,
        out_specs=(
            P(None, "ctx", None),
            P(None, "ctx", None),
            P(),
            P(None, None, "tp"),
            P(None, "tp"),
            P("tp", None),
            P(),
            P(),
            P(),
            P(None, None, "tp"),
            P(None, "tp"),
            P("tp", None),
            P(),
            P(),
        ),
        check_vma=False,
    )
```

```python
import jax
import jax.numpy as jnp
from jax import lax
from jax.experimental import pallas as pl
from jax.experimental.pallas import tpu as pltpu
from jax.sharding import PartitionSpec as P

HD = 128
SEGS = 4
X = 4
Y = 4
Z = 4

epsilon = 1e-05
adapter_scale = 2.0
rotary_base = 10000.0
F32 = jnp.float32
BF16 = jnp.bfloat16


def halves(a):
    high = lax.reduce_precision(a, 8, 7)
    return high.astype(BF16), (a - high).astype(BF16)


def dot32(a, b, dims):
    return lax.dot_general(a, b, (dims, ((), ())), preferred_element_type=F32)


def exact_dot(bf, full, dims):
    high, low = halves(full)
    return dot32(bf, high, dims) + dot32(bf, low, dims)


def rotate(tensor, cosine, sine_part):
    half_width = tensor.shape[-1] // 2
    turned = jnp.concatenate([-tensor[..., half_width:], tensor[..., :half_width]], axis=-1)
    return tensor * cosine + turned * sine_part


MESH = pl.DeviceIdType.MESH
ANY = pl.BlockSpec(memory_space=pl.ANY)
VM = pl.BlockSpec(memory_space=pltpu.VMEM)
NEAR_LAST = (2, 1, 3)


def place():
    ctx = lax.axis_index("ctx")
    tp = lax.axis_index("tp")
    return ctx // 2, ctx % 2, tp // X, tp % X


def device(dz=0, dc=0, dy=0, dx=0):
    z, core, y, x = place()
    return (((z + dz) % Z) * 2 + (core + dc) % 2, ((y + dy) % Y) * X + (x + dx) % X)


def greet(devices):
    barrier = pltpu.get_barrier_semaphore()
    for d in devices:
        pl.semaphore_signal(barrier, inc=1, device_id=d, device_id_type=MESH)
    pl.semaphore_wait(barrier, len(devices))


def send(src, dst, send_sem, recv_sem, to):
    copy = pltpu.make_async_remote_copy(
        src_ref=src,
        dst_ref=dst,
        send_sem=send_sem,
        recv_sem=recv_sem,
        device_id=to,
        device_id_type=MESH,
    )
    copy.start()
    return copy


def keep(src, dst, sem):
    copy = pltpu.make_async_copy(src, dst, sem)
    copy.start()
    return copy


def dma(*shape):
    return pltpu.SemaphoreType.DMA(shape)


def call(kernel, outs, in_specs, out_specs, scratch, number, flops, moved):
    return pl.pallas_call(
        kernel,
        out_shape=outs,
        in_specs=in_specs,
        out_specs=out_specs,
        scratch_shapes=scratch,
        cost_estimate=pl.CostEstimate(flops=flops, bytes_accessed=moved, transcendentals=0),
        compiler_params=pltpu.CompilerParams(
            collective_id=number, has_side_effects=True, vmem_limit_bytes=58 * 2**20
        ),
    )


def mask_of(begin, spot_q, key_tag, key_spot):
    return ((key_tag >= begin) & (key_tag <= spot_q)) | (key_spot == spot_q)


KB = 512


def tiles(total, size):
    return [(s, min(size, total - s)) for s in range(0, total, size)]


PIECES = 3


def relay_plan(weights, send_a, recv_a, send_b, recv_b, send_s, recv_s, cols):
    def begin(p, own, start, size):
        return [
            send(own, weights(1, start, size), send_a.at[p, 0], recv_a.at[p, 0], device(dx=1)),
            send(own, weights(3, start, size), send_a.at[p, 1], recv_a.at[p, 1], device(dx=3)),
        ]

    def relay(p, copies, start, size):
        half = size // 2
        more = []
        for k, (slot, at, to) in enumerate(((1, start, 1), (3, start + half, 3))):
            copies[k].wait_recv()
            more.append(
                send(
                    weights(slot, at, half), weights(2, at, half),
                    send_b.at[p, k], recv_b.at[p, k], device(dx=to),
                )
            )
            there = weights(slot, start, size)
            more.append(send(there, there, send_s.at[p, k], recv_s.at[p, k], device(dc=1)))
        return more

    def relay_far(p, more, start, size):
        more[0].wait_recv()
        more[2].wait_recv()
        there = weights(2, start, size)
        return send(there, there, send_s.at[p, 2], recv_s.at[p, 2], device(dc=1))

    def finish(copies, more, last):
        more[1].wait_recv()
        more[3].wait_recv()
        last.wait_recv()
        for copy in copies + more + [last]:
            copy.wait_send()

    return begin, relay, relay_far, finish


def front_kernel(
    hid_ref, gain_ref, fa_ref, la_ref, ua_ref, maga_ref, thin_ref, fo_ref, fe_ref, fr_ref, aw_ref, bw_ref,
    mage_ref, mago_ref, el_ref, small_ref, cos_ref, sin_ref, begin_ref, tag_ref,
    mixed_out, soft_out, log_out, kv_out, weights_out, wq_out, q_out, pre_out, thr_out,
    cola_out, cole_out, sq_out, ina_out, ine_out, ino_out, n1_out, small,
    kv_all, score, soft, logs, mixed, mixed_x, joined, w_own, wq_all, normed, kv_own,
    sq_x, sq_y, sq_one, ja,
    kv_send, kv_recv, sib_send, sib_recv, a_send, a_recv, b_send, b_recv, ws_send, ws_recv,
    wz_send, wz_recv, wo_send, wo_recv, m_send, m_recv, sq_send, sq_recv, local, n_local,
):
    z, core, y, x = place()
    me = z * 2 + core
    rows, here, width = hid_ref.shape
    length = Z * 2 * here
    ff = fr_ref.shape[0]
    piece = here // Y
    step = width // 16
    odd = z % 2
    xcols = pl.ds(pl.multiple_of((core * 8 + odd * 3) * step, step), 5 * step)
    zmine = pl.ds(pl.multiple_of((core * 8 + odd * 5) * step, step), 3 * step)
    zother = pl.ds(pl.multiple_of((core * 8 + (1 - odd) * 5) * step, step), 3 * step)
    greet(
        [device(dx=d) for d in (1, 2, 3)]
        + [device(dy=d) for d in (1, 2, 3)]
        + [device(dz=d) for d in (1, 2, 3)]
        + [device(dc=1)]
    )

    def join(matrix, start, size, at):
        low = dot32(aw_ref[start : start + size], bw_ref[matrix, :, at], ((1,), (0,)))
        if matrix in (1, 2):
            frozen = fe_ref[matrix - 1, :, at]
        else:
            frozen = fr_ref[:, at] if matrix else fo_ref[:, at]
        return frozen.astype(F32) + adapter_scale * low

    for s, size in tiles(width, 512):
        at = slice(s, s + size)
        one = join(0, 0, HD, at)
        two = join(3, HD + 2 * ff, ff, at)
        sq_one[0:1, at] = jnp.sum(one * one, axis=0, keepdims=True)
        sq_one[1:2, at] = jnp.sum(two * two, axis=0, keepdims=True)
    sq_copies = [
        send(sq_one, sq_x.at[d - 1], sq_send.at[0, d - 1], sq_recv.at[0, d - 1], device(dx=d))
        for d in NEAR_LAST
    ]

    where = ((HD, ff), (HD + ff, ff), (0, HD))
    moves = [{}, {}, {}]

    def there(slot, start, size, cols):
        return weights_out.at[slot, pl.ds(start, size), cols]

    def begin(p):
        start, size = where[p]
        for k, (slot, d) in enumerate(((1, 1), (3, 3))):
            moves[p]["a", k] = send(
                w_own.at[pl.ds(start, size), xcols], there(slot, start, size, xcols),
                a_send.at[p, k], a_recv.at[p, k], device(dx=d),
            )

    def share(p, slot):
        start, size = where[p]
        half = size // 2
        at = there(slot, start, size, xcols)
        moves[p]["s", slot] = send(
            at, at, ws_send.at[p, slot - 1], ws_recv.at[p, slot - 1], device(dc=1)
        )
        for k, (first, d) in enumerate(((start, 1), (start + half, 3))):
            at = there(slot, first, half, zmine)
            moves[p]["z", slot, k] = send(
                at, at, wz_send.at[p, slot - 1, k], wz_recv.at[p, slot - 1, k], device(dz=d)
            )

    def relay(p):
        start, size = where[p]
        half = size // 2
        for k, (slot, first) in enumerate(((1, start), (3, start + half))):
            moves[p]["a", k].wait_recv()
            moves[p]["b", k] = send(
                there(slot, first, half, xcols), there(2, first, half, xcols),
                b_send.at[p, k], b_recv.at[p, k], device(dx=slot),
            )
            share(p, slot)

    def relay_far(p):
        moves[p]["b", 0].wait_recv()
        moves[p]["b", 1].wait_recv()
        share(p, 2)

    def relay_z(p, slot):
        start, size = where[p]
        moves[p]["z", slot, 0].wait_recv()
        moves[p]["z", slot, 1].wait_recv()
        at = there(slot, start, size, zother)
        moves[p]["o", slot] = send(
            at, at, wo_send.at[p, slot - 1], wo_recv.at[p, slot - 1], device(dc=1)
        )

    def finish(p):
        for slot in (1, 2, 3):
            moves[p]["s", slot].wait_recv()
            moves[p]["o", slot].wait_recv()
        for copy in moves[p].values():
            copy.wait_send()

    for m in range(2):
        start = HD + m * ff
        total = jnp.zeros((ff, 1), F32)
        for s, size in tiles(width, 512):
            at = slice(s, s + size)
            value = join(1 + m, start, ff, at)
            joined[:, at] = value
            total = total + jnp.sum(value * value, axis=1, keepdims=True)
        column = jnp.sqrt(total)
        cole_out[m * ff : (m + 1) * ff] = column
        magnitude = mage_ref[m * ff : (m + 1) * ff]
        ratio = magnitude / column
        for s, size in tiles(width, 512):
            at = slice(s, s + size)
            w_own[start : start + ff, at] = (joined[:, at] * ratio).astype(BF16)
        begin(m)
        inner = dot32(w_own[start : start + ff], el_ref[...], ((1,), (0,)))
        ine_out[m * ff : (m + 1) * ff] = inner / ratio
        source = small_ref[0:ff, m * 16 : (m + 1) * 16]
        small[0:ff, m * 16 : (m + 1) * 16] = (source * ratio).astype(BF16)
        small[0:ff, (3 + m) * 16 : (4 + m) * 16] = (source / (magnitude * column)).astype(BF16)
    small[0:ff, 32:48] = small_ref[0:ff, 32:48].astype(BF16)
    small[0:ff, 80:] = jnp.zeros((ff, HD - 80), BF16)
    small[ff:] = small_ref[ff:].astype(BF16)
    own = []
    for copy in sq_copies:
        copy.wait()
    sq_one[...] += sq_x[0] + sq_x[1] + sq_x[2]
    sq_copies = [
        send(sq_one, sq_y.at[d - 1], sq_send.at[1, d - 1], sq_recv.at[1, d - 1], device(dy=d))
        for d in NEAR_LAST
    ]
    for m in range(3):
        total = jnp.zeros((1, HD), F32)
        for s, size in tiles(width, 512):
            at = slice(s, s + size)
            value = fa_ref[m, at].astype(F32) + adapter_scale * dot32(
                la_ref[m, at], ua_ref[m], ((1,), (0,))
            )
            ja[at] = value
            total = total + jnp.sum(value * value, axis=0, keepdims=True)
        column = jnp.sqrt(total)
        cola_out[m : m + 1] = column
        ratio = maga_ref[m : m + 1] / column
        wq_all[:, m * HD : (m + 1) * HD] = (ja[...] * ratio).astype(BF16)
        inner = dot32(la_ref[m], ja[...].astype(BF16), ((0,), (0,)))
        ina_out[m] = inner[0:16] + inner[32:48]
    own.append(keep(wq_all, wq_out, local.at[1]))
    kv_copies, sib_copies, n_copies = {}, [], []
    gain = gain_ref[...]
    for r in range(rows):
        inputs = hid_ref[r].astype(F32)
        inverse = lax.rsqrt(jnp.mean(inputs * inputs, axis=1, keepdims=True) + epsilon)
        if r >= 2:
            n_copies[r - 2].wait()
        normed[r % 2] = (inputs * inverse * gain).astype(BF16)
        n_copies.append(keep(normed.at[r % 2], n1_out.at[r], n_local.at[r]))
        pre = dot32(normed[r % 2], wq_all[...], ((1,), (0,)))
        pre_out[r] = pre
        thin = dot32(normed[r % 2], thin_ref[...], ((1,), (0,)))
        thr_out[r] = thin
        cosine, sine = cos_ref[r], sin_ref[r]
        q_out[r] = rotate(pre[:, :HD], cosine, sine).astype(BF16)
        kv_own[r, :, :HD] = rotate(pre[:, HD : 2 * HD], cosine, sine).astype(BF16)
        kv_own[r, :, HD:] = pre[:, 2 * HD :].astype(BF16)
        for k, d in enumerate((1, 3)):
            kv_copies[r, k] = send(
                kv_own.at[r], kv_all.at[me, r], kv_send.at[r, k], kv_recv.at[r, k], device(dz=d)
            )
        sib_copies.append(
            send(kv_own.at[r], kv_all.at[me, r], sib_send.at[r, 0], sib_recv.at[r, 0], device(dc=1))
        )
    own.append(keep(kv_own, kv_all.at[me], local.at[2]))
    for copy in sq_copies:
        copy.wait()
    squares = sq_one[...] + (sq_y[0] + sq_y[1] + sq_y[2])
    sq_out[...] = squares
    ratios = mago_ref[...] / jnp.sqrt(squares)
    for s, size in tiles(width, 512):
        at = slice(s, s + size)
        one = join(0, 0, HD, at)
        two = join(3, HD + 2 * ff, ff, at)
        w_own[0:HD, at] = (one * ratios[0:1, at]).astype(BF16)
        w_own[HD + 2 * ff :, at] = (two * ratios[1:2, at]).astype(BF16)
        ino_out[0:16, at] = dot32(small[ff:], one.astype(BF16), ((0,), (0,)))[0:16]
        ino_out[16:32, at] = dot32(small[0:ff], two.astype(BF16), ((0,), (0,)))[32:48]
    begin(2)
    own.append(keep(w_own, weights_out.at[0], local.at[3]))

    def pass_kv(r):
        for k, d in enumerate((1, 3)):
            kv_copies[r, k].wait_recv()
            at = kv_all.at[((z + Z - d) % Z) * 2 + core, r]
            if (k == 0) == (r < rows // 2):
                kv_copies[r, 2] = send(at, at, kv_send.at[r, 2], kv_recv.at[r, 2], device(dz=d))
            sib_copies.append(
                send(at, at, sib_send.at[r, 1 + k], sib_recv.at[r, 1 + k], device(dc=1))
            )

    def pass_far(r):
        kv_copies[r, 2].wait_recv()
        at = kv_all.at[((z + 2) % Z) * 2 + core, r]
        sib_copies.append(send(at, at, sib_send.at[r, 3], sib_recv.at[r, 3], device(dc=1)))

    for r in range(rows):
        pass_kv(r)
    relay(0)
    for r in range(rows):
        pass_far(r)
    relay(1)
    own[1].wait()
    for copy in sib_copies:
        copy.wait_recv()
    own.append(keep(kv_all, kv_out, local.at[4]))
    spot_q = lax.broadcasted_iota(jnp.int32, (here, 1), 0) + me * here
    m_copies = []
    for i in (2, 1, 3, 0):
        row = (x + i) % X
        query = q_out[row]
        first = begin_ref[row]
        peak = jnp.full((here, 1), -1e30, F32)
        for b in range(length // KB):
            keys = jnp.concatenate(
                [kv_all[b * (KB // here) + k, row, :, :HD] for k in range(KB // here)], axis=0
            )
            raw = dot32(query, keys, ((1,), (1,))) * (HD**-0.5)
            key_spot = lax.broadcasted_iota(jnp.int32, (1, KB), 1) + b * KB
            ok = mask_of(first, spot_q, tag_ref[row, :, b * KB : (b + 1) * KB], key_spot)
            raw = jnp.where(ok, raw, -1e30)
            score[:, b * KB : (b + 1) * KB] = raw
            peak = jnp.maximum(peak, jnp.max(raw, axis=1, keepdims=True))
        total = jnp.zeros((here, 1), F32)
        gathered = jnp.zeros((here, HD), F32)
        for b in range(length // KB):
            power = jnp.exp(score[:, b * KB : (b + 1) * KB] - peak)
            total = total + jnp.sum(power, axis=1, keepdims=True)
            values = jnp.concatenate(
                [kv_all[b * (KB // here) + k, row, :, HD:] for k in range(KB // here)], axis=0
            )
            gathered = gathered + dot32(power.astype(BF16), values, ((1,), (0,)))
        soft[row] = gathered / total
        logs[row] = peak + jnp.log(total)
        for j in range(Y):
            mixed[i, j * piece : (j + 1) * piece] = soft[
                row, pl.ds(pl.multiple_of(((y + j) % Y) * piece, piece), piece)
            ].astype(BF16)
        if i:
            m_copies.append(
                send(mixed.at[i], mixed_x.at[i], m_send.at[i - 1], m_recv.at[i - 1], device(dx=i))
            )
        else:
            mixed_x[0] = mixed[0]
        if i == 2:
            relay(2)
        if i == 1:
            relay_far(0)
            relay_z(0, 1)
            relay_z(0, 3)
        if i == 3:
            relay_far(1)
            relay_z(1, 1)
            relay_z(1, 3)
    own.append(keep(soft, soft_out, local.at[5]))
    own.append(keep(logs, log_out, local.at[6]))
    relay_far(2)
    relay_z(2, 1)
    relay_z(2, 3)
    for p in range(PIECES):
        relay_z(p, 2)
    for copy in m_copies:
        copy.wait()
    own.append(keep(mixed_x, mixed_out, local.at[7]))
    for copy in list(kv_copies.values()) + sib_copies:
        copy.wait_send()
    for p in range(PIECES):
        finish(p)
    for copy in n_copies[rows - 2 :]:
        copy.wait()
    own.pop(1)
    for copy in own:
        copy.wait()


def front(
    hidden, gain, fa, la, ua, maga, thin, fo, fe, fr, aw, bw, mage, mago, el, small, cos, sin,
    begin, tag,
):
    rows, here, width = hidden.shape
    ff = fr.shape[0]
    count = HD + 3 * ff
    length = 2 * Z * here
    s = jax.ShapeDtypeStruct
    return call(
        front_kernel,
        (
            s((X, here, HD), BF16),
            s((rows, here, HD), F32),
            s((rows, here, 1), F32),
            s((2 * Z, rows, here, 2 * HD), BF16),
            s((X, count, width), BF16),
            s((width, 3 * HD), BF16),
            s((rows, here, HD), BF16),
            s((rows, here, 3 * HD), F32),
            s((rows, here, HD), F32),
            s((3, HD), F32),
            s((2 * ff, 1), F32),
            s((2, width), F32),
            s((3, 16, HD), F32),
            s((2 * ff, HD), F32),
            s((32, width), F32),
            s((rows, here, width), BF16),
            s((ff + HD, HD), BF16),
        ),
        [VM] * 20,
        (ANY,) * 6 + (VM,) * 9 + (ANY, VM),
        [
            pltpu.VMEM((2 * Z, rows, here, 2 * HD), BF16),
            pltpu.VMEM((here, length), F32),
            pltpu.VMEM((rows, here, HD), F32),
            pltpu.VMEM((rows, here, 1), F32),
            pltpu.VMEM((X, here, HD), BF16),
            pltpu.VMEM((X, here, HD), BF16),
            pltpu.VMEM((ff, width), F32),
            pltpu.VMEM((count, width), BF16),
            pltpu.VMEM((width, 3 * HD), BF16),
            pltpu.VMEM((2, here, width), BF16),
            pltpu.VMEM((rows, here, 2 * HD), BF16),
            pltpu.VMEM((3, 2, width), F32),
            pltpu.VMEM((3, 2, width), F32),
            pltpu.VMEM((2, width), F32),
            pltpu.VMEM((width, HD), F32),
            dma(rows, 3), dma(rows, 3), dma(rows, 4), dma(rows, 4),
            dma(PIECES, 2), dma(PIECES, 2), dma(PIECES, 2), dma(PIECES, 2),
            dma(PIECES, 3), dma(PIECES, 3), dma(PIECES, 3, 2), dma(PIECES, 3, 2),
            dma(PIECES, 3), dma(PIECES, 3),
            dma(3), dma(3), dma(2, 3), dma(2, 3), dma(8), dma(rows),
        ],
        0,
        2 * 2 * rows * here * length * HD + 2 * rows * here * width * 4 * HD,
        32 * 2**20,
    )(
        hidden, gain, fa, la, ua, maga, thin, fo, fe, fr, aw, bw, mage, mago, el, small, cos, sin,
        begin, tag,
    )


def feed_kernel(
    mixed_ref, hidden_ref, gain_ref, cotangent_ref, weights_ref, small_ref, el_ref, upper_ref, mago_ref,
    sq_ref,
    resid_grad_out, resid_s, ff_own, ff_send, dmix_out, early_out, columns_out, lower_out,
    out_w, gate_w, up_w, down_w, normed, low, act, dgate, dup, far, near, held, hop, came, acc, mags,
    hid_ref, cot_ref, gate_s, up_s, dact_s,
    small_x, load, s_send, s_recv, local, sm_send, sm_recv, a_send, a_recv, b_send, b_recv, ws_send, ws_recv,
):
    z, core, y, x = place()
    width = hid_ref.shape[1]
    piece = hid_ref.shape[0]
    here = cot_ref.shape[0]
    ff = gate_w.shape[0] // X
    sub = piece // 2
    many = here // 2
    cols = pl.ds(pl.multiple_of(core * (width // 2), width // 2), width // 2)
    down_rows = pl.ds(HD + 2 * ff, ff)
    tokens = pl.ds(pl.multiple_of(y * piece, piece), piece)
    loads = [[], [], [], [], [keep(hidden_ref.at[x, tokens], hid_ref, local.at[0])]]
    for u in range(2):
        for j in range(Y):
            first = ((y + j) % Y) * piece + u * sub
            loads[4].append(
                keep(
                    cotangent_ref.at[x, pl.ds(pl.multiple_of(first, sub), sub)],
                    cot_ref.at[pl.ds(u * many + j * sub, sub)],
                    local.at[1 + u * Y + j],
                )
            )
    for w, (dst, start, size) in enumerate(((out_w, 0, HD), (gate_w, HD, ff), (up_w, HD + ff, ff))):
        for i in range(X):
            loads[w].append(
                keep(
                    weights_ref.at[i, pl.ds(start, size)], dst.at[pl.ds(i * size, size)],
                    load.at[w, i],
                )
            )
    loads[3].append(keep(weights_ref.at[0, down_rows], down_w.at[pl.ds(0, ff)], load.at[3, 0]))
    greet(
        [device(dy=d) for d in (1, 2, 3)] + [device(dx=1), device(dx=2), device(dx=3), device(dc=1)]
    )

    def there(slot, start, size):
        return down_w.at[pl.ds(slot * ff + start, size), cols]

    begin, relay, relay_far, finish = relay_plan(
        there, a_send, a_recv, b_send, b_recv, ws_send, ws_recv, cols
    )
    sent = begin(0, weights_ref.at[0, down_rows, cols], 0, ff)

    def loaded(w):
        for copy in loads[w]:
            copy.wait()

    half = width // 2
    cut_a, cut_b = pl.ds(0, half), pl.ds(half, half)
    moves = {}

    def put(k, u, part, start, size):
        at = slice(start, start + size)
        acc[k, u * sub : (u + 1) * sub, at] = part[0:sub]
        far[k, u, :, at] = part[2 * sub : 3 * sub].astype(BF16)
        for side, block in enumerate((1, 3)):
            value = part[block * sub : (block + 1) * sub]
            if (start < half) == (side == 1):
                near[k, u, side, :, at] = value.astype(BF16)
            else:
                inner = start % half
                held[k, u, side, :, inner : inner + size] = value

    def scatter_start(k, u):
        for side, (cut, d) in enumerate(((cut_a, 1), (cut_b, 3))):
            moves[k, u, side] = send(
                far.at[k, u, :, cut], hop.at[k, u, side], s_send.at[k, u, side],
                s_recv.at[k, u, side], device(dy=d),
            )
        for side, (cut, d) in enumerate(((cut_b, 1), (cut_a, 3))):
            moves[k, u, 2 + side] = send(
                near.at[k, u, side, :, cut], came.at[k, u, side, :, cut],
                s_send.at[k, u, 2 + side], s_recv.at[k, u, 2 + side], device(dy=d),
            )

    def scatter_relay(k, u):
        for side, (cut, d) in enumerate(((cut_a, 1), (cut_b, 3))):
            moves[k, u, side].wait_recv()
            near[k, u, side, :, side * half : (side + 1) * half] = (
                held[k, u, side] + hop[k, u, side].astype(F32)
            ).astype(BF16)
            moves[k, u, 4 + side] = send(
                near.at[k, u, side, :, cut], came.at[k, u, side, :, cut],
                s_send.at[k, u, 4 + side], s_recv.at[k, u, 4 + side], device(dy=d),
            )

    def scatter_sum(k, u):
        for index in range(2):
            moves[k, u, index].wait_send()
        for index in range(2, 6):
            moves[k, u, index].wait()
        return acc[k, u * sub : (u + 1) * sub] + (
            came[k, u, 0].astype(F32) + came[k, u, 1].astype(F32)
        )

    def block_at(buffer, u, block, cut=slice(None)):
        return buffer.at[pl.ds(u * many + block * sub, sub), cut]

    def gather_start(buffer, k, u):
        for side, (d, block) in enumerate(((1, 3), (3, 1))):
            moves[k, u, side] = send(
                block_at(buffer, u, 0), block_at(buffer, u, block), s_send.at[k, u, side],
                s_recv.at[k, u, side], device(dy=d),
            )

    def gather_relay(buffer, k, u):
        for side, (d, block, cut) in enumerate(((1, 3, cut_a), (3, 1, cut_b))):
            moves[k, u, side].wait_recv()
            moves[k, u, 2 + side] = send(
                block_at(buffer, u, block, cut), block_at(buffer, u, 2, cut),
                s_send.at[k, u, 2 + side], s_recv.at[k, u, 2 + side], device(dy=d),
            )

    def gather_wait(k, u):
        for side in range(2):
            moves[k, u, side].wait_send()
            moves[k, u, 2 + side].wait()

    loaded(0)
    mixed_cat = jnp.concatenate(
        [
            jnp.concatenate(
                [mixed_ref[i, b * piece + u * sub : b * piece + (u + 1) * sub] for i in range(X)],
                axis=1,
            )
            for u in range(2)
            for b in range(Y)
        ],
        axis=0,
    )
    for start, size in tiles(width, 512):
        at = slice(start, start + size)
        part = dot32(mixed_cat, out_w[:, at], ((1,), (0,)))
        for u in range(2):
            put(0, u, part[u * many : (u + 1) * many], start, size)
    for u in range(2):
        scatter_start(0, u)
    ratios = mago_ref[...] / jnp.sqrt(sq_ref[...])
    upper_o = (upper_ref[0:16] * ratios[0:1]).astype(BF16)
    upper_d = (upper_ref[16:32] * ratios[1:2]).astype(BF16)
    loaded(4)
    through_down = dot32(cot_ref[...], upper_d, ((1,), (1,))).astype(BF16)
    gain = gain_ref[...]
    for u in range(2):
        scatter_relay(0, u)
    for u in range(2):
        own = slice(u * sub, (u + 1) * sub)
        attended = scatter_sum(0, u)
        acc[0, own] = attended
        resid = hid_ref[own].astype(F32) + attended
        inverse = lax.rsqrt(jnp.mean(resid * resid, axis=1, keepdims=True) + epsilon)
        resid_s[own] = resid
        normed[u * many : u * many + sub] = (resid * inverse * gain).astype(BF16)
        gather_start(normed, 2, u)
        if u == 0:
            more = relay(0, sent, 0, ff)
            sm_copies = [
                send(small_ref, small_x.at[d], sm_send.at[d - 1], sm_recv.at[d - 1], device(dx=d))
                for d in NEAR_LAST
            ]
    loaded(1)
    loaded(2)
    loaded(3)
    for u in range(2):
        gather_relay(normed, 2, u)
    for u in range(2):
        rows = slice(u * many, (u + 1) * many)
        gather_wait(2, u)
        for start, size in tiles(X * ff, 256):
            at = slice(start, start + size)
            gate_s[:, at] = dot32(normed[rows], gate_w[at], ((1,), (1,)))
            up_s[:, at] = dot32(normed[rows], up_w[at], ((1,), (1,)))
        if u == 0:
            more_far = relay_far(0, more, 0, ff)
            finish(sent, more, more_far)
            for start, size in tiles(X * ff, 256):
                at = slice(start, start + size)
                dact_s[:, at] = dot32(cot_ref[...], down_w[at], ((1,), (1,)))
        else:
            scatter_relay(1, 0)
        for start, size in tiles(X * ff, 256):
            at = slice(start, start + size)
            gate, up, d_act = gate_s[:, at], up_s[:, at], dact_s[rows, at]
            sig = 1.0 / (1.0 + jnp.exp(-gate))
            gated = gate * sig
            act[rows, at] = (gated * up).astype(BF16)
            d_gate = (d_act * up * sig * (1.0 + gate * (1.0 - sig))).astype(BF16)
            d_up = (d_act * gated).astype(BF16)
            dgate[rows, at] = d_gate
            dup[rows, at] = d_up
            both = jnp.concatenate(
                [
                    jnp.sum(d_gate.astype(F32) * gate, axis=0, keepdims=True),
                    jnp.sum(d_up.astype(F32) * up, axis=0, keepdims=True),
                ],
                axis=0,
            )
            mags[:, at] = mags[:, at] + both if u else both
        for start, size in tiles(width, 512):
            at = slice(start, start + size)
            part = dot32(dgate[rows], gate_w[:, at], ((1,), (0,)))
            part = part + dot32(dup[rows], up_w[:, at], ((1,), (0,)))
            put(1, u, part, start, size)
        scatter_start(1, u)

    def residual(u):
        own = slice(u * sub, (u + 1) * sub)
        d_two = scatter_sum(1, u)
        resid = resid_s[own]
        inverse = lax.rsqrt(jnp.mean(resid * resid, axis=1, keepdims=True) + epsilon)
        scaled = d_two * gain
        mean = jnp.mean(resid * scaled, axis=1, keepdims=True)
        d_resid = cot_ref[u * many : u * many + sub].astype(F32) + (
            inverse * scaled - resid * (inverse * inverse * inverse) * mean
        )
        resid_grad_out[own] = d_resid
        own_low = d_resid.astype(BF16)
        low[u * many : u * many + sub] = own_low
        gather_start(low, 3, u)
        return jnp.sum(own_low.astype(F32) * acc[0, own], axis=0, keepdims=True)

    mag_first = residual(0)
    scatter_relay(1, 1)
    for start, size in tiles(width, 512):
        at = slice(start, start + size)
        part = dot32(act[...], down_w[:, at], ((1,), (0,)))
        for u in range(2):
            own = slice(u * sub, (u + 1) * sub)
            ff_own[own, at] = part[u * many : u * many + sub]
            for d in range(1, Y):
                first = u * many + d * sub
                ff_send[d - 1, own, at] = part[first : first + sub].astype(BF16)
    mag_second = residual(1)
    for u in range(2):
        gather_relay(low, 3, u)
    for copy in sm_copies:
        copy.wait()
    small = jnp.concatenate([small_ref[0:ff]] + [small_x[i, 0:ff] for i in range(1, X)], axis=0)
    small_o = jnp.concatenate([small_ref[ff:]] + [small_x[i, ff:] for i in range(1, X)], axis=0)
    from_mixed = dot32(mixed_cat, small_o, ((1,), (0,)))[:, 0:16].astype(BF16)
    through = dot32(normed[...], el_ref[...], ((1,), (0,)))
    through = (through[:, 0:32] + through[:, 32:64]).astype(BF16)
    gate_down = dot32(dgate[...], small, ((1,), (0,)))[:, 0:16].astype(BF16)
    up_down = dot32(dup[...], small, ((1,), (0,)))[:, 16:32].astype(BF16)
    from_act = dot32(act[...], small, ((1,), (0,)))[:, 32:48].astype(BF16)
    small_t = jnp.transpose(small.astype(F32))
    pull_gate = (small_t[48:64] * mags[0:1]).astype(BF16)
    pull_up = (small_t[64:80] * mags[1:2]).astype(BF16)

    def columns(row, value):
        for i in range(X):
            columns_out[i, row : row + value.shape[0]] = value[:, i * ff : (i + 1) * ff]

    columns(0, dot32(through[:, 0:16], dgate[...], ((0,), (0,))))
    columns(16, dot32(through[:, 16:32], dup[...], ((0,), (0,))))
    columns(32, dot32(through_down, act[...], ((0,), (0,))))
    columns(48, jnp.concatenate([mags[...], jnp.zeros((6, X * ff), F32)], axis=0))
    early_out[0:16] = dot32(gate_down, normed[...], ((0,), (0,))) - dot32(
        pull_gate, gate_w[...], ((1,), (0,))
    )
    early_out[16:32] = dot32(up_down, normed[...], ((0,), (0,))) - dot32(
        pull_up, up_w[...], ((1,), (0,))
    )
    early_out[48:64] = dot32(from_act, cot_ref[...], ((0,), (0,)))
    early_out[64:80] = jnp.concatenate(
        [mag_first + mag_second, jnp.zeros((15, width), F32)], axis=0
    )
    for u in range(2):
        gather_wait(3, u)
    d_mixed = dot32(low[...], out_w[...], ((1,), (1,))).astype(BF16)
    for i in range(X):
        for u in range(2):
            for b in range(Y):
                first = u * many + b * sub
                dmix_out[i, b * piece + u * sub : b * piece + (u + 1) * sub] = d_mixed[
                    first : first + sub, i * HD : (i + 1) * HD
                ]
    through_out = dot32(low[...], upper_o, ((1,), (1,))).astype(BF16)
    value = dot32(through_out, mixed_cat, ((0,), (0,)))
    for i in range(X):
        lower_out[i] = value[:, i * HD : (i + 1) * HD]
    early_out[32:48] = dot32(from_mixed, low[...], ((0,), (0,)))


def feed(mixed_x, hidden, gain, cotangent, weights, small, el, upper, mago, squares):
    _, here, width = hidden.shape
    piece = here // Y
    many = (weights.shape[1] - HD) // 3 * X
    s = jax.ShapeDtypeStruct
    return call(
        feed_kernel,
        (
            s((piece, width), F32),
            s((piece, width), F32),
            s((piece, width), F32),
            s((Y - 1, piece, width), BF16),
            s((X, here, HD), BF16),
            s((80, width), F32),
            s((X, 56, many // X), F32),
            s((X, 16, HD), F32),
        ),
        [VM, ANY, VM, ANY, ANY, VM, VM, VM, VM, VM],
        (VM,) * 8,
        [
            pltpu.VMEM((X * HD, width), BF16),
            pltpu.VMEM((many, width), BF16),
            pltpu.VMEM((many, width), BF16),
            pltpu.VMEM((many, width), BF16),
            pltpu.VMEM((here, width), BF16),
            pltpu.VMEM((here, width), BF16),
            pltpu.VMEM((here, many), BF16),
            pltpu.VMEM((here, many), BF16),
            pltpu.VMEM((here, many), BF16),
            pltpu.VMEM((2, 2, piece // 2, width), BF16),
            pltpu.VMEM((2, 2, 2, piece // 2, width), BF16),
            pltpu.VMEM((2, 2, 2, piece // 2, width // 2), F32),
            pltpu.VMEM((2, 2, 2, piece // 2, width // 2), BF16),
            pltpu.VMEM((2, 2, 2, piece // 2, width), BF16),
            pltpu.VMEM((2, piece, width), F32),
            pltpu.VMEM((2, many), F32),
            pltpu.VMEM((piece, width), BF16),
            pltpu.VMEM((here, width), BF16),
            pltpu.VMEM((here // 2, many), F32),
            pltpu.VMEM((here // 2, many), F32),
            pltpu.VMEM((here, many), F32),
            pltpu.VMEM((X,) + small.shape, BF16),
            dma(4, X), dma(4, 2, 6), dma(4, 2, 6), dma(1 + 2 * Y), dma(3), dma(3), dma(1, 2), dma(1, 2), dma(1, 2), dma(1, 2),
            dma(1, 3), dma(1, 3),
        ],
        1,
        2 * here * many * width * 6,
        32 * 2**20,
    )(mixed_x, hidden, gain, cotangent, weights, small, el, upper, mago, squares)


def attend_back_kernel(
    q_ref, kv_ref, dmix_ref, soft_ref, log_ref, begin_ref, tag_ref, cos_ref, sin_ref, resid_ref,
    ff_own, ff_send, cot_ref,
    grads_out, block_out, mag_out,
    kv_all, dmix_all, dmix_abs, part, own, sib_s, sib_r, z_own, z_s, z_r, dq_s, ff_r, block_ref,
    cot_own, f_send, f_recv, d_send, d_recv, b_send, b_recv, sib_send, sib_recv, z_send, z_recv, local,
):
    z, core, y, x = place()
    me = z * 2 + core
    rows, here = q_ref.shape[0], q_ref.shape[1]
    piece, width = resid_ref.shape
    half = width // 2
    load = keep(kv_ref, kv_all, local.at[0])
    greet(
        [device(dx=d) for d in (1, 2, 3)]
        + [device(dy=d) for d in (1, 2, 3)]
        + [device(dz=d) for d in (1, 2, 3)]
        + [device(dc=1)]
    )
    d_copies = [
        send(
            dmix_ref.at[X - d], dmix_all.at[x], d_send.at[d - 1], d_recv.at[d - 1], device(dx=d)
        )
        for d in NEAR_LAST
    ]
    own_mix = keep(dmix_ref.at[0], dmix_all.at[x], local.at[1])
    tokens = pl.ds(pl.multiple_of(y * piece, piece), piece)
    left, right = pl.ds(0, half), pl.ds(half, half)
    load_cot = keep(cot_ref.at[x, tokens], cot_own, local.at[2])
    f_copies = [
        send(ff_send.at[d - 1], ff_r.at[d - 1], f_send.at[d - 1], f_recv.at[d - 1], device(dy=d))
        for d in NEAR_LAST
    ]
    block_one, block_two = [], {}
    load.wait()
    own_mix.wait()
    for copy in d_copies:
        copy.wait()
    spot_q = lax.broadcasted_iota(jnp.int32, (here, 1), 0) + me * here
    sib_copies, z_copies = [], []

    def pass_on(r):
        sib_copies[r].wait()
        z_own[r] = own[r, z] + sib_r[r, z].astype(F32)
        for d in NEAR_LAST:
            to = (z + d) % Z
            z_s[r, d - 1] = (own[r, to] + sib_r[r, to].astype(F32)).astype(BF16)
            z_copies.append(
                send(
                    z_s.at[r, d - 1], z_r.at[r, d - 1], z_send.at[r, d - 1], z_recv.at[r, d - 1],
                    device(dz=d),
                )
            )

    def back(a, r):
        cosine, sine = cos_ref[r], sin_ref[r]
        weighted = a * sine
        turned = jnp.concatenate([weighted[:, HD // 2 :], -weighted[:, : HD // 2]], axis=1)
        return a * cosine + turned

    for r in range(rows):
        for j in range(Y):
            dmix_abs[pl.ds(pl.multiple_of(((y + j) % Y) * piece, piece), piece)] = dmix_all[
                r, j * piece : (j + 1) * piece
            ]
        query = q_ref[r]
        grad = dmix_abs[...]
        delta = jnp.sum(grad.astype(F32) * soft_ref[r], axis=1, keepdims=True)
        begin = begin_ref[r]
        log = log_ref[r]
        d_query = jnp.zeros((here, HD), F32)
        for b in range(Z):
            keys = jnp.concatenate([kv_all[2 * b + k, r, :, :HD] for k in range(2)], axis=0)
            values = jnp.concatenate([kv_all[2 * b + k, r, :, HD:] for k in range(2)], axis=0)
            raw = dot32(query, keys, ((1,), (1,))) * (HD**-0.5)
            key_spot = lax.broadcasted_iota(jnp.int32, (1, KB), 1) + b * KB
            ok = mask_of(begin, spot_q, tag_ref[r, :, b * KB : (b + 1) * KB], key_spot)
            probs = jnp.exp(jnp.where(ok, raw, -1e30) - log)
            d_probs = dot32(grad, values, ((1,), (1,)))
            d_scores = (probs * (d_probs - delta)).astype(BF16)
            d_query = d_query + dot32(d_scores, keys, ((1,), (0,)))
            d_keys = dot32(d_scores, query, ((0,), (0,))) * (HD**-0.5)
            d_values = dot32(probs.astype(BF16), grad, ((0,), (0,)))
            for k in range(2):
                part[b, k, :, :HD] = d_keys[k * here : (k + 1) * here]
                part[b, k, :, HD:] = d_values[k * here : (k + 1) * here]
        dq_s[r] = d_query * (HD**-0.5)
        for b in range(Z):
            sib_s[r, b] = part[b, 1 - core].astype(BF16)
            own[r, b] = part[b, core]
        sib_copies.append(
            send(sib_s.at[r], sib_r.at[r], sib_send.at[r], sib_recv.at[r], device(dc=1))
        )
        grads_out[r, :, :HD] = back(dq_s[r], r).astype(BF16)
        if r:
            pass_on(r - 1)
        if r == 0:
            load_cot.wait()
            for copy in f_copies:
                copy.wait()
            feedforward = ff_own[...] + (
                ff_r[0].astype(F32) + ff_r[1].astype(F32) + ff_r[2].astype(F32)
            )
            mag_out[...] = jnp.zeros(mag_out.shape, F32) + jnp.sum(
                cot_own[...].astype(F32) * feedforward, axis=0, keepdims=True
            )
            block_ref[...] = (resid_ref[...] + feedforward).astype(BF16)
            own_block = keep(block_ref, block_out.at[x, tokens], local.at[3])
            for d in NEAR_LAST:
                for k, cut in enumerate((left, right)):
                    block_one.append(
                        send(
                            block_ref.at[:, cut], block_out.at[x, tokens, cut],
                            b_send.at[k, d - 1], b_recv.at[k, d - 1],
                            device(dy=d) if k else device(dx=d),
                        )
                    )
        if r == 1:
            own_block.wait()
            for copy in block_one:
                copy.wait()
            for k in range(2):
                for side, d in enumerate((1, 3)):
                    at = block_out.at[x, :, right] if k else block_out.at[:, tokens, left]
                    block_two[k, side] = send(
                        at, at, b_send.at[2 + k, side], b_recv.at[2 + k, side],
                        device(dx=d) if k else device(dy=d),
                    )
        if r == 3:
            for k in range(2):
                for side, d in enumerate((1, 3)):
                    block_two[k, side].wait_recv()
                    if k:
                        at = block_out.at[
                            (x + X - d) % X, pl.ds(side * (here // 2), here // 2), right
                        ]
                    else:
                        block = pl.ds(pl.multiple_of(((y + Y - d) % Y) * piece, piece), piece)
                        at = block_out.at[pl.ds(side * (rows // 2), rows // 2), block, left]
                    block_two[k, 2 + side] = send(
                        at, at, b_send.at[4 + k, side], b_recv.at[4 + k, side],
                        device(dx=d) if k else device(dy=d),
                    )
    pass_on(rows - 1)
    for r in range(rows):
        for copy in z_copies[3 * r : 3 * r + 3]:
            copy.wait()
        total = z_own[r] + (
            z_r[r, 0].astype(F32) + z_r[r, 1].astype(F32) + z_r[r, 2].astype(F32)
        )
        grads_out[r, :, HD : 2 * HD] = back(total[:, :HD], r).astype(BF16)
        grads_out[r, :, 2 * HD :] = total[:, HD:].astype(BF16)
    for k in range(2):
        for side in range(2):
            block_two[k, side].wait_send()
            block_two[k, 2 + side].wait()


def attend_back(
    queries, kv, dmix, soft, log, begin, tag, cosine, sine, resid, ff_own, ff_send, cotangent
):
    rows, here, _ = queries.shape
    piece, width = resid.shape
    return call(
        attend_back_kernel,
        (
            jax.ShapeDtypeStruct((rows, here, 3 * HD), BF16),
            jax.ShapeDtypeStruct((rows, here, width), BF16),
            jax.ShapeDtypeStruct((8, width), F32),
        ),
        [VM, ANY] + [VM] * 9 + [ANY, ANY],
        (VM, ANY, VM),
        [
            pltpu.VMEM((2 * Z, rows, here, 2 * HD), BF16),
            pltpu.VMEM((rows, here, HD), BF16),
            pltpu.VMEM((here, HD), BF16),
            pltpu.VMEM((Z, 2, here, 2 * HD), F32),
            pltpu.VMEM((rows, Z, here, 2 * HD), F32),
            pltpu.VMEM((rows, Z, here, 2 * HD), BF16),
            pltpu.VMEM((rows, Z, here, 2 * HD), BF16),
            pltpu.VMEM((rows, here, 2 * HD), F32),
            pltpu.VMEM((rows, Z - 1, here, 2 * HD), BF16),
            pltpu.VMEM((rows, Z - 1, here, 2 * HD), BF16),
            pltpu.VMEM((rows, here, HD), F32),
            pltpu.VMEM((Y - 1, piece, width), BF16),
            pltpu.VMEM((piece, width), BF16),
            pltpu.VMEM((piece, width), BF16),
            dma(3), dma(3), dma(3), dma(3), dma(6, 3), dma(6, 3), dma(rows), dma(rows),
            dma(rows, 3), dma(rows, 3), dma(4),
        ],
        2,
        2 * 5 * rows * here * 2 * Z * here * HD,
        32 * 2**20,
    )(
        queries, kv, dmix, soft, log, begin, tag, cosine, sine, resid, ff_own, ff_send, cotangent
    )


def tail_kernel(
    grads_ref, weight_ref, hidden_ref, gain_ref, dres_ref, pre_ref, thr_ref, n1_ref, inner_ref,
    cola_ref, maga_ref, uppera_ref, early_ref, both_ref, block_ref, lower_ref,
    magd_ref, grad_out, all_out, block_out, ctx_out,
    rel, two, near, held, hop, came, acc, send_2, recv_2, d_one, spread, n1, down, all_s,
    hid_ref, gath, c_r, z_s, z_b, z_r, x_s, x_r, y_v, bx_r, lx_r, b_one, b_two, e_one, e_two, e_z, b_z,
    s_one, r_one, s_two, r_two, s_gat, r_gat, ss, rs, local,
):
    z, core, y, x = place()
    rows, here, deep = grads_ref.shape
    piece, width = dres_ref.shape
    half = width // 2
    sub = piece // 2
    mid = here // 4
    n = all_s.shape[0]
    nc = n // 2
    wz, wx = width // Z, width // Z // X
    rank = 16
    load_hid = keep(
        hidden_ref.at[x, pl.ds(pl.multiple_of(y * piece, piece), piece)], hid_ref, local.at[2]
    )
    load = keep(n1_ref, n1, local.at[0])
    for i in range(X):
        for j in range(Y):
            rel[i, j] = grads_ref[
                (x + i) % X, pl.ds(pl.multiple_of(((y + j) % Y) * piece, piece), piece)
            ]
    greet(
        [device(dx=d) for d in (1, 2, 3)]
        + [device(dy=d) for d in (1, 2, 3)]
        + [device(dz=d) for d in (1, 2, 3)]
        + [device(dc=1)]
    )

    def to(k, d):
        return device(dy=d) if k else device(dx=d)

    def ds(index, size):
        return pl.ds(pl.multiple_of(index * size, size), size)

    def done(copies):
        for copy in copies:
            copy.wait()

    def term(k, d, begin, size):
        if k:
            lhs = jnp.concatenate([rel[i, d] for i in range(X)], axis=0)
        else:
            lhs = rel[d].reshape(here, deep)
        return dot32(lhs, weight_ref[k * half + begin : k * half + begin + size], ((1,), (1,)))

    def cut(part, u, first, count):
        return jnp.concatenate(
            [
                part[b * piece + u * sub : b * piece + (u + 1) * sub]
                for b in range(first, first + count)
            ],
            axis=0,
        )

    one = {}

    def start_far(u):
        for k in range(2):
            for side, d in enumerate((1, 3)):
                one[k, u, side] = send(
                    two.at[k, u, pl.ds(side * mid, mid)], hop.at[k, u, side],
                    s_one.at[k, u, side], r_one.at[k, u, side], to(k, d),
                )

    def start_near(u):
        for k in range(2):
            for side, d in enumerate((1, 3)):
                plain = pl.ds((1 - side) * mid, mid)
                one[k, u, 2 + side] = send(
                    near.at[k, u, side, plain], came.at[k, u, side, plain],
                    s_one.at[k, u, 2 + side], r_one.at[k, u, 2 + side], to(k, d),
                )

    for k in range(2):
        for start, size in tiles(half, 512):
            part = term(k, 2, start, size)
            for u in range(2):
                two[k, u, :, start : start + size] = cut(part, u, 0, 4).astype(BF16)
    start_far(0)
    for k in range(2):
        for side, d in enumerate((1, 3)):
            for start, size in tiles(half, 512):
                at = slice(start, start + size)
                part = term(k, d, start, size)
                rest = (1 - side) * mid
                for u in range(2):
                    near[k, u, side, rest : rest + mid, at] = cut(
                        part, u, 2 * (1 - side), 2
                    ).astype(BF16)
                    held[k, u, side, :, at] = cut(part, u, 2 * side, 2)
    start_near(0)
    start_far(1)
    start_near(1)
    for k in range(2):
        for start, size in tiles(half, 512):
            part = term(k, 0, start, size)
            for u in range(2):
                acc[k, u, :, start : start + size] = cut(part, u, 0, 4)

    for m in range(3):
        at = slice(m * HD, (m + 1) * HD)
        grad = grads_ref[:, :, at].reshape(rows * here, HD)
        before = pre_ref[:, :, at].reshape(rows * here, HD)
        column, magnitude = cola_ref[m : m + 1], maga_ref[m : m + 1]
        ratio = magnitude / column
        mag = jnp.sum(grad.astype(F32) * before, axis=0, keepdims=True) / magnitude
        pull = magnitude * mag / (column * column)
        thin = thr_ref[:, :, m * rank : (m + 1) * rank] + thr_ref[
            :, :, (3 + m) * rank : (4 + m) * rank
        ]
        thin = thin.reshape(rows * here, rank).astype(BF16)
        part = dot32(thin, grad, ((0,), (0,)))
        e_one[(1 + m) * rank : (2 + m) * rank] = adapter_scale * (
            part * ratio - inner_ref[m] * pull
        )
        e_one[4 * rank + m : 4 * rank + m + 1] = mag
        upper = uppera_ref[m]
        down[:, m * rank : (m + 1) * rank] = dot32(
            grad, (upper * ratio).astype(BF16), ((1,), (1,))
        ).astype(BF16)
        pulled = (upper * (mag / column)).astype(BF16)
        for start, size in tiles(width, 512):
            all_s[(7 + m) * rank : (8 + m) * rank, start : start + size] = dot32(
                pulled, weight_ref[start : start + size, at], ((1,), (1,))
            )
    e_one[4 * rank + 3 :] = jnp.zeros((e_one.shape[0] - 4 * rank - 3, HD), F32)
    load.wait()
    for start, size in tiles(width, 512):
        at = slice(start, start + size)
        value = dot32(
            down[...], n1[:, :, at].reshape(rows * here, size), ((0,), (0,))
        )
        all_s[7 * rank : 10 * rank, at] = value - all_s[7 * rank : 10 * rank, at]
    all_s[0 : 5 * rank] = early_ref[...]
    all_s[4 * rank + 1 : 4 * rank + 2] = magd_ref[0:1]
    all_s[5 * rank : 7 * rank] = both_ref[...] * (1.0 / (2 * Z))
    all_s[10 * rank :] = jnp.zeros((n - 10 * rank, width), F32)

    def go(k, d, src, dst, where):
        return send(src, dst, ss.at[k, d], rs.at[k, d], where)

    first = [go(0, 0, all_s.at[ds(1 - core, nc)], c_r, device(dc=1))]
    slots = []
    for d in NEAR_LAST:
        slots.append(go(1, d, block_ref.at[X - d], bx_r.at[d - 1], device(dx=d)))
        slots.append(go(2, d, lower_ref.at[X - d], lx_r.at[d - 1], device(dx=d)))
    for u in range(2):
        for k in range(2):
            for side, d in enumerate((1, 3)):
                one[k, u, side].wait_recv()
                other = pl.ds(side * mid, mid)
                near[k, u, side, side * mid : (side + 1) * mid] = (
                    held[k, u, side] + hop[k, u, side].astype(F32)
                ).astype(BF16)
                one[k, u, 4 + side] = send(
                    near.at[k, u, side, other], came.at[k, u, side, other],
                    s_one.at[k, u, 4 + side], r_one.at[k, u, 4 + side], to(k, d),
                )
    done(first)
    z_s[...] = all_s[ds(core, nc)] + c_r[...]
    z_b[...] = z_s[...].astype(BF16)
    zc = [
        go(3, d, z_b.at[:, ds((z + d) % Z, wz)], z_r.at[d - 1], device(dz=d)) for d in NEAR_LAST
    ]
    done(slots)
    b_one[...] = block_ref[0] + (bx_r[0] + bx_r[1] + bx_r[2])
    e_one[:rank] = lower_ref[0] + (lx_r[0] + lx_r[1] + lx_r[2])
    cc = [go(4, 0, b_one, b_two, device(dc=1)), go(5, 0, e_one, e_two, device(dc=1))]
    seconds = [[], []]
    for u in range(2):
        for k in range(2):
            for index in range(2):
                one[k, u, index].wait_send()
            for index in (2, 3, 4, 5):
                one[k, u, index].wait()
        for k in range(2):
            for d in (2, 1, 3, 0):
                at = slice(d * sub, (d + 1) * sub)
                part = acc[k, u, at] + (
                    came[k, u, 0, at].astype(F32) + came[k, u, 1, at].astype(F32)
                )
                if d:
                    send_2[u, k, d - 1] = part.astype(BF16)
                    seconds[u].append(
                        send(
                            send_2.at[u, k, d - 1], recv_2.at[u, k, d - 1], s_two.at[u, k, d - 1],
                            r_two.at[u, k, d - 1], to(1 - k, d),
                        )
                    )
                else:
                    d_one[u, :, k * half : (k + 1) * half] = part
    done(cc)
    b_two[...] += b_one[...]
    e_two[...] += e_one[...]
    done(zc)
    x_s[...] = z_s[:, ds(z, wz)] + (
        z_r[0].astype(F32) + z_r[1].astype(F32) + z_r[2].astype(F32)
    )
    cz = []
    b_z[z] = b_two[...]
    e_z[z] = e_two[...]
    for d in NEAR_LAST:
        cz.append(go(6, d, b_two, b_z.at[z], device(dz=d)))
        cz.append(go(7, d, e_two, e_z.at[z], device(dz=d)))
    xc = [go(8, d, x_s.at[:, ds((x + d) % X, wx)], x_r.at[d - 1], device(dx=d)) for d in NEAR_LAST]
    left, right = pl.ds(0, half), pl.ds(half, half)
    load_hid.wait()
    gat = [[], []]
    for u in range(2):
        done(seconds[u])
        for k in range(2):
            d_one[u, :, k * half : (k + 1) * half] += (
                recv_2[u, k, 0].astype(F32)
                + recv_2[u, k, 1].astype(F32)
                + recv_2[u, k, 2].astype(F32)
            )
        own = slice(u * sub, (u + 1) * sub)
        inputs = hid_ref[own].astype(F32)
        inverse = lax.rsqrt(jnp.mean(inputs * inputs, axis=1, keepdims=True) + epsilon)
        scaled = d_one[u] * gain_ref[...]
        result = dres_ref[own] + (
            inverse * scaled
            - inputs
            * (inverse * inverse * inverse)
            * jnp.mean(inputs * scaled, axis=1, keepdims=True)
        )
        spread[x, y, own] = result.astype(BF16)
        for d in NEAR_LAST:
            for k, side in enumerate((left, right)):
                at = spread.at[x, y, pl.ds(u * sub, sub), side]
                gat[u].append(
                    send(at, at, s_gat.at[u, k, d - 1], r_gat.at[u, k, d - 1], to(k, d))
                )
        if u == 0:
            done(xc)
            y_v[y] = x_s[:, ds(x, wx)] + (x_r[0] + x_r[1] + x_r[2])
            yc = [go(9, d, y_v.at[y], y_v.at[y], device(dy=d)) for d in NEAR_LAST]
    done(yc)
    mine = ds(core, nc)
    at_x = ds(z * X + x, wx)
    gath[mine, at_x] = (((y_v[0] + y_v[1]) + y_v[2]) + y_v[3]).astype(BF16)
    sx = [go(10, d, gath.at[mine, at_x], gath.at[mine, at_x], device(dx=d)) for d in NEAR_LAST]

    def part_of(k, u, d, first, count):
        tokens = pl.ds(u * sub, sub)
        if k:
            return spread.at[(x + d) % X, pl.ds(first, count), tokens, right]
        return spread.at[pl.ds(first, count), (y + d) % Y, tokens, left]

    last = {}
    for u in range(2):
        done(gat[u])
        for k in range(2):
            for side, d in enumerate((1, 3)):
                at = part_of(k, u, 0, 0, 4)
                last[k, u, side] = send(
                    at, at, s_gat.at[u, 2 + k, side], r_gat.at[u, 2 + k, side], to(1 - k, d)
                )
    done(sx)
    spot = gath.at[mine, ds(z, wz)]
    sz = [go(11, d, spot, spot, device(dz=d)) for d in NEAR_LAST]
    done(cz)
    block_out[...] = ((b_z[0] + b_z[1]) + b_z[2]) + b_z[3]
    ctx_out[...] = ((e_z[0] + e_z[1]) + e_z[2]) + e_z[3]
    done(sz)
    spot = gath.at[mine]
    sc = go(12, 0, spot, spot, device(dc=1))
    for u in range(2):
        for k in range(2):
            for side, d in enumerate((1, 3)):
                last[k, u, side].wait_recv()
                at = part_of(k, u, 4 - d, 2 * side, 2)
                last[k, u, 2 + side] = send(
                    at, at, s_gat.at[u, 4 + k, side], r_gat.at[u, 4 + k, side], to(1 - k, d)
                )
    for u in range(2):
        for k in range(2):
            for side in range(2):
                last[k, u, side].wait_send()
                last[k, u, 2 + side].wait()
    out = keep(spread, grad_out, local.at[1])
    sc.wait()
    all_out[...] = gath[...]
    out.wait()


def tail(
    grads, weight, hidden, gain, d_resid, pre, thr, n1, inner, cola, maga, uppera, early, both,
    block, lower, magd,
):
    rows, here, deep = grads.shape
    piece, width = d_resid.shape
    half = width // 2
    mid = here // 4
    sub = piece // 2
    _, bn, bw = block.shape
    n = 192
    en = 72
    nc = n // 2
    wz, wx = width // Z, width // Z // X
    s = jax.ShapeDtypeStruct
    v = pltpu.VMEM
    return call(
        tail_kernel,
        (s((rows, Y, piece, width), BF16), s((n, width), BF16), s((bn, bw), F32), s((en, HD), F32)),
        [VM] * 2 + [ANY] + [VM] * 4 + [ANY] + [VM] * 9,
        (ANY, VM, VM, VM),
        [
            v((X, Y, piece, deep), BF16),
            v((2, 2, 2 * mid, half), BF16),
            v((2, 2, 2, 2 * mid, half), BF16),
            v((2, 2, 2, mid, half), F32),
            v((2, 2, 2, mid, half), BF16),
            v((2, 2, 2, 2 * mid, half), BF16),
            v((2, 2, 2 * mid, half), F32),
            v((2, 2, 3, sub, half), BF16),
            v((2, 2, 3, sub, half), BF16),
            v((2, sub, width), F32),
            v((X, Y, piece, width), BF16),
            v((rows, here, width), BF16),
            v((rows * here, 48), BF16),
            v((n, width), F32),
            v((piece, width), BF16),
            v((n, width), BF16),
            v((nc, width), F32),
            v((nc, width), F32),
            v((nc, width), BF16),
            v((3, nc, wz), BF16),
            v((nc, wz), F32),
            v((3, nc, wx), F32),
            v((Y, nc, wx), F32),
            v((3, bn, bw), F32),
            v((3, 16, HD), F32),
            v((bn, bw), F32),
            v((bn, bw), F32),
            v((en, HD), F32),
            v((en, HD), F32),
            v((Z, en, HD), F32),
            v((Z, bn, bw), F32),
            dma(2, 2, 6), dma(2, 2, 6), dma(2, 2, 3), dma(2, 2, 3), dma(2, 6, 3), dma(2, 6, 3),
            dma(13, 4), dma(13, 4), dma(3),
        ],
        3,
        2 * rows * here * deep * width,
        16 * 2**20,
    )(
        grads, weight, hidden, gain, d_resid, pre, thr, n1, inner, cola, maga, uppera, early, both,
        block, lower, magd,
    )


def widen_kernel(a_ref, b_ref, wide_out, same_out, narrow, wide, passed, loads, stores):
    rows = a_ref.shape[0]
    copies = [keep(a_ref.at[r], narrow.at[r], loads.at[0, r]) for r in range(rows)]
    others = [keep(b_ref.at[r], passed.at[r], loads.at[1, r]) for r in range(rows)]
    outs = []
    for r in range(rows):
        copies[r].wait()
        wide[r] = narrow[r].astype(F32)
        outs.append(keep(wide.at[r], wide_out.at[r], stores.at[0, r]))
    for r in range(rows):
        others[r].wait()
        outs.append(keep(passed.at[r], same_out.at[r], stores.at[1, r]))
    for copy in outs:
        copy.wait()


def widen(a, b):
    parts = 16
    many, width = a.shape[0] * a.shape[1] * a.shape[2] // parts, a.shape[3]
    wide, same = pl.pallas_call(
        widen_kernel,
        out_shape=(
            jax.ShapeDtypeStruct((parts, many, width), F32),
            jax.ShapeDtypeStruct((parts, many, width), BF16),
        ),
        in_specs=[ANY, ANY],
        out_specs=(ANY, ANY),
        scratch_shapes=[
            pltpu.VMEM((parts, many, width), BF16),
            pltpu.VMEM((parts, many, width), F32),
            pltpu.VMEM((parts, many, width), BF16),
            dma(2, parts), dma(2, parts),
        ],
        compiler_params=pltpu.CompilerParams(vmem_limit_bytes=58 * 2**20),
    )(a.reshape(parts, many, width), b.reshape(parts, many, width))
    return wide.reshape(b.shape), same.reshape(b.shape)


def on_device(
    hidden,
    segments,
    key_attendable,
    attention_gain,
    feedforward_gain,
    attend_frozen,
    output_frozen,
    expand_frozen,
    reduce_frozen,
    attend_lower,
    attend_upper,
    attend_magnitude,
    output_lower,
    output_upper,
    output_magnitude,
    expand_lower,
    expand_upper,
    expand_magnitude,
    reduce_lower,
    reduce_upper,
    reduce_magnitude,
    cotangent,
):
    rows, here, width = hidden.shape
    length = segments.shape[1]
    ff = reduce_frozen.shape[0]
    rank = output_lower.shape[1]
    ctx = lax.axis_index("ctx")
    offset = ctx * here

    def left_factor(a):
        high, low = halves(a)
        return jnp.concatenate([high, high, low], axis=-1)

    def right_factor(a):
        high, low = halves(a)
        return jnp.concatenate([high, low, high], axis=-2)

    expand_upper_t = expand_upper.transpose(0, 2, 1)
    aw = left_factor(
        jnp.concatenate([output_lower, expand_upper_t[0], expand_upper_t[1], reduce_lower], axis=0)
    )
    bw = right_factor(
        jnp.stack([output_upper, expand_lower[0].T, expand_lower[1].T, reduce_upper], axis=0)
    )
    la = left_factor(attend_lower)
    ua = right_factor(attend_upper)
    flat_lower = attend_lower.transpose(1, 0, 2).reshape(width, 3 * rank)
    high, low = halves(flat_lower)
    thin = jnp.concatenate([high, low, jnp.zeros((width, HD - 6 * rank), BF16)], axis=1)
    flat_lower = expand_lower.transpose(1, 0, 2).reshape(width, 2 * rank)
    high, low = halves(flat_lower)
    el = jnp.concatenate([high, low, jnp.zeros((width, HD - 4 * rank), BF16)], axis=1)
    small = jnp.concatenate([expand_upper_t[0], expand_upper_t[1], reduce_lower], axis=1)
    small = jnp.concatenate(
        [
            jnp.pad(small, ((0, 0), (0, HD - 3 * rank))),
            jnp.pad(output_lower, ((0, 0), (0, HD - rank))),
        ],
        axis=0,
    )
    mago = jnp.stack([output_magnitude, reduce_magnitude])
    upper = jnp.concatenate([output_upper, reduce_upper], axis=0)

    levels = jnp.arange(SEGS, dtype=jnp.int32)
    below_count = jnp.sum((segments[:, None, :] < levels[None, :, None]).astype(F32), axis=2)
    segments_here = lax.dynamic_slice_in_dim(segments, offset, here, 1)
    begin_here = jnp.sum(
        (segments_here[:, :, None] == levels[None, None, :]).astype(F32) * below_count[:, None, :],
        axis=2,
    )
    spot_here = offset + jnp.arange(here, dtype=jnp.int32)
    places = spot_here.astype(F32)[None, :] - begin_here
    frequency = rotary_base ** (-(2.0 * jnp.arange(HD // 2).astype(F32)) / HD)
    frequency = jnp.concatenate([frequency, frequency])
    angles = places[:, :, None] * frequency[None, None, :]
    cosine, sine_part = jnp.cos(angles), jnp.sin(angles)
    spots = jnp.arange(length, dtype=jnp.int32)[None]
    key_tag = jnp.where(key_attendable == 1, spots, -1)[:, None, :]
    begin = begin_here.astype(jnp.int32)[:, :, None]
    gain_one = attention_gain.astype(F32)
    gain_two = feedforward_gain.astype(F32)

    (
        mixed_parts,
        soft,
        log_total,
        all_pairs,
        weights_x,
        weight_attend,
        queries,
        pre,
        through_three,
        column_attend,
        column_expand,
        squares,
        inner_attend,
        inner_expand,
        inner_both,
        normed_one,
        small_own,
    ) = front(
        hidden,
        gain_one[None],
        attend_frozen,
        la,
        ua,
        attend_magnitude,
        thin,
        output_frozen,
        expand_frozen.transpose(0, 2, 1),
        reduce_frozen,
        aw,
        bw,
        expand_magnitude.reshape(2 * ff, 1),
        mago,
        el,
        small,
        cosine,
        sine_part,
        begin,
        key_tag,
    )
    d_resid, resid, ff_own, ff_send, d_mixed_parts, early, block_x, lower_out = feed(
        mixed_parts, hidden, gain_two[None], cotangent, weights_x, small_own, el, upper, mago, squares
    )
    grads_low, block_output, mag_down = attend_back(
        queries,
        all_pairs,
        d_mixed_parts,
        soft,
        log_total,
        begin,
        key_tag,
        cosine,
        sine_part,
        resid,
        ff_own,
        ff_send,
        cotangent,
    )
    hidden_grad, everywhere, block_x, small_ctx = tail(
        grads_low,
        weight_attend,
        hidden,
        gain_one[None],
        d_resid,
        pre,
        through_three,
        normed_one,
        inner_attend,
        column_attend,
        attend_magnitude,
        attend_upper,
        early,
        inner_both,
        block_x,
        lower_out,
        mag_down,
    )
    hidden_grad, block_output = widen(hidden_grad, block_output)
    everywhere = everywhere.astype(F32)
    lower_out, local = small_ctx[:rank], small_ctx[rank:]
    late = adapter_scale * everywhere[7 * rank : 10 * rank]
    early = everywhere[: 7 * rank]

    attend_lower_grad = late.reshape(3, rank, width).transpose(0, 2, 1)
    attend_upper_grad = local[: 3 * rank].reshape(3, rank, HD)
    attend_magnitude_grad = local[3 * rank : 3 * rank + 3]
    column_expand = column_expand.reshape(2, ff)
    inner_expand = inner_expand.reshape(2, ff, HD)
    inner_expand = inner_expand[..., : 2 * rank] + inner_expand[..., 2 * rank : 4 * rank]
    expand_magnitude_grad = block_x[3 * rank : 3 * rank + 2] / expand_magnitude
    pull_expand = expand_magnitude * expand_magnitude_grad / column_expand**2
    ratio_expand = expand_magnitude / column_expand
    expand_upper_grad = jnp.stack(
        [
            adapter_scale
            * (
                block_x[m * rank : (m + 1) * rank] * ratio_expand[m]
                - inner_expand[m, :, m * rank : (m + 1) * rank].T * pull_expand[m]
            )
            for m in range(2)
        ]
    )
    expand_lower_grad = adapter_scale * early[: 2 * rank].reshape(2, rank, width).transpose(0, 2, 1)
    columns = jnp.sqrt(squares)
    magnitude_grads = early[4 * rank : 4 * rank + 2] / mago
    pulls = mago * magnitude_grads / squares
    ratios = mago / columns
    output_magnitude_grad = magnitude_grads[0]
    reduce_magnitude_grad = magnitude_grads[1]
    output_upper_grad = adapter_scale * (
        early[2 * rank : 3 * rank] * ratios[0] - early[5 * rank : 6 * rank] * pulls[0]
    )
    reduce_upper_grad = adapter_scale * (
        early[3 * rank : 4 * rank] * ratios[1] - early[6 * rank : 7 * rank] * pulls[1]
    )

    def pulled_rows(frozen, lower, upper, pull):
        pulled = upper * pull
        rows_part = exact_dot(frozen, pulled, ((1,), (1,)))
        return rows_part + adapter_scale * jnp.dot(
            lower,
            jnp.dot(upper, pulled.T, precision=lax.Precision.HIGHEST),
            precision=lax.Precision.HIGHEST,
        )

    output_lower_grad = adapter_scale * (
        lower_out.T - pulled_rows(output_frozen, output_lower, output_upper, pulls[0])
    )
    reduce_lower_grad = adapter_scale * (
        block_x[2 * rank : 3 * rank].T
        - pulled_rows(reduce_frozen, reduce_lower, reduce_upper, pulls[1])
    )
    return (
        block_output,
        hidden_grad,
        attend_lower_grad,
        attend_upper_grad,
        attend_magnitude_grad,
        output_lower_grad,
        output_upper_grad,
        output_magnitude_grad,
        expand_lower_grad,
        expand_upper_grad,
        expand_magnitude_grad,
        reduce_lower_grad,
        reduce_upper_grad,
        reduce_magnitude_grad,
    )


def solution(mesh):
    placed = (
        P(None, "ctx", None),
        P(),
        P(),
        P(),
        P(),
        P(None, None, "tp"),
        P("tp", None),
        P(None, None, "tp"),
        P("tp", None),
        P(),
        P(None, None, "tp"),
        P(None, "tp"),
        P("tp", None),
        P(),
        P(),
        P(),
        P(None, None, "tp"),
        P(None, "tp"),
        P("tp", None),
        P(),
        P(),
        P(None, "ctx", None),
    )
    return jax.shard_map(
        on_device,
        mesh=mesh,
        in_specs=placed,
        out_specs=(
            P(None, "ctx", None),
            P(None, "ctx", None),
            P(),
            P(None, None, "tp"),
            P(None, "tp"),
            P("tp", None),
            P(),
            P(),
            P(),
            P(None, None, "tp"),
            P(None, "tp"),
            P("tp", None),
            P(),
            P(),
        ),
        check_vma=False,
    )
```

```python
import jax
import jax.numpy as jnp
from jax import lax
from jax.experimental import pallas as pl
from jax.experimental.pallas import tpu as pltpu
from jax.sharding import PartitionSpec as P

HD = 128
SEGS = 4
X = 4
Y = 4
Z = 4

epsilon = 1e-05
adapter_scale = 2.0
rotary_base = 10000.0
F32 = jnp.float32
BF16 = jnp.bfloat16


def halves(a):
    high = lax.reduce_precision(a, 8, 7)
    return high.astype(BF16), (a - high).astype(BF16)


def dot32(a, b, dims):
    return lax.dot_general(a, b, (dims, ((), ())), preferred_element_type=F32)


def exact_dot(bf, full, dims):
    high, low = halves(full)
    return dot32(bf, high, dims) + dot32(bf, low, dims)


def rotate(tensor, cosine, sine_part):
    half_width = tensor.shape[-1] // 2
    turned = jnp.concatenate([-tensor[..., half_width:], tensor[..., :half_width]], axis=-1)
    return tensor * cosine + turned * sine_part


MESH = pl.DeviceIdType.MESH
ANY = pl.BlockSpec(memory_space=pl.ANY)
VM = pl.BlockSpec(memory_space=pltpu.VMEM)
NEAR_LAST = (2, 1, 3)


def place():
    ctx = lax.axis_index("ctx")
    tp = lax.axis_index("tp")
    return ctx // 2, ctx % 2, tp // X, tp % X


def device(dz=0, dc=0, dy=0, dx=0):
    z, core, y, x = place()
    return (((z + dz) % Z) * 2 + (core + dc) % 2, ((y + dy) % Y) * X + (x + dx) % X)


def greet(devices):
    barrier = pltpu.get_barrier_semaphore()
    for d in devices:
        pl.semaphore_signal(barrier, inc=1, device_id=d, device_id_type=MESH)
    pl.semaphore_wait(barrier, len(devices))


def send(src, dst, send_sem, recv_sem, to):
    copy = pltpu.make_async_remote_copy(
        src_ref=src,
        dst_ref=dst,
        send_sem=send_sem,
        recv_sem=recv_sem,
        device_id=to,
        device_id_type=MESH,
    )
    copy.start()
    return copy


def keep(src, dst, sem):
    copy = pltpu.make_async_copy(src, dst, sem)
    copy.start()
    return copy


def dma(*shape):
    return pltpu.SemaphoreType.DMA(shape)


def call(kernel, outs, in_specs, out_specs, scratch, number, flops, moved):
    return pl.pallas_call(
        kernel,
        out_shape=outs,
        in_specs=in_specs,
        out_specs=out_specs,
        scratch_shapes=scratch,
        cost_estimate=pl.CostEstimate(flops=flops, bytes_accessed=moved, transcendentals=0),
        compiler_params=pltpu.CompilerParams(
            collective_id=number, has_side_effects=True, vmem_limit_bytes=58 * 2**20
        ),
    )


def mask_of(begin, spot_q, key_tag, key_spot):
    return ((key_tag >= begin) & (key_tag <= spot_q)) | (key_spot == spot_q)


KB = 512


def tiles(total, size):
    return [(s, min(size, total - s)) for s in range(0, total, size)]


PIECES = 3


def relay_plan(weights, send_a, recv_a, send_b, recv_b, send_s, recv_s, cols):
    def begin(p, own, start, size):
        return [
            send(own, weights(1, start, size), send_a.at[p, 0], recv_a.at[p, 0], device(dx=1)),
            send(own, weights(3, start, size), send_a.at[p, 1], recv_a.at[p, 1], device(dx=3)),
        ]

    def relay(p, copies, start, size):
        half = size // 2
        more = []
        for k, (slot, at, to) in enumerate(((1, start, 1), (3, start + half, 3))):
            copies[k].wait_recv()
            more.append(
                send(
                    weights(slot, at, half), weights(2, at, half),
                    send_b.at[p, k], recv_b.at[p, k], device(dx=to),
                )
            )
            there = weights(slot, start, size)
            more.append(send(there, there, send_s.at[p, k], recv_s.at[p, k], device(dc=1)))
        return more

    def relay_far(p, more, start, size):
        more[0].wait_recv()
        more[2].wait_recv()
        there = weights(2, start, size)
        return send(there, there, send_s.at[p, 2], recv_s.at[p, 2], device(dc=1))

    def finish(copies, more, last):
        more[1].wait_recv()
        more[3].wait_recv()
        last.wait_recv()
        for copy in copies + more + [last]:
            copy.wait_send()

    return begin, relay, relay_far, finish


def parts_of(a):
    high = a.astype(BF16)
    return high, (a - high.astype(F32)).astype(BF16)


def left_parts(a):
    high, low = parts_of(a)
    return jnp.concatenate([high, high, low], axis=0)


def right_parts(a):
    high, low = parts_of(a)
    return jnp.concatenate([high, low, high], axis=0)


def front_kernel(
    hidden_ref, vec_ref, frozen_ref, la_ref, ua_ref, maga_ref, fo_ref, fe_ref, fr_ref, lo_ref, ue_ref,
    lr_ref, uo_ref, le_ref, small_ref, cos_ref, sin_ref, begin_ref, tag_ref,
    mixed_out, soft_out, log_out, kv_out, weights_out, wq_out, q_out, pre_out, thr_out,
    cola_out, cole_out, sq_out, ina_out, ine_out, ino_out, n1_out, small,
    kv_all, score, soft, logs, mixed, mixed_x, joined, w_own, wq_all, normed, kv_own, hid_ref, fa_ref, right_s, la_s, thin_s, el_s,
    sq_x, sq_y, sq_one, ja,
    kv_send, kv_recv, sib_send, sib_recv, a_send, a_recv, b_send, b_recv, ws_send, ws_recv,
    wz_send, wz_recv, wo_send, wo_recv, m_send, m_recv, sq_send, sq_recv, local, n_local, in_local,
):
    z, core, y, x = place()
    me = z * 2 + core
    rows, here, width = hidden_ref.shape
    length = Z * 2 * here
    ff = fr_ref.shape[0]
    piece = here // Y
    step = width // 16
    odd = z % 2
    xcols = pl.ds(pl.multiple_of((core * 8 + odd * 3) * step, step), 5 * step)
    zmine = pl.ds(pl.multiple_of((core * 8 + odd * 5) * step, step), 3 * step)
    zother = pl.ds(pl.multiple_of((core * 8 + (1 - odd) * 5) * step, step), 3 * step)
    loads = [keep(frozen_ref, fa_ref, in_local.at[0])]
    loads += [keep(hidden_ref.at[r], hid_ref.at[r], in_local.at[1 + r]) for r in range(rows)]
    greet(
        [device(dx=d) for d in (1, 2, 3)]
        + [device(dy=d) for d in (1, 2, 3)]
        + [device(dz=d) for d in (1, 2, 3)]
        + [device(dc=1)]
    )

    lefts = [left_parts(lo_ref[...])] + [left_parts(ue_ref[m]) for m in range(2)]
    lefts.append(left_parts(lr_ref[...]))
    right_s[0] = right_parts(uo_ref[0:16])
    right_s[3] = right_parts(uo_ref[16:32])
    for m in range(2):
        right_s[1 + m] = right_parts(le_ref[m * 16 : (m + 1) * 16])
    for m in range(3):
        la_s[m] = left_parts(la_ref[m * 16 : (m + 1) * 16])
    high, low = parts_of(la_ref[...])
    thin_s[...] = jnp.concatenate([high, low, jnp.zeros((32, width), BF16)], axis=0)
    high, low = parts_of(le_ref[...])
    el_s[...] = jnp.concatenate([high, low, jnp.zeros((64, width), BF16)], axis=0)

    def join(matrix, at):
        low = dot32(lefts[matrix], right_s[matrix, :, at], ((0,), (0,)))
        if matrix in (1, 2):
            frozen = fe_ref[matrix - 1, :, at]
        else:
            frozen = fr_ref[:, at] if matrix else fo_ref[:, at]
        return frozen.astype(F32) + adapter_scale * low

    for s, size in tiles(width, 512):
        at = slice(s, s + size)
        one = join(0, at)
        two = join(3, at)
        sq_one[0:1, at] = jnp.sum(one * one, axis=0, keepdims=True)
        sq_one[1:2, at] = jnp.sum(two * two, axis=0, keepdims=True)
    sq_copies = [
        send(sq_one, sq_x.at[d - 1], sq_send.at[0, d - 1], sq_recv.at[0, d - 1], device(dx=d))
        for d in NEAR_LAST
    ]

    where = ((HD, ff), (HD + ff, ff), (0, HD))
    moves = [{}, {}, {}]

    def there(slot, start, size, cols):
        return weights_out.at[slot, pl.ds(start, size), cols]

    def begin(p):
        start, size = where[p]
        for k, (slot, d) in enumerate(((1, 1), (3, 3))):
            moves[p]["a", k] = send(
                w_own.at[pl.ds(start, size), xcols], there(slot, start, size, xcols),
                a_send.at[p, k], a_recv.at[p, k], device(dx=d),
            )

    def share(p, slot):
        start, size = where[p]
        half = size // 2
        at = there(slot, start, size, xcols)
        moves[p]["s", slot] = send(
            at, at, ws_send.at[p, slot - 1], ws_recv.at[p, slot - 1], device(dc=1)
        )
        for k, (first, d) in enumerate(((start, 1), (start + half, 3))):
            at = there(slot, first, half, zmine)
            moves[p]["z", slot, k] = send(
                at, at, wz_send.at[p, slot - 1, k], wz_recv.at[p, slot - 1, k], device(dz=d)
            )

    def relay(p):
        start, size = where[p]
        half = size // 2
        for k, (slot, first) in enumerate(((1, start), (3, start + half))):
            moves[p]["a", k].wait_recv()
            moves[p]["b", k] = send(
                there(slot, first, half, xcols), there(2, first, half, xcols),
                b_send.at[p, k], b_recv.at[p, k], device(dx=slot),
            )
            share(p, slot)

    def relay_far(p):
        moves[p]["b", 0].wait_recv()
        moves[p]["b", 1].wait_recv()
        share(p, 2)

    def relay_z(p, slot):
        start, size = where[p]
        moves[p]["z", slot, 0].wait_recv()
        moves[p]["z", slot, 1].wait_recv()
        at = there(slot, start, size, zother)
        moves[p]["o", slot] = send(
            at, at, wo_send.at[p, slot - 1], wo_recv.at[p, slot - 1], device(dc=1)
        )

    def finish(p):
        for slot in (1, 2, 3):
            moves[p]["s", slot].wait_recv()
            moves[p]["o", slot].wait_recv()
        for copy in moves[p].values():
            copy.wait_send()

    for m in range(2):
        start = HD + m * ff
        total = jnp.zeros((ff, 1), F32)
        for s, size in tiles(width, 512):
            at = slice(s, s + size)
            value = join(1 + m, at)
            joined[:, at] = value
            total = total + jnp.sum(value * value, axis=1, keepdims=True)
        column = jnp.sqrt(total)
        cole_out[m * ff : (m + 1) * ff] = column
        magnitude = small_ref[0:ff, 48 + m : 49 + m]
        ratio = magnitude / column
        for s, size in tiles(width, 512):
            at = slice(s, s + size)
            w_own[start : start + ff, at] = (joined[:, at] * ratio).astype(BF16)
        begin(m)
        inner = dot32(w_own[start : start + ff], el_s[...], ((1,), (1,)))
        ine_out[m * ff : (m + 1) * ff] = inner / ratio
        source = small_ref[0:ff, m * 16 : (m + 1) * 16]
        small[0:ff, m * 16 : (m + 1) * 16] = (source * ratio).astype(BF16)
        small[0:ff, (3 + m) * 16 : (4 + m) * 16] = (source / (magnitude * column)).astype(BF16)
    small[0:ff, 32:48] = small_ref[0:ff, 32:48].astype(BF16)
    small[0:ff, 80:] = jnp.zeros((ff, HD - 80), BF16)
    small[ff:] = small_ref[ff:].astype(BF16)
    own = []
    for copy in sq_copies:
        copy.wait()
    sq_one[...] += sq_x[0] + sq_x[1] + sq_x[2]
    sq_copies = [
        send(sq_one, sq_y.at[d - 1], sq_send.at[1, d - 1], sq_recv.at[1, d - 1], device(dy=d))
        for d in NEAR_LAST
    ]
    loads[0].wait()
    for m in range(3):
        total = jnp.zeros((1, HD), F32)
        upper = right_parts(ua_ref[m])
        for s, size in tiles(width, 512):
            at = slice(s, s + size)
            value = fa_ref[m, at].astype(F32) + adapter_scale * dot32(
                la_s[m, :, at], upper, ((0,), (0,))
            )
            ja[at] = value
            total = total + jnp.sum(value * value, axis=0, keepdims=True)
        column = jnp.sqrt(total)
        cola_out[m : m + 1] = column
        ratio = maga_ref[m : m + 1] / column
        wq_all[:, m * HD : (m + 1) * HD] = (ja[...] * ratio).astype(BF16)
        inner = dot32(la_s[m], ja[...].astype(BF16), ((1,), (0,)))
        ina_out[m] = inner[0:16] + inner[32:48]
    own.append(keep(wq_all, wq_out, local.at[1]))
    kv_copies, sib_copies, n_copies = {}, [], []
    gain = vec_ref[0:1]
    for r in range(rows):
        loads[1 + r].wait()
        inputs = hid_ref[r].astype(F32)
        inverse = lax.rsqrt(jnp.mean(inputs * inputs, axis=1, keepdims=True) + epsilon)
        if r >= 2:
            n_copies[r - 2].wait()
        normed[r % 2] = (inputs * inverse * gain).astype(BF16)
        n_copies.append(keep(normed.at[r % 2], n1_out.at[r], n_local.at[r]))
        pre = dot32(normed[r % 2], wq_all[...], ((1,), (0,)))
        pre_out[r] = pre
        thin = dot32(normed[r % 2], thin_s[...], ((1,), (1,)))
        thr_out[r] = thin
        cosine, sine = cos_ref[r], sin_ref[r]
        q_out[r] = rotate(pre[:, :HD], cosine, sine).astype(BF16)
        kv_own[r, :, :HD] = rotate(pre[:, HD : 2 * HD], cosine, sine).astype(BF16)
        kv_own[r, :, HD:] = pre[:, 2 * HD :].astype(BF16)
        for k, d in enumerate((1, 3)):
            kv_copies[r, k] = send(
                kv_own.at[r], kv_all.at[me, r], kv_send.at[r, k], kv_recv.at[r, k], device(dz=d)
            )
        sib_copies.append(
            send(kv_own.at[r], kv_all.at[me, r], sib_send.at[r, 0], sib_recv.at[r, 0], device(dc=1))
        )
    own.append(keep(kv_own, kv_all.at[me], local.at[2]))
    for copy in sq_copies:
        copy.wait()
    squares = sq_one[...] + (sq_y[0] + sq_y[1] + sq_y[2])
    sq_out[...] = squares
    ratios = vec_ref[2:4] / jnp.sqrt(squares)
    for s, size in tiles(width, 512):
        at = slice(s, s + size)
        one = join(0, at)
        two = join(3, at)
        w_own[0:HD, at] = (one * ratios[0:1, at]).astype(BF16)
        w_own[HD + 2 * ff :, at] = (two * ratios[1:2, at]).astype(BF16)
        ino_out[0:16, at] = dot32(small[ff:], one.astype(BF16), ((0,), (0,)))[0:16]
        ino_out[16:32, at] = dot32(small[0:ff], two.astype(BF16), ((0,), (0,)))[32:48]
    begin(2)
    own.append(keep(w_own, weights_out.at[0], local.at[3]))

    def pass_kv(r):
        for k, d in enumerate((1, 3)):
            kv_copies[r, k].wait_recv()
            at = kv_all.at[((z + Z - d) % Z) * 2 + core, r]
            if (k == 0) == (r < rows // 2):
                kv_copies[r, 2] = send(at, at, kv_send.at[r, 2], kv_recv.at[r, 2], device(dz=d))
            sib_copies.append(
                send(at, at, sib_send.at[r, 1 + k], sib_recv.at[r, 1 + k], device(dc=1))
            )

    def pass_far(r):
        kv_copies[r, 2].wait_recv()
        at = kv_all.at[((z + 2) % Z) * 2 + core, r]
        sib_copies.append(send(at, at, sib_send.at[r, 3], sib_recv.at[r, 3], device(dc=1)))

    for r in range(rows):
        pass_kv(r)
    relay(0)
    for r in range(rows):
        pass_far(r)
    relay(1)
    own[1].wait()
    for copy in sib_copies:
        copy.wait_recv()
    own.append(keep(kv_all, kv_out, local.at[4]))
    spot_q = lax.broadcasted_iota(jnp.int32, (here, 1), 0) + me * here
    m_copies = []
    for i in (2, 1, 3, 0):
        row = (x + i) % X
        query = q_out[row]
        first = begin_ref[row]
        peak = jnp.full((here, 1), -1e30, F32)
        for b in range(length // KB):
            keys = jnp.concatenate(
                [kv_all[b * (KB // here) + k, row, :, :HD] for k in range(KB // here)], axis=0
            )
            raw = dot32(query, keys, ((1,), (1,))) * (HD**-0.5)
            key_spot = lax.broadcasted_iota(jnp.int32, (1, KB), 1) + b * KB
            ok = mask_of(first, spot_q, tag_ref[row, :, b * KB : (b + 1) * KB], key_spot)
            raw = jnp.where(ok, raw, -1e30)
            score[:, b * KB : (b + 1) * KB] = raw
            peak = jnp.maximum(peak, jnp.max(raw, axis=1, keepdims=True))
        total = jnp.zeros((here, 1), F32)
        gathered = jnp.zeros((here, HD), F32)
        for b in range(length // KB):
            power = jnp.exp(score[:, b * KB : (b + 1) * KB] - peak)
            total = total + jnp.sum(power, axis=1, keepdims=True)
            values = jnp.concatenate(
                [kv_all[b * (KB // here) + k, row, :, HD:] for k in range(KB // here)], axis=0
            )
            gathered = gathered + dot32(power.astype(BF16), values, ((1,), (0,)))
        soft[row] = gathered / total
        logs[row] = peak + jnp.log(total)
        for j in range(Y):
            mixed[i, j * piece : (j + 1) * piece] = soft[
                row, pl.ds(pl.multiple_of(((y + j) % Y) * piece, piece), piece)
            ].astype(BF16)
        if i:
            m_copies.append(
                send(mixed.at[i], mixed_x.at[i], m_send.at[i - 1], m_recv.at[i - 1], device(dx=i))
            )
        else:
            mixed_x[0] = mixed[0]
        if i == 2:
            relay(2)
        if i == 1:
            relay_far(0)
            relay_z(0, 1)
            relay_z(0, 3)
        if i == 3:
            relay_far(1)
            relay_z(1, 1)
            relay_z(1, 3)
    own.append(keep(soft, soft_out, local.at[5]))
    own.append(keep(logs, log_out, local.at[6]))
    relay_far(2)
    relay_z(2, 1)
    relay_z(2, 3)
    for p in range(PIECES):
        relay_z(p, 2)
    for copy in m_copies:
        copy.wait()
    own.append(keep(mixed_x, mixed_out, local.at[7]))
    for copy in list(kv_copies.values()) + sib_copies:
        copy.wait_send()
    for p in range(PIECES):
        finish(p)
    for copy in n_copies[rows - 2 :]:
        copy.wait()
    own.pop(1)
    for copy in own:
        copy.wait()


def front(
    hidden, vectors, fa, la, ua, maga, fo, fe, fr, lo, ue, lr, uo, le, small, cos, sin, begin, tag
):
    rows, here, width = hidden.shape
    ff = fr.shape[0]
    count = HD + 3 * ff
    length = 2 * Z * here
    s = jax.ShapeDtypeStruct
    return call(
        front_kernel,
        (
            s((X, here, HD), BF16),
            s((rows, here, HD), F32),
            s((rows, here, 1), F32),
            s((2 * Z, rows, here, 2 * HD), BF16),
            s((X, count, width), BF16),
            s((width, 3 * HD), BF16),
            s((rows, here, HD), BF16),
            s((rows, here, 3 * HD), F32),
            s((rows, here, HD), F32),
            s((3, HD), F32),
            s((2 * ff, 1), F32),
            s((2, width), F32),
            s((3, 16, HD), F32),
            s((2 * ff, HD), F32),
            s((32, width), F32),
            s((rows, here, width), BF16),
            s((ff + HD, HD), BF16),
        ),
        [ANY, VM, ANY] + [VM] * 16,
        (ANY,) * 6 + (VM,) * 9 + (ANY, VM),
        [
            pltpu.VMEM((2 * Z, rows, here, 2 * HD), BF16),
            pltpu.VMEM((here, length), F32),
            pltpu.VMEM((rows, here, HD), F32),
            pltpu.VMEM((rows, here, 1), F32),
            pltpu.VMEM((X, here, HD), BF16),
            pltpu.VMEM((X, here, HD), BF16),
            pltpu.VMEM((ff, width), F32),
            pltpu.VMEM((count, width), BF16),
            pltpu.VMEM((width, 3 * HD), BF16),
            pltpu.VMEM((2, here, width), BF16),
            pltpu.VMEM((rows, here, 2 * HD), BF16),
            pltpu.VMEM(hidden.shape, BF16),
            pltpu.VMEM(fa.shape, BF16),
            pltpu.VMEM((4, 48, width), BF16),
            pltpu.VMEM((3, 48, width), BF16),
            pltpu.VMEM((HD, width), BF16),
            pltpu.VMEM((HD, width), BF16),
            pltpu.VMEM((3, 2, width), F32),
            pltpu.VMEM((3, 2, width), F32),
            pltpu.VMEM((2, width), F32),
            pltpu.VMEM((width, HD), F32),
            dma(rows, 3), dma(rows, 3), dma(rows, 4), dma(rows, 4),
            dma(PIECES, 2), dma(PIECES, 2), dma(PIECES, 2), dma(PIECES, 2),
            dma(PIECES, 3), dma(PIECES, 3), dma(PIECES, 3, 2), dma(PIECES, 3, 2),
            dma(PIECES, 3), dma(PIECES, 3),
            dma(3), dma(3), dma(2, 3), dma(2, 3), dma(8), dma(rows), dma(1 + rows),
        ],
        0,
        2 * 2 * rows * here * length * HD + 2 * rows * here * width * 4 * HD,
        32 * 2**20,
    )(
        hidden, vectors, fa, la, ua, maga, fo, fe, fr, lo, ue, lr, uo, le, small, cos, sin, begin, tag
    )


def feed_kernel(
    mixed_ref, hidden_ref, vec_ref, cotangent_ref, weights_ref, small_ref, el_ref, upper_ref,
    sq_ref,
    resid_grad_out, resid_s, ff_own, ff_send, dmix_out, early_out, columns_out, lower_out,
    out_w, gate_w, up_w, down_w, normed, low, act, dgate, dup, far, near, held, hop, came, acc, mags,
    hid_ref, cot_ref, gate_s, up_s, dact_s,
    small_x, load, s_send, s_recv, local, sm_send, sm_recv, a_send, a_recv, b_send, b_recv, ws_send, ws_recv,
):
    z, core, y, x = place()
    width = hid_ref.shape[1]
    piece = hid_ref.shape[0]
    here = cot_ref.shape[0]
    ff = gate_w.shape[0] // X
    sub = piece // 2
    many = here // 2
    cols = pl.ds(pl.multiple_of(core * (width // 2), width // 2), width // 2)
    down_rows = pl.ds(HD + 2 * ff, ff)
    tokens = pl.ds(pl.multiple_of(y * piece, piece), piece)
    loads = [[], [], [], [], [keep(hidden_ref.at[x, tokens], hid_ref, local.at[0])]]
    for u in range(2):
        for j in range(Y):
            first = ((y + j) % Y) * piece + u * sub
            loads[4].append(
                keep(
                    cotangent_ref.at[x, pl.ds(pl.multiple_of(first, sub), sub)],
                    cot_ref.at[pl.ds(u * many + j * sub, sub)],
                    local.at[1 + u * Y + j],
                )
            )
    for w, (dst, start, size) in enumerate(((out_w, 0, HD), (gate_w, HD, ff), (up_w, HD + ff, ff))):
        for i in range(X):
            loads[w].append(
                keep(
                    weights_ref.at[i, pl.ds(start, size)], dst.at[pl.ds(i * size, size)],
                    load.at[w, i],
                )
            )
    loads[3].append(keep(weights_ref.at[0, down_rows], down_w.at[pl.ds(0, ff)], load.at[3, 0]))
    greet(
        [device(dy=d) for d in (1, 2, 3)] + [device(dx=1), device(dx=2), device(dx=3), device(dc=1)]
    )

    def there(slot, start, size):
        return down_w.at[pl.ds(slot * ff + start, size), cols]

    begin, relay, relay_far, finish = relay_plan(
        there, a_send, a_recv, b_send, b_recv, ws_send, ws_recv, cols
    )
    sent = begin(0, weights_ref.at[0, down_rows, cols], 0, ff)

    def loaded(w):
        for copy in loads[w]:
            copy.wait()

    half = width // 2
    cut_a, cut_b = pl.ds(0, half), pl.ds(half, half)
    moves = {}

    def put(k, u, part, start, size):
        at = slice(start, start + size)
        acc[k, u * sub : (u + 1) * sub, at] = part[0:sub]
        far[k, u, :, at] = part[2 * sub : 3 * sub].astype(BF16)
        for side, block in enumerate((1, 3)):
            value = part[block * sub : (block + 1) * sub]
            if (start < half) == (side == 1):
                near[k, u, side, :, at] = value.astype(BF16)
            else:
                inner = start % half
                held[k, u, side, :, inner : inner + size] = value

    def scatter_start(k, u):
        for side, (cut, d) in enumerate(((cut_a, 1), (cut_b, 3))):
            moves[k, u, side] = send(
                far.at[k, u, :, cut], hop.at[k, u, side], s_send.at[k, u, side],
                s_recv.at[k, u, side], device(dy=d),
            )
        for side, (cut, d) in enumerate(((cut_b, 1), (cut_a, 3))):
            moves[k, u, 2 + side] = send(
                near.at[k, u, side, :, cut], came.at[k, u, side, :, cut],
                s_send.at[k, u, 2 + side], s_recv.at[k, u, 2 + side], device(dy=d),
            )

    def scatter_relay(k, u):
        for side, (cut, d) in enumerate(((cut_a, 1), (cut_b, 3))):
            moves[k, u, side].wait_recv()
            near[k, u, side, :, side * half : (side + 1) * half] = (
                held[k, u, side] + hop[k, u, side].astype(F32)
            ).astype(BF16)
            moves[k, u, 4 + side] = send(
                near.at[k, u, side, :, cut], came.at[k, u, side, :, cut],
                s_send.at[k, u, 4 + side], s_recv.at[k, u, 4 + side], device(dy=d),
            )

    def scatter_sum(k, u):
        for index in range(2):
            moves[k, u, index].wait_send()
        for index in range(2, 6):
            moves[k, u, index].wait()
        return acc[k, u * sub : (u + 1) * sub] + (
            came[k, u, 0].astype(F32) + came[k, u, 1].astype(F32)
        )

    def block_at(buffer, u, block, cut=slice(None)):
        return buffer.at[pl.ds(u * many + block * sub, sub), cut]

    def gather_start(buffer, k, u):
        for side, (d, block) in enumerate(((1, 3), (3, 1))):
            moves[k, u, side] = send(
                block_at(buffer, u, 0), block_at(buffer, u, block), s_send.at[k, u, side],
                s_recv.at[k, u, side], device(dy=d),
            )

    def gather_relay(buffer, k, u):
        for side, (d, block, cut) in enumerate(((1, 3, cut_a), (3, 1, cut_b))):
            moves[k, u, side].wait_recv()
            moves[k, u, 2 + side] = send(
                block_at(buffer, u, block, cut), block_at(buffer, u, 2, cut),
                s_send.at[k, u, 2 + side], s_recv.at[k, u, 2 + side], device(dy=d),
            )

    def gather_wait(k, u):
        for side in range(2):
            moves[k, u, side].wait_send()
            moves[k, u, 2 + side].wait()

    loaded(0)
    mixed_cat = jnp.concatenate(
        [
            jnp.concatenate(
                [mixed_ref[i, b * piece + u * sub : b * piece + (u + 1) * sub] for i in range(X)],
                axis=1,
            )
            for u in range(2)
            for b in range(Y)
        ],
        axis=0,
    )
    for start, size in tiles(width, 512):
        at = slice(start, start + size)
        part = dot32(mixed_cat, out_w[:, at], ((1,), (0,)))
        for u in range(2):
            put(0, u, part[u * many : (u + 1) * many], start, size)
    for u in range(2):
        scatter_start(0, u)
    ratios = vec_ref[2:4] / jnp.sqrt(sq_ref[...])
    upper_o = (upper_ref[0:16] * ratios[0:1]).astype(BF16)
    upper_d = (upper_ref[16:32] * ratios[1:2]).astype(BF16)
    loaded(4)
    through_down = dot32(cot_ref[...], upper_d, ((1,), (1,))).astype(BF16)
    gain = vec_ref[1:2]
    for u in range(2):
        scatter_relay(0, u)
    for u in range(2):
        own = slice(u * sub, (u + 1) * sub)
        attended = scatter_sum(0, u)
        acc[0, own] = attended
        resid = hid_ref[own].astype(F32) + attended
        inverse = lax.rsqrt(jnp.mean(resid * resid, axis=1, keepdims=True) + epsilon)
        resid_s[own] = resid
        normed[u * many : u * many + sub] = (resid * inverse * gain).astype(BF16)
        gather_start(normed, 2, u)
        if u == 0:
            more = relay(0, sent, 0, ff)
            sm_copies = [
                send(small_ref, small_x.at[d], sm_send.at[d - 1], sm_recv.at[d - 1], device(dx=d))
                for d in NEAR_LAST
            ]
    loaded(1)
    loaded(2)
    loaded(3)
    for u in range(2):
        gather_relay(normed, 2, u)
    for u in range(2):
        rows = slice(u * many, (u + 1) * many)
        gather_wait(2, u)
        for start, size in tiles(X * ff, 256):
            at = slice(start, start + size)
            gate_s[:, at] = dot32(normed[rows], gate_w[at], ((1,), (1,)))
            up_s[:, at] = dot32(normed[rows], up_w[at], ((1,), (1,)))
        if u == 0:
            more_far = relay_far(0, more, 0, ff)
            finish(sent, more, more_far)
            for start, size in tiles(X * ff, 256):
                at = slice(start, start + size)
                dact_s[:, at] = dot32(cot_ref[...], down_w[at], ((1,), (1,)))
        else:
            scatter_relay(1, 0)
        for start, size in tiles(X * ff, 256):
            at = slice(start, start + size)
            gate, up, d_act = gate_s[:, at], up_s[:, at], dact_s[rows, at]
            sig = 1.0 / (1.0 + jnp.exp(-gate))
            gated = gate * sig
            act[rows, at] = (gated * up).astype(BF16)
            d_gate = (d_act * up * sig * (1.0 + gate * (1.0 - sig))).astype(BF16)
            d_up = (d_act * gated).astype(BF16)
            dgate[rows, at] = d_gate
            dup[rows, at] = d_up
            both = jnp.concatenate(
                [
                    jnp.sum(d_gate.astype(F32) * gate, axis=0, keepdims=True),
                    jnp.sum(d_up.astype(F32) * up, axis=0, keepdims=True),
                ],
                axis=0,
            )
            mags[:, at] = mags[:, at] + both if u else both
        for start, size in tiles(width, 512):
            at = slice(start, start + size)
            part = dot32(dgate[rows], gate_w[:, at], ((1,), (0,)))
            part = part + dot32(dup[rows], up_w[:, at], ((1,), (0,)))
            put(1, u, part, start, size)
        scatter_start(1, u)

    def residual(u):
        own = slice(u * sub, (u + 1) * sub)
        d_two = scatter_sum(1, u)
        resid = resid_s[own]
        inverse = lax.rsqrt(jnp.mean(resid * resid, axis=1, keepdims=True) + epsilon)
        scaled = d_two * gain
        mean = jnp.mean(resid * scaled, axis=1, keepdims=True)
        d_resid = cot_ref[u * many : u * many + sub].astype(F32) + (
            inverse * scaled - resid * (inverse * inverse * inverse) * mean
        )
        resid_grad_out[own] = d_resid
        own_low = d_resid.astype(BF16)
        low[u * many : u * many + sub] = own_low
        gather_start(low, 3, u)
        return jnp.sum(own_low.astype(F32) * acc[0, own], axis=0, keepdims=True)

    mag_first = residual(0)
    scatter_relay(1, 1)
    for start, size in tiles(width, 512):
        at = slice(start, start + size)
        part = dot32(act[...], down_w[:, at], ((1,), (0,)))
        for u in range(2):
            own = slice(u * sub, (u + 1) * sub)
            ff_own[own, at] = part[u * many : u * many + sub]
            for d in range(1, Y):
                first = u * many + d * sub
                ff_send[d - 1, own, at] = part[first : first + sub].astype(BF16)
    mag_second = residual(1)
    for u in range(2):
        gather_relay(low, 3, u)
    for copy in sm_copies:
        copy.wait()
    small = jnp.concatenate([small_ref[0:ff]] + [small_x[i, 0:ff] for i in range(1, X)], axis=0)
    small_o = jnp.concatenate([small_ref[ff:]] + [small_x[i, ff:] for i in range(1, X)], axis=0)
    from_mixed = dot32(mixed_cat, small_o, ((1,), (0,)))[:, 0:16].astype(BF16)
    high, low_part = parts_of(el_ref[...])
    through = dot32(
        normed[...], jnp.concatenate([high, low_part], axis=0), ((1,), (1,))
    )
    through = (through[:, 0:32] + through[:, 32:64]).astype(BF16)
    gate_down = dot32(dgate[...], small, ((1,), (0,)))[:, 0:16].astype(BF16)
    up_down = dot32(dup[...], small, ((1,), (0,)))[:, 16:32].astype(BF16)
    from_act = dot32(act[...], small, ((1,), (0,)))[:, 32:48].astype(BF16)
    small_t = jnp.transpose(small.astype(F32))
    pull_gate = (small_t[48:64] * mags[0:1]).astype(BF16)
    pull_up = (small_t[64:80] * mags[1:2]).astype(BF16)

    def columns(row, value):
        for i in range(X):
            columns_out[i, row : row + value.shape[0]] = value[:, i * ff : (i + 1) * ff]

    columns(0, dot32(through[:, 0:16], dgate[...], ((0,), (0,))))
    columns(16, dot32(through[:, 16:32], dup[...], ((0,), (0,))))
    columns(32, dot32(through_down, act[...], ((0,), (0,))))
    columns(48, jnp.concatenate([mags[...], jnp.zeros((6, X * ff), F32)], axis=0))
    early_out[0:16] = dot32(gate_down, normed[...], ((0,), (0,))) - dot32(
        pull_gate, gate_w[...], ((1,), (0,))
    )
    early_out[16:32] = dot32(up_down, normed[...], ((0,), (0,))) - dot32(
        pull_up, up_w[...], ((1,), (0,))
    )
    early_out[48:64] = dot32(from_act, cot_ref[...], ((0,), (0,)))
    early_out[64:80] = jnp.concatenate(
        [mag_first + mag_second, jnp.zeros((15, width), F32)], axis=0
    )
    for u in range(2):
        gather_wait(3, u)
    d_mixed = dot32(low[...], out_w[...], ((1,), (1,))).astype(BF16)
    for i in range(X):
        for u in range(2):
            for b in range(Y):
                first = u * many + b * sub
                dmix_out[i, b * piece + u * sub : b * piece + (u + 1) * sub] = d_mixed[
                    first : first + sub, i * HD : (i + 1) * HD
                ]
    through_out = dot32(low[...], upper_o, ((1,), (1,))).astype(BF16)
    value = dot32(through_out, mixed_cat, ((0,), (0,)))
    for i in range(X):
        lower_out[i] = value[:, i * HD : (i + 1) * HD]
    early_out[32:48] = dot32(from_mixed, low[...], ((0,), (0,)))


def feed(mixed_x, hidden, vectors, cotangent, weights, small, el, upper, squares):
    _, here, width = hidden.shape
    piece = here // Y
    many = (weights.shape[1] - HD) // 3 * X
    s = jax.ShapeDtypeStruct
    return call(
        feed_kernel,
        (
            s((piece, width), F32),
            s((piece, width), F32),
            s((piece, width), F32),
            s((Y - 1, piece, width), BF16),
            s((X, here, HD), BF16),
            s((80, width), F32),
            s((X, 56, many // X), F32),
            s((X, 16, HD), F32),
        ),
        [VM, ANY, VM, ANY, ANY, VM, VM, VM, VM],
        (VM,) * 8,
        [
            pltpu.VMEM((X * HD, width), BF16),
            pltpu.VMEM((many, width), BF16),
            pltpu.VMEM((many, width), BF16),
            pltpu.VMEM((many, width), BF16),
            pltpu.VMEM((here, width), BF16),
            pltpu.VMEM((here, width), BF16),
            pltpu.VMEM((here, many), BF16),
            pltpu.VMEM((here, many), BF16),
            pltpu.VMEM((here, many), BF16),
            pltpu.VMEM((2, 2, piece // 2, width), BF16),
            pltpu.VMEM((2, 2, 2, piece // 2, width), BF16),
            pltpu.VMEM((2, 2, 2, piece // 2, width // 2), F32),
            pltpu.VMEM((2, 2, 2, piece // 2, width // 2), BF16),
            pltpu.VMEM((2, 2, 2, piece // 2, width), BF16),
            pltpu.VMEM((2, piece, width), F32),
            pltpu.VMEM((2, many), F32),
            pltpu.VMEM((piece, width), BF16),
            pltpu.VMEM((here, width), BF16),
            pltpu.VMEM((here // 2, many), F32),
            pltpu.VMEM((here // 2, many), F32),
            pltpu.VMEM((here, many), F32),
            pltpu.VMEM((X,) + small.shape, BF16),
            dma(4, X), dma(4, 2, 6), dma(4, 2, 6), dma(1 + 2 * Y), dma(3), dma(3), dma(1, 2), dma(1, 2), dma(1, 2), dma(1, 2),
            dma(1, 3), dma(1, 3),
        ],
        1,
        2 * here * many * width * 6,
        32 * 2**20,
    )(mixed_x, hidden, vectors, cotangent, weights, small, el, upper, squares)


def attend_back_kernel(
    q_ref, kv_ref, dmix_ref, soft_ref, log_ref, begin_ref, tag_ref, cos_ref, sin_ref, resid_ref,
    ff_own, ff_send, cot_ref,
    grads_out, block_out, mag_out,
    kv_all, dmix_all, dmix_abs, part, own, sib_s, sib_r, z_own, z_s, z_r, dq_s, ff_r, block_ref,
    cot_own, f_send, f_recv, d_send, d_recv, b_send, b_recv, sib_send, sib_recv, z_send, z_recv, local,
):
    z, core, y, x = place()
    me = z * 2 + core
    rows, here = q_ref.shape[0], q_ref.shape[1]
    piece, width = resid_ref.shape
    half = width // 2
    load = keep(kv_ref, kv_all, local.at[0])
    greet(
        [device(dx=d) for d in (1, 2, 3)]
        + [device(dy=d) for d in (1, 2, 3)]
        + [device(dz=d) for d in (1, 2, 3)]
        + [device(dc=1)]
    )
    d_copies = [
        send(
            dmix_ref.at[X - d], dmix_all.at[x], d_send.at[d - 1], d_recv.at[d - 1], device(dx=d)
        )
        for d in NEAR_LAST
    ]
    own_mix = keep(dmix_ref.at[0], dmix_all.at[x], local.at[1])
    tokens = pl.ds(pl.multiple_of(y * piece, piece), piece)
    left, right = pl.ds(0, half), pl.ds(half, half)
    load_cot = keep(cot_ref.at[x, tokens], cot_own, local.at[2])
    f_copies = [
        send(ff_send.at[d - 1], ff_r.at[d - 1], f_send.at[d - 1], f_recv.at[d - 1], device(dy=d))
        for d in NEAR_LAST
    ]
    block_one, block_two = [], {}
    load.wait()
    own_mix.wait()
    for copy in d_copies:
        copy.wait()
    spot_q = lax.broadcasted_iota(jnp.int32, (here, 1), 0) + me * here
    sib_copies, z_copies = [], []

    def pass_on(r):
        sib_copies[r].wait()
        z_own[r] = own[r, z] + sib_r[r, z].astype(F32)
        for d in NEAR_LAST:
            to = (z + d) % Z
            z_s[r, d - 1] = (own[r, to] + sib_r[r, to].astype(F32)).astype(BF16)
            z_copies.append(
                send(
                    z_s.at[r, d - 1], z_r.at[r, d - 1], z_send.at[r, d - 1], z_recv.at[r, d - 1],
                    device(dz=d),
                )
            )

    def back(a, r):
        cosine, sine = cos_ref[r], sin_ref[r]
        weighted = a * sine
        turned = jnp.concatenate([weighted[:, HD // 2 :], -weighted[:, : HD // 2]], axis=1)
        return a * cosine + turned

    for r in range(rows):
        for j in range(Y):
            dmix_abs[pl.ds(pl.multiple_of(((y + j) % Y) * piece, piece), piece)] = dmix_all[
                r, j * piece : (j + 1) * piece
            ]
        query = q_ref[r]
        grad = dmix_abs[...]
        delta = jnp.sum(grad.astype(F32) * soft_ref[r], axis=1, keepdims=True)
        begin = begin_ref[r]
        log = log_ref[r]
        d_query = jnp.zeros((here, HD), F32)
        for b in range(Z):
            keys = jnp.concatenate([kv_all[2 * b + k, r, :, :HD] for k in range(2)], axis=0)
            values = jnp.concatenate([kv_all[2 * b + k, r, :, HD:] for k in range(2)], axis=0)
            raw = dot32(query, keys, ((1,), (1,))) * (HD**-0.5)
            key_spot = lax.broadcasted_iota(jnp.int32, (1, KB), 1) + b * KB
            ok = mask_of(begin, spot_q, tag_ref[r, :, b * KB : (b + 1) * KB], key_spot)
            probs = jnp.exp(jnp.where(ok, raw, -1e30) - log)
            d_probs = dot32(grad, values, ((1,), (1,)))
            d_scores = (probs * (d_probs - delta)).astype(BF16)
            d_query = d_query + dot32(d_scores, keys, ((1,), (0,)))
            d_keys = dot32(d_scores, query, ((0,), (0,))) * (HD**-0.5)
            d_values = dot32(probs.astype(BF16), grad, ((0,), (0,)))
            for k in range(2):
                part[b, k, :, :HD] = d_keys[k * here : (k + 1) * here]
                part[b, k, :, HD:] = d_values[k * here : (k + 1) * here]
        dq_s[r] = d_query * (HD**-0.5)
        for b in range(Z):
            sib_s[r, b] = part[b, 1 - core].astype(BF16)
            own[r, b] = part[b, core]
        sib_copies.append(
            send(sib_s.at[r], sib_r.at[r], sib_send.at[r], sib_recv.at[r], device(dc=1))
        )
        grads_out[r, :, :HD] = back(dq_s[r], r).astype(BF16)
        if r:
            pass_on(r - 1)
        if r == 0:
            load_cot.wait()
            for copy in f_copies:
                copy.wait()
            feedforward = ff_own[...] + (
                ff_r[0].astype(F32) + ff_r[1].astype(F32) + ff_r[2].astype(F32)
            )
            mag_out[...] = jnp.zeros(mag_out.shape, F32) + jnp.sum(
                cot_own[...].astype(F32) * feedforward, axis=0, keepdims=True
            )
            block_ref[...] = (resid_ref[...] + feedforward).astype(BF16)
            own_block = keep(block_ref, block_out.at[x, tokens], local.at[3])
            for d in NEAR_LAST:
                for k, cut in enumerate((left, right)):
                    block_one.append(
                        send(
                            block_ref.at[:, cut], block_out.at[x, tokens, cut],
                            b_send.at[k, d - 1], b_recv.at[k, d - 1],
                            device(dy=d) if k else device(dx=d),
                        )
                    )
        if r == 1:
            own_block.wait()
            for copy in block_one:
                copy.wait()
            for k in range(2):
                for side, d in enumerate((1, 3)):
                    at = block_out.at[x, :, right] if k else block_out.at[:, tokens, left]
                    block_two[k, side] = send(
                        at, at, b_send.at[2 + k, side], b_recv.at[2 + k, side],
                        device(dx=d) if k else device(dy=d),
                    )
        if r == 3:
            for k in range(2):
                for side, d in enumerate((1, 3)):
                    block_two[k, side].wait_recv()
                    if k:
                        at = block_out.at[
                            (x + X - d) % X, pl.ds(side * (here // 2), here // 2), right
                        ]
                    else:
                        block = pl.ds(pl.multiple_of(((y + Y - d) % Y) * piece, piece), piece)
                        at = block_out.at[pl.ds(side * (rows // 2), rows // 2), block, left]
                    block_two[k, 2 + side] = send(
                        at, at, b_send.at[4 + k, side], b_recv.at[4 + k, side],
                        device(dx=d) if k else device(dy=d),
                    )
    pass_on(rows - 1)
    for r in range(rows):
        for copy in z_copies[3 * r : 3 * r + 3]:
            copy.wait()
        total = z_own[r] + (
            z_r[r, 0].astype(F32) + z_r[r, 1].astype(F32) + z_r[r, 2].astype(F32)
        )
        grads_out[r, :, HD : 2 * HD] = back(total[:, :HD], r).astype(BF16)
        grads_out[r, :, 2 * HD :] = total[:, HD:].astype(BF16)
    for k in range(2):
        for side in range(2):
            block_two[k, side].wait_send()
            block_two[k, 2 + side].wait()


def attend_back(
    queries, kv, dmix, soft, log, begin, tag, cosine, sine, resid, ff_own, ff_send, cotangent
):
    rows, here, _ = queries.shape
    piece, width = resid.shape
    return call(
        attend_back_kernel,
        (
            jax.ShapeDtypeStruct((rows, here, 3 * HD), BF16),
            jax.ShapeDtypeStruct((rows, here, width), BF16),
            jax.ShapeDtypeStruct((8, width), F32),
        ),
        [VM, ANY] + [VM] * 9 + [ANY, ANY],
        (VM, ANY, VM),
        [
            pltpu.VMEM((2 * Z, rows, here, 2 * HD), BF16),
            pltpu.VMEM((rows, here, HD), BF16),
            pltpu.VMEM((here, HD), BF16),
            pltpu.VMEM((Z, 2, here, 2 * HD), F32),
            pltpu.VMEM((rows, Z, here, 2 * HD), F32),
            pltpu.VMEM((rows, Z, here, 2 * HD), BF16),
            pltpu.VMEM((rows, Z, here, 2 * HD), BF16),
            pltpu.VMEM((rows, here, 2 * HD), F32),
            pltpu.VMEM((rows, Z - 1, here, 2 * HD), BF16),
            pltpu.VMEM((rows, Z - 1, here, 2 * HD), BF16),
            pltpu.VMEM((rows, here, HD), F32),
            pltpu.VMEM((Y - 1, piece, width), BF16),
            pltpu.VMEM((piece, width), BF16),
            pltpu.VMEM((piece, width), BF16),
            dma(3), dma(3), dma(3), dma(3), dma(6, 3), dma(6, 3), dma(rows), dma(rows),
            dma(rows, 3), dma(rows, 3), dma(4),
        ],
        2,
        2 * 5 * rows * here * 2 * Z * here * HD,
        32 * 2**20,
    )(
        queries, kv, dmix, soft, log, begin, tag, cosine, sine, resid, ff_own, ff_send, cotangent
    )


def tail_kernel(
    grads_ref, weight_ref, hidden_ref, vec_ref, dres_ref, pre_hbm, thr_hbm, n1_ref, inner_ref,
    cola_ref, maga_ref, uppera_ref, early_ref, both_ref, block_ref, lower_ref,
    magd_ref, grad_out, all_out, block_out, ctx_out,
    rel, two, near, held, hop, came, acc, send_2, recv_2, d_one, spread, n1, down, all_s,
    hid_ref, pre_ref, thr_ref, gath, c_r, z_s, z_b, z_r, x_s, x_r, y_v, bx_r, lx_r, b_one, b_two, e_one, e_two, e_z, b_z,
    s_one, r_one, s_two, r_two, s_gat, r_gat, ss, rs, local,
):
    z, core, y, x = place()
    rows, here, deep = grads_ref.shape
    piece, width = dres_ref.shape
    half = width // 2
    sub = piece // 2
    mid = here // 4
    n = all_s.shape[0]
    nc = n // 2
    wz, wx = width // Z, width // Z // X
    rank = 16
    load_hid = keep(
        hidden_ref.at[x, pl.ds(pl.multiple_of(y * piece, piece), piece)], hid_ref, local.at[2]
    )
    load = keep(n1_ref, n1, local.at[0])
    load_pre = keep(pre_hbm, pre_ref, local.at[3])
    load_thr = keep(thr_hbm, thr_ref, local.at[4])
    for i in range(X):
        for j in range(Y):
            rel[i, j] = grads_ref[
                (x + i) % X, pl.ds(pl.multiple_of(((y + j) % Y) * piece, piece), piece)
            ]
    greet(
        [device(dx=d) for d in (1, 2, 3)]
        + [device(dy=d) for d in (1, 2, 3)]
        + [device(dz=d) for d in (1, 2, 3)]
        + [device(dc=1)]
    )

    def to(k, d):
        return device(dy=d) if k else device(dx=d)

    def ds(index, size):
        return pl.ds(pl.multiple_of(index * size, size), size)

    def done(copies):
        for copy in copies:
            copy.wait()

    def term(k, d, begin, size):
        if k:
            lhs = jnp.concatenate([rel[i, d] for i in range(X)], axis=0)
        else:
            lhs = rel[d].reshape(here, deep)
        return dot32(lhs, weight_ref[k * half + begin : k * half + begin + size], ((1,), (1,)))

    def cut(part, u, first, count):
        return jnp.concatenate(
            [
                part[b * piece + u * sub : b * piece + (u + 1) * sub]
                for b in range(first, first + count)
            ],
            axis=0,
        )

    one = {}

    def start_far(u):
        for k in range(2):
            for side, d in enumerate((1, 3)):
                one[k, u, side] = send(
                    two.at[k, u, pl.ds(side * mid, mid)], hop.at[k, u, side],
                    s_one.at[k, u, side], r_one.at[k, u, side], to(k, d),
                )

    def start_near(u):
        for k in range(2):
            for side, d in enumerate((1, 3)):
                plain = pl.ds((1 - side) * mid, mid)
                one[k, u, 2 + side] = send(
                    near.at[k, u, side, plain], came.at[k, u, side, plain],
                    s_one.at[k, u, 2 + side], r_one.at[k, u, 2 + side], to(k, d),
                )

    for k in range(2):
        for start, size in tiles(half, 512):
            part = term(k, 2, start, size)
            for u in range(2):
                two[k, u, :, start : start + size] = cut(part, u, 0, 4).astype(BF16)
    start_far(0)
    for k in range(2):
        for side, d in enumerate((1, 3)):
            for start, size in tiles(half, 512):
                at = slice(start, start + size)
                part = term(k, d, start, size)
                rest = (1 - side) * mid
                for u in range(2):
                    near[k, u, side, rest : rest + mid, at] = cut(
                        part, u, 2 * (1 - side), 2
                    ).astype(BF16)
                    held[k, u, side, :, at] = cut(part, u, 2 * side, 2)
    start_near(0)
    start_far(1)
    start_near(1)
    for k in range(2):
        for start, size in tiles(half, 512):
            part = term(k, 0, start, size)
            for u in range(2):
                acc[k, u, :, start : start + size] = cut(part, u, 0, 4)

    load_pre.wait()
    load_thr.wait()
    for m in range(3):
        at = slice(m * HD, (m + 1) * HD)
        grad = grads_ref[:, :, at].reshape(rows * here, HD)
        before = pre_ref[:, :, at].reshape(rows * here, HD)
        column, magnitude = cola_ref[m : m + 1], maga_ref[m : m + 1]
        ratio = magnitude / column
        mag = jnp.sum(grad.astype(F32) * before, axis=0, keepdims=True) / magnitude
        pull = magnitude * mag / (column * column)
        thin = thr_ref[:, :, m * rank : (m + 1) * rank] + thr_ref[
            :, :, (3 + m) * rank : (4 + m) * rank
        ]
        thin = thin.reshape(rows * here, rank).astype(BF16)
        part = dot32(thin, grad, ((0,), (0,)))
        e_one[(1 + m) * rank : (2 + m) * rank] = adapter_scale * (
            part * ratio - inner_ref[m] * pull
        )
        e_one[4 * rank + m : 4 * rank + m + 1] = mag
        upper = uppera_ref[m]
        down[:, m * rank : (m + 1) * rank] = dot32(
            grad, (upper * ratio).astype(BF16), ((1,), (1,))
        ).astype(BF16)
        pulled = (upper * (mag / column)).astype(BF16)
        for start, size in tiles(width, 512):
            all_s[(7 + m) * rank : (8 + m) * rank, start : start + size] = dot32(
                pulled, weight_ref[start : start + size, at], ((1,), (1,))
            )
    e_one[4 * rank + 3 :] = jnp.zeros((e_one.shape[0] - 4 * rank - 3, HD), F32)
    load.wait()
    for start, size in tiles(width, 512):
        at = slice(start, start + size)
        value = dot32(
            down[...], n1[:, :, at].reshape(rows * here, size), ((0,), (0,))
        )
        all_s[7 * rank : 10 * rank, at] = value - all_s[7 * rank : 10 * rank, at]
    all_s[0 : 5 * rank] = early_ref[...]
    all_s[4 * rank + 1 : 4 * rank + 2] = magd_ref[0:1]
    all_s[5 * rank : 7 * rank] = both_ref[...] * (1.0 / (2 * Z))
    all_s[10 * rank :] = jnp.zeros((n - 10 * rank, width), F32)

    def go(k, d, src, dst, where):
        return send(src, dst, ss.at[k, d], rs.at[k, d], where)

    first = [go(0, 0, all_s.at[ds(1 - core, nc)], c_r, device(dc=1))]
    slots = []
    for d in NEAR_LAST:
        slots.append(go(1, d, block_ref.at[X - d], bx_r.at[d - 1], device(dx=d)))
        slots.append(go(2, d, lower_ref.at[X - d], lx_r.at[d - 1], device(dx=d)))
    for u in range(2):
        for k in range(2):
            for side, d in enumerate((1, 3)):
                one[k, u, side].wait_recv()
                other = pl.ds(side * mid, mid)
                near[k, u, side, side * mid : (side + 1) * mid] = (
                    held[k, u, side] + hop[k, u, side].astype(F32)
                ).astype(BF16)
                one[k, u, 4 + side] = send(
                    near.at[k, u, side, other], came.at[k, u, side, other],
                    s_one.at[k, u, 4 + side], r_one.at[k, u, 4 + side], to(k, d),
                )
    done(first)
    z_s[...] = all_s[ds(core, nc)] + c_r[...]
    z_b[...] = z_s[...].astype(BF16)
    zc = [
        go(3, d, z_b.at[:, ds((z + d) % Z, wz)], z_r.at[d - 1], device(dz=d)) for d in NEAR_LAST
    ]
    done(slots)
    b_one[...] = block_ref[0] + (bx_r[0] + bx_r[1] + bx_r[2])
    e_one[:rank] = lower_ref[0] + (lx_r[0] + lx_r[1] + lx_r[2])
    cc = [go(4, 0, b_one, b_two, device(dc=1)), go(5, 0, e_one, e_two, device(dc=1))]
    seconds = [[], []]
    for u in range(2):
        for k in range(2):
            for index in range(2):
                one[k, u, index].wait_send()
            for index in (2, 3, 4, 5):
                one[k, u, index].wait()
        for k in range(2):
            for d in (2, 1, 3, 0):
                at = slice(d * sub, (d + 1) * sub)
                part = acc[k, u, at] + (
                    came[k, u, 0, at].astype(F32) + came[k, u, 1, at].astype(F32)
                )
                if d:
                    send_2[u, k, d - 1] = part.astype(BF16)
                    seconds[u].append(
                        send(
                            send_2.at[u, k, d - 1], recv_2.at[u, k, d - 1], s_two.at[u, k, d - 1],
                            r_two.at[u, k, d - 1], to(1 - k, d),
                        )
                    )
                else:
                    d_one[u, :, k * half : (k + 1) * half] = part
    done(cc)
    b_two[...] += b_one[...]
    e_two[...] += e_one[...]
    done(zc)
    x_s[...] = z_s[:, ds(z, wz)] + (
        z_r[0].astype(F32) + z_r[1].astype(F32) + z_r[2].astype(F32)
    )
    cz = []
    b_z[z] = b_two[...]
    e_z[z] = e_two[...]
    for d in NEAR_LAST:
        cz.append(go(6, d, b_two, b_z.at[z], device(dz=d)))
        cz.append(go(7, d, e_two, e_z.at[z], device(dz=d)))
    xc = [go(8, d, x_s.at[:, ds((x + d) % X, wx)], x_r.at[d - 1], device(dx=d)) for d in NEAR_LAST]
    left, right = pl.ds(0, half), pl.ds(half, half)
    load_hid.wait()
    gat = [[], []]
    for u in range(2):
        done(seconds[u])
        for k in range(2):
            d_one[u, :, k * half : (k + 1) * half] += (
                recv_2[u, k, 0].astype(F32)
                + recv_2[u, k, 1].astype(F32)
                + recv_2[u, k, 2].astype(F32)
            )
        own = slice(u * sub, (u + 1) * sub)
        inputs = hid_ref[own].astype(F32)
        inverse = lax.rsqrt(jnp.mean(inputs * inputs, axis=1, keepdims=True) + epsilon)
        scaled = d_one[u] * vec_ref[0:1]
        result = dres_ref[own] + (
            inverse * scaled
            - inputs
            * (inverse * inverse * inverse)
            * jnp.mean(inputs * scaled, axis=1, keepdims=True)
        )
        spread[x, y, own] = result.astype(BF16)
        for d in NEAR_LAST:
            for k, side in enumerate((left, right)):
                at = spread.at[x, y, pl.ds(u * sub, sub), side]
                gat[u].append(
                    send(at, at, s_gat.at[u, k, d - 1], r_gat.at[u, k, d - 1], to(k, d))
                )
        if u == 0:
            done(xc)
            y_v[y] = x_s[:, ds(x, wx)] + (x_r[0] + x_r[1] + x_r[2])
            yc = [go(9, d, y_v.at[y], y_v.at[y], device(dy=d)) for d in NEAR_LAST]
    done(yc)
    mine = ds(core, nc)
    at_x = ds(z * X + x, wx)
    gath[mine, at_x] = (((y_v[0] + y_v[1]) + y_v[2]) + y_v[3]).astype(BF16)
    sx = [go(10, d, gath.at[mine, at_x], gath.at[mine, at_x], device(dx=d)) for d in NEAR_LAST]

    def part_of(k, u, d, first, count):
        tokens = pl.ds(u * sub, sub)
        if k:
            return spread.at[(x + d) % X, pl.ds(first, count), tokens, right]
        return spread.at[pl.ds(first, count), (y + d) % Y, tokens, left]

    last = {}
    for u in range(2):
        done(gat[u])
        for k in range(2):
            for side, d in enumerate((1, 3)):
                at = part_of(k, u, 0, 0, 4)
                last[k, u, side] = send(
                    at, at, s_gat.at[u, 2 + k, side], r_gat.at[u, 2 + k, side], to(1 - k, d)
                )
    done(sx)
    spot = gath.at[mine, ds(z, wz)]
    sz = [go(11, d, spot, spot, device(dz=d)) for d in NEAR_LAST]
    done(cz)
    block_out[...] = ((b_z[0] + b_z[1]) + b_z[2]) + b_z[3]
    ctx_out[...] = ((e_z[0] + e_z[1]) + e_z[2]) + e_z[3]
    done(sz)
    spot = gath.at[mine]
    sc = go(12, 0, spot, spot, device(dc=1))
    for u in range(2):
        for k in range(2):
            for side, d in enumerate((1, 3)):
                last[k, u, side].wait_recv()
                at = part_of(k, u, 4 - d, 2 * side, 2)
                last[k, u, 2 + side] = send(
                    at, at, s_gat.at[u, 4 + k, side], r_gat.at[u, 4 + k, side], to(1 - k, d)
                )
    for u in range(2):
        for k in range(2):
            for side in range(2):
                last[k, u, side].wait_send()
                last[k, u, 2 + side].wait()
    out = keep(spread, grad_out, local.at[1])
    sc.wait()
    all_out[...] = gath[...]
    out.wait()


def tail(
    grads, weight, hidden, gain, d_resid, pre, thr, n1, inner, cola, maga, uppera, early, both,
    block, lower, magd,
):
    rows, here, deep = grads.shape
    piece, width = d_resid.shape
    half = width // 2
    mid = here // 4
    sub = piece // 2
    _, bn, bw = block.shape
    n = 192
    en = 72
    nc = n // 2
    wz, wx = width // Z, width // Z // X
    s = jax.ShapeDtypeStruct
    v = pltpu.VMEM
    return call(
        tail_kernel,
        (s((rows, Y, piece, width), BF16), s((n, width), BF16), s((bn, bw), F32), s((en, HD), F32)),
        [VM] * 2 + [ANY] + [VM] * 2 + [ANY] * 3 + [VM] * 9,
        (ANY, VM, VM, VM),
        [
            v((X, Y, piece, deep), BF16),
            v((2, 2, 2 * mid, half), BF16),
            v((2, 2, 2, 2 * mid, half), BF16),
            v((2, 2, 2, mid, half), F32),
            v((2, 2, 2, mid, half), BF16),
            v((2, 2, 2, 2 * mid, half), BF16),
            v((2, 2, 2 * mid, half), F32),
            v((2, 2, 3, sub, half), BF16),
            v((2, 2, 3, sub, half), BF16),
            v((2, sub, width), F32),
            v((X, Y, piece, width), BF16),
            v((rows, here, width), BF16),
            v((rows * here, 48), BF16),
            v((n, width), F32),
            v((piece, width), BF16),
            v(pre.shape, F32),
            v(thr.shape, F32),
            v((n, width), BF16),
            v((nc, width), F32),
            v((nc, width), F32),
            v((nc, width), BF16),
            v((3, nc, wz), BF16),
            v((nc, wz), F32),
            v((3, nc, wx), F32),
            v((Y, nc, wx), F32),
            v((3, bn, bw), F32),
            v((3, 16, HD), F32),
            v((bn, bw), F32),
            v((bn, bw), F32),
            v((en, HD), F32),
            v((en, HD), F32),
            v((Z, en, HD), F32),
            v((Z, bn, bw), F32),
            dma(2, 2, 6), dma(2, 2, 6), dma(2, 2, 3), dma(2, 2, 3), dma(2, 6, 3), dma(2, 6, 3),
            dma(13, 4), dma(13, 4), dma(5),
        ],
        3,
        2 * rows * here * deep * width,
        16 * 2**20,
    )(
        grads, weight, hidden, gain, d_resid, pre, thr, n1, inner, cola, maga, uppera, early, both,
        block, lower, magd,
    )


def widen_kernel(a_ref, b_ref, wide_out, same_out, narrow, wide, passed, loads, stores):
    rows = a_ref.shape[0]
    copies = [keep(a_ref.at[r], narrow.at[r], loads.at[0, r]) for r in range(rows)]
    others = [keep(b_ref.at[r], passed.at[r], loads.at[1, r]) for r in range(rows)]
    outs = []
    for r in range(rows):
        copies[r].wait()
        wide[r] = narrow[r].astype(F32)
        outs.append(keep(wide.at[r], wide_out.at[r], stores.at[0, r]))
    for r in range(rows):
        others[r].wait()
        outs.append(keep(passed.at[r], same_out.at[r], stores.at[1, r]))
    for copy in outs:
        copy.wait()


def widen(a, b):
    parts = 16
    many, width = a.shape[0] * a.shape[1] * a.shape[2] // parts, a.shape[3]
    wide, same = pl.pallas_call(
        widen_kernel,
        out_shape=(
            jax.ShapeDtypeStruct((parts, many, width), F32),
            jax.ShapeDtypeStruct((parts, many, width), BF16),
        ),
        in_specs=[ANY, ANY],
        out_specs=(ANY, ANY),
        scratch_shapes=[
            pltpu.VMEM((parts, many, width), BF16),
            pltpu.VMEM((parts, many, width), F32),
            pltpu.VMEM((parts, many, width), BF16),
            dma(2, parts), dma(2, parts),
        ],
        compiler_params=pltpu.CompilerParams(vmem_limit_bytes=58 * 2**20),
    )(a.reshape(parts, many, width), b.reshape(parts, many, width))
    return wide.reshape(b.shape), same.reshape(b.shape)


def on_device(
    hidden,
    segments,
    key_attendable,
    attention_gain,
    feedforward_gain,
    attend_frozen,
    output_frozen,
    expand_frozen,
    reduce_frozen,
    attend_lower,
    attend_upper,
    attend_magnitude,
    output_lower,
    output_upper,
    output_magnitude,
    expand_lower,
    expand_upper,
    expand_magnitude,
    reduce_lower,
    reduce_upper,
    reduce_magnitude,
    cotangent,
):
    rows, here, width = hidden.shape
    length = segments.shape[1]
    ff = reduce_frozen.shape[0]
    rank = output_lower.shape[1]
    ctx = lax.axis_index("ctx")
    offset = ctx * here

    lower_attend = attend_lower.transpose(0, 2, 1).reshape(3 * rank, width)
    lower_expand = expand_lower.transpose(0, 2, 1).reshape(2 * rank, width)
    upper_t = expand_upper.transpose(0, 2, 1)
    small = jnp.concatenate(
        [upper_t[0], upper_t[1], reduce_lower, expand_magnitude.T], axis=1
    )
    small = jnp.concatenate(
        [
            jnp.pad(small, ((0, 0), (0, HD - 3 * rank - 2))),
            jnp.pad(output_lower, ((0, 0), (0, HD - rank))),
        ],
        axis=0,
    )
    vectors = jnp.stack(
        [
            attention_gain.astype(F32),
            feedforward_gain.astype(F32),
            output_magnitude,
            reduce_magnitude,
        ]
    )
    upper = jnp.concatenate([output_upper, reduce_upper], axis=0)

    levels = jnp.arange(SEGS, dtype=jnp.int32)
    below_count = jnp.sum((segments[:, None, :] < levels[None, :, None]).astype(F32), axis=2)
    segments_here = lax.dynamic_slice_in_dim(segments, offset, here, 1)
    begin_here = jnp.sum(
        (segments_here[:, :, None] == levels[None, None, :]).astype(F32) * below_count[:, None, :],
        axis=2,
    )
    spot_here = offset + jnp.arange(here, dtype=jnp.int32)
    places = spot_here.astype(F32)[None, :] - begin_here
    frequency = rotary_base ** (-(2.0 * jnp.arange(HD // 2).astype(F32)) / HD)
    frequency = jnp.concatenate([frequency, frequency])
    angles = places[:, :, None] * frequency[None, None, :]
    cosine, sine_part = jnp.cos(angles), jnp.sin(angles)
    spots = jnp.arange(length, dtype=jnp.int32)[None]
    key_tag = jnp.where(key_attendable == 1, spots, -1)[:, None, :]
    begin = begin_here.astype(jnp.int32)[:, :, None]

    (
        mixed_parts,
        soft,
        log_total,
        all_pairs,
        weights_x,
        weight_attend,
        queries,
        pre,
        through_three,
        column_attend,
        column_expand,
        squares,
        inner_attend,
        inner_expand,
        inner_both,
        normed_one,
        small_own,
    ) = front(
        hidden,
        vectors,
        attend_frozen,
        lower_attend,
        attend_upper,
        attend_magnitude,
        output_frozen,
        expand_frozen.transpose(0, 2, 1),
        reduce_frozen,
        output_lower.T,
        expand_upper,
        reduce_lower.T,
        upper,
        lower_expand,
        small,
        cosine,
        sine_part,
        begin,
        key_tag,
    )
    d_resid, resid, ff_own, ff_send, d_mixed_parts, early, block_x, lower_out = feed(
        mixed_parts, hidden, vectors, cotangent, weights_x, small_own, lower_expand, upper, squares
    )
    grads_low, block_output, mag_down = attend_back(
        queries,
        all_pairs,
        d_mixed_parts,
        soft,
        log_total,
        begin,
        key_tag,
        cosine,
        sine_part,
        resid,
        ff_own,
        ff_send,
        cotangent,
    )
    hidden_grad, everywhere, block_x, small_ctx = tail(
        grads_low,
        weight_attend,
        hidden,
        vectors,
        d_resid,
        pre,
        through_three,
        normed_one,
        inner_attend,
        column_attend,
        attend_magnitude,
        attend_upper,
        early,
        inner_both,
        block_x,
        lower_out,
        mag_down,
    )
    hidden_grad, block_output = widen(hidden_grad, block_output)
    everywhere = everywhere.astype(F32)
    lower_out, local = small_ctx[:rank], small_ctx[rank:]
    late = adapter_scale * everywhere[7 * rank : 10 * rank]
    early = everywhere[: 7 * rank]

    attend_lower_grad = late.reshape(3, rank, width).transpose(0, 2, 1)
    attend_upper_grad = local[: 3 * rank].reshape(3, rank, HD)
    attend_magnitude_grad = local[3 * rank : 3 * rank + 3]
    column_expand = column_expand.reshape(2, ff)
    inner_expand = inner_expand.reshape(2, ff, HD)
    inner_expand = inner_expand[..., : 2 * rank] + inner_expand[..., 2 * rank : 4 * rank]
    expand_magnitude_grad = block_x[3 * rank : 3 * rank + 2] / expand_magnitude
    pull_expand = expand_magnitude * expand_magnitude_grad / column_expand**2
    ratio_expand = expand_magnitude / column_expand
    expand_upper_grad = jnp.stack(
        [
            adapter_scale
            * (
                block_x[m * rank : (m + 1) * rank] * ratio_expand[m]
                - inner_expand[m, :, m * rank : (m + 1) * rank].T * pull_expand[m]
            )
            for m in range(2)
        ]
    )
    expand_lower_grad = adapter_scale * early[: 2 * rank].reshape(2, rank, width).transpose(0, 2, 1)
    columns = jnp.sqrt(squares)
    mago = vectors[2:]
    magnitude_grads = early[4 * rank : 4 * rank + 2] / mago
    pulls = mago * magnitude_grads / squares
    ratios = mago / columns
    output_magnitude_grad = magnitude_grads[0]
    reduce_magnitude_grad = magnitude_grads[1]
    output_upper_grad = adapter_scale * (
        early[2 * rank : 3 * rank] * ratios[0] - early[5 * rank : 6 * rank] * pulls[0]
    )
    reduce_upper_grad = adapter_scale * (
        early[3 * rank : 4 * rank] * ratios[1] - early[6 * rank : 7 * rank] * pulls[1]
    )

    def pulled_rows(frozen, lower, upper, pull):
        pulled = upper * pull
        rows_part = exact_dot(frozen, pulled, ((1,), (1,)))
        return rows_part + adapter_scale * jnp.dot(
            lower,
            jnp.dot(upper, pulled.T, precision=lax.Precision.HIGHEST),
            precision=lax.Precision.HIGHEST,
        )

    output_lower_grad = adapter_scale * (
        lower_out.T - pulled_rows(output_frozen, output_lower, output_upper, pulls[0])
    )
    reduce_lower_grad = adapter_scale * (
        block_x[2 * rank : 3 * rank].T
        - pulled_rows(reduce_frozen, reduce_lower, reduce_upper, pulls[1])
    )
    return (
        block_output,
        hidden_grad,
        attend_lower_grad,
        attend_upper_grad,
        attend_magnitude_grad,
        output_lower_grad,
        output_upper_grad,
        output_magnitude_grad,
        expand_lower_grad,
        expand_upper_grad,
        expand_magnitude_grad,
        reduce_lower_grad,
        reduce_upper_grad,
        reduce_magnitude_grad,
    )


def solution(mesh):
    placed = (
        P(None, "ctx", None),
        P(),
        P(),
        P(),
        P(),
        P(None, None, "tp"),
        P("tp", None),
        P(None, None, "tp"),
        P("tp", None),
        P(),
        P(None, None, "tp"),
        P(None, "tp"),
        P("tp", None),
        P(),
        P(),
        P(),
        P(None, None, "tp"),
        P(None, "tp"),
        P("tp", None),
        P(),
        P(),
        P(None, "ctx", None),
    )
    return jax.shard_map(
        on_device,
        mesh=mesh,
        in_specs=placed,
        out_specs=(
            P(None, "ctx", None),
            P(None, "ctx", None),
            P(),
            P(None, None, "tp"),
            P(None, "tp"),
            P("tp", None),
            P(),
            P(),
            P(),
            P(None, None, "tp"),
            P(None, "tp"),
            P("tp", None),
            P(),
            P(),
        ),
        check_vma=False,
    )
```
